32 devices in a mesh: dp: 4 (over y, core), tensor: 8 (over z, x).
Axes of the slice: x: 2, y: 2, z: 4, core: 2. Of those that a mesh axis runs over, the one named last changes fastest.
Arguments:
- queries: bfloat16 [4096, 1024], P('dp'), may hold values from -6 to 6
- passages: bfloat16 [4096, 1024], P('dp'), may hold values from -6 to 6
- query_lengths: int32 [4], replicated, may hold values from 256 to 1024, as said below
- passage_lengths: int32 [4], replicated, may hold values from 256 to 1024, as said below
- w_qkv: bfloat16 [3, 1024, 1024], P(None, None, 'tensor'), may hold values from -0.1875 to 0.1875
- qv_bias: bfloat16 [2, 1024], P(None, 'tensor'), may hold values from -2 to 2
- w_out: bfloat16 [1024, 1024], P('tensor'), may hold values from -1.5 to 1.5
- w_in: bfloat16 [1024, 4096], P(None, 'tensor'), may hold values from -0.1875 to 0.1875
- in_bias: bfloat16 [4096], P('tensor'), may hold values from -3 to 3
- w_down: bfloat16 [4096, 1024], P('tensor'), may hold values from -0.09375 to 0.09375
- norm_gain: float32 [2, 1024], replicated, may hold values from 0.5 to 1.5
- norm_shift: float32 [2, 1024], replicated, may hold values from -2 to 2
- layer_bias: float32 [3, 1024], replicated, may hold values from -2 to 2
- w_colbert: bfloat16 [1024, 1024], replicated, may hold values from -0.1875 to 0.1875
- dense_cot: float32 [4, 4], replicated, may hold values from -8 to 8
- colbert_cot: float32 [4, 4], replicated, may hold values from -64 to 64
Outputs:
- out_queries: bfloat16 [4096, 1024], P(('dp', 'tensor'))
- out_passages: bfloat16 [4096, 1024], P(('dp', 'tensor'))
- grad_queries: float32 [4096, 1024], P(('dp', 'tensor'))
- grad_passages: float32 [4096, 1024], P(('dp', 'tensor'))
- grad_w_qkv: float32 [3, 1024, 1024], P(None, None, 'tensor')
- grad_qv_bias: float32 [2, 1024], P(None, 'tensor')
- grad_w_out: float32 [1024, 1024], P('tensor')
- grad_w_in: float32 [1024, 4096], P(None, 'tensor')
- grad_in_bias: float32 [4096], P('tensor')
- grad_w_down: float32 [4096, 1024], P('tensor')
- grad_norm_gain: float32 [2, 1024], replicated
- grad_norm_shift: float32 [2, 1024], replicated
- grad_layer_bias: float32 [3, 1024], replicated
- grad_w_colbert: float32 [1024, 1024], replicated
The draws below stay inside these ranges and needn't reach their ends.
Inputs may be any that keep to these rules, and one draw needn't show every extreme that they name: `query_lengths`: in every data group the query or the passage uses all its positions; in every draw some query uses all 1024 and some passage all 1024. `passage_lengths`: drawn together with query_lengths.
All inputs are finite; a program needn't handle non-finite values.
Results may differ from the reference program's by a relative error of at most 0.023.
Values may be sent and summed in bfloat16 or wider, within the bound.
A program may use at most 192 MiB of HBM per device.

```python
import jax
import jax.numpy as jnp
from jax import lax

D = 1024
HEADS = 16
HEAD_DIM = 64
FF = 4096
QLEN = 1024
PLEN = 1024
NQ = 4
NP = 4
QTOK = 4096
PTOK = 4096


def length_plan(key):
    mixed = jax.random.fold_in(key, 7)
    keys = jax.random.split(mixed, 5)
    side = jax.random.randint(keys[0], (NQ,), 0, 2)
    first = jax.random.randint(keys[1], (), 0, NQ)
    second = (first + 1 + jax.random.randint(keys[2], (), 0, NQ - 1)) % NQ
    index = jnp.arange(NQ)
    side = jnp.where(index == first, 1, jnp.where(index == second, 0, side))
    query_part = jax.random.randint(keys[3], (NQ,), QLEN // 4, QLEN + 1)
    passage_part = jax.random.randint(keys[4], (NQ,), PLEN // 4, PLEN + 1)
    query_lengths = jnp.where(side == 0, QLEN, query_part).astype(jnp.int32)
    passage_lengths = jnp.where(side == 1, PLEN, passage_part).astype(jnp.int32)
    return (query_lengths, passage_lengths)


def draw_query_lengths(key, part):
    return length_plan(key)[0]


def draw_passage_lengths(key, part):
    return length_plan(key)[1]


def shard_levels(rng, extent, cuts, least, high):
    factor_of = 1.0
    for axis_at, blocks in cuts:
        draws = jax.random.uniform(jax.random.fold_in(jax.random.fold_in(rng, 6), axis_at), (blocks,), jnp.float32, least / len(cuts), high / len(cuts))
        factor_of = factor_of * jnp.repeat(jnp.exp(draws), extent[axis_at] // blocks).reshape((-1,) + (1,) * (len(extent) - 1 - axis_at))
    return factor_of


def noise(own_key, extent, scale, bound, shards=(), kind=jnp.bfloat16):
    result = scale * jax.random.normal(own_key, extent, jnp.float32)
    if shards:
        result = result * shard_levels(own_key, extent, shards, -0.22, 0.18)
    return jnp.clip(result, -bound, bound).astype(kind)


def setup_inputs(seed: int = 0) -> dict:
    streams_of = jax.random.split(jax.random.key(seed), 17)
    queries = noise(streams_of[0], (QTOK, D), 1.0, 6.0, ((0, 4),))
    passages = noise(streams_of[1], (PTOK, D), 1.0, 6.0, ((0, 4),))
    query_lengths = draw_query_lengths(jax.random.fold_in(streams_of[16], 71), 0)
    passage_lengths = draw_passage_lengths(jax.random.fold_in(streams_of[16], 71), 0)
    w_qkv = noise(streams_of[4], (3, D, D), D ** -0.5, 0.1875, ((2, 8),))
    qv_bias = noise(streams_of[5], (2, D), 0.3, 2.0, ((1, 8),))
    w_out = noise(streams_of[6], (D, D), (max(D // 64, 4)) ** -0.5, 1.5, ((0, 8),))
    w_in = noise(streams_of[7], (D, FF), D ** -0.5, 0.1875, ((1, 8),))
    in_bias = noise(streams_of[8], (FF,), 0.5, 3.0, ((0, 8),))
    w_down = noise(streams_of[9], (FF, D), FF ** -0.5, 0.09375, ((0, 8),))
    norm_gain = jnp.clip(1.0 + 0.1 * jax.random.normal(streams_of[10], (2, D), jnp.float32), 0.5, 1.5)
    norm_shift = noise(streams_of[11], (2, D), 0.3, 2.0, (), jnp.float32)
    layer_bias = noise(streams_of[12], (3, D), 0.3, 2.0, (), jnp.float32)
    w_colbert = noise(streams_of[13], (D, D), D ** -0.5, 0.1875)
    dense_cot = noise(streams_of[14], (NQ, NP), 2.0, 8.0, (), jnp.float32)
    colbert_cot = noise(streams_of[15], (NQ, NP), 16.0, 64.0, (), jnp.float32)
    return {"queries": queries, "passages": passages, "query_lengths": query_lengths, "passage_lengths": passage_lengths, "w_qkv": w_qkv, "qv_bias": qv_bias, "w_out": w_out, "w_in": w_in, "in_bias": in_bias, "w_down": w_down, "norm_gain": norm_gain, "norm_shift": norm_shift, "layer_bias": layer_bias, "w_colbert": w_colbert, "dense_cot": dense_cot, "colbert_cot": colbert_cot}


@jax.custom_vjp
def low(v):
    return lax.optimization_barrier(v.astype(jnp.bfloat16)).astype(jnp.float32)

@jax.custom_vjp
def low_back(v):
    return v

def low_keep(v):
    return (low(v), None)

def low_pass(kept, grad):
    return (grad,)

def back_keep(v):
    return (v, None)

def back_low(kept, grad):
    return (low(grad),)
low.defvjp(low_keep, low_pass)
low_back.defvjp(back_keep, back_low)

def matmul(left, right):
    return jnp.dot(left, right, precision=lax.Precision.HIGHEST, preferred_element_type=jnp.float32)

def layer_norm(hidden, gain, shift):
    centre = hidden - lax.optimization_barrier(jnp.mean(hidden, axis=-1, keepdims=True))
    spread = lax.optimization_barrier(jnp.mean(centre * centre, axis=-1, keepdims=True))
    return centre * lax.rsqrt(spread + 1e-05) * gain + shift

def unit_rows(vectors):
    return vectors * lax.rsqrt(lax.optimization_barrier(jnp.sum(vectors * vectors, axis=-1, keepdims=True)) + 1e-06)

def encode(tokens, length, params):
    w_qkv, qv_bias, w_out, w_in, in_bias, w_down, norm_gain, norm_shift, layer_bias, w_colbert = params
    span = tokens.shape[0]
    query = low_back(low(matmul(tokens, w_qkv[0]) + qv_bias[0]))
    key = low_back(low(matmul(tokens, w_qkv[1])))
    value = low_back(low(matmul(tokens, w_qkv[2]) + qv_bias[1]))
    keep = jnp.arange(span) < length
    scale = HEAD_DIM ** (-0.5)

    def one_head(triple):
        head_query, head_key, head_value = triple
        scores = low_back(matmul(head_query, head_key.T) * scale)
        scores = jnp.where(keep[None, :], scores, -1e+30)
        weights = jax.nn.softmax(scores, axis=-1)
        return matmul(low(weights), head_value)

    def split(matrix):
        return matrix.reshape(span, HEADS, HEAD_DIM).transpose(1, 0, 2)
    per_head = lax.map(jax.checkpoint(one_head), (split(query), split(key), split(value)))
    context = low_back(low(per_head.transpose(1, 0, 2).reshape(span, D)))
    attention = low_back(matmul(context, w_out))
    first = layer_norm(tokens + attention + layer_bias[0], norm_gain[0], norm_shift[0])
    inner = low_back(matmul(low(first), w_in) + in_bias)
    active = jax.nn.gelu(inner, approximate=False)
    feed = low_back(matmul(low(active), w_down))
    output = layer_norm(first + feed + layer_bias[1], norm_gain[1], norm_shift[1])
    projected = low_back(matmul(low(output), w_colbert) + layer_bias[2])
    leading = jnp.arange(span) == 0
    vectors = low(unit_rows(jnp.where(leading[:, None], output, projected)))
    return (output, vectors)

def reference(queries, passages, query_lengths, passage_lengths, w_qkv, qv_bias, w_out, w_in, in_bias, w_down, norm_gain, norm_shift, layer_bias, w_colbert, dense_cot, colbert_cot):
    floats = [item.astype(jnp.float32) for item in (queries, passages, w_qkv, qv_bias, w_out, w_in, in_bias, w_down, norm_gain, norm_shift, layer_bias, w_colbert)]
    colbert_grad = colbert_cot.astype(jnp.float32)
    dense_grad = dense_cot.astype(jnp.float32)

    def forward(query_rows, passage_rows, *params):

        def run_sequence(item):
            return encode(item[0], item[1], params)
        query_out, query_vec = lax.map(jax.checkpoint(run_sequence), (query_rows.reshape(NQ, QLEN, D), query_lengths))
        passage_out, passage_vec = lax.map(jax.checkpoint(run_sequence), (passage_rows.reshape(NP, PLEN, D), passage_lengths))
        flat = passage_vec.reshape(NP * PLEN, D)
        place = jnp.arange(PLEN)
        counted = (place[None, :] >= 1) & (place[None, :] < passage_lengths[:, None])
        scale = D ** 0.5

        def score_query(item):
            vectors, length, colbert_row, dense_row = item
            dots = low_back(matmul(vectors, flat.T)).reshape(QLEN, NP, PLEN)
            scaled = jnp.where(counted[None], dots * scale, -1e+30)
            totals = jax.nn.logsumexp(scaled, axis=-1)
            rows = jnp.arange(QLEN)
            used = (rows >= 1) & (rows < length)
            late = lax.optimization_barrier(jnp.sum(jnp.where(used[:, None], totals, 0.0), axis=0))
            dense = 50.0 * dots[0, :, 0]
            return jnp.sum(colbert_row * late) + jnp.sum(dense_row * dense)
        losses = lax.map(jax.checkpoint(score_query), (query_vec, query_lengths, colbert_grad, dense_grad))
        return (jnp.sum(losses), (query_out, passage_out))
    loss, pullback, outs = jax.vjp(forward, *floats, has_aux=True)
    grads = pullback(jnp.ones_like(loss))
    return (outs[0].reshape(NQ * QLEN, D).astype(jnp.bfloat16), outs[1].reshape(NP * PLEN, D).astype(jnp.bfloat16), grads[0], grads[1], grads[2], grads[3], grads[4], grads[5], grads[6], grads[7], grads[8], grads[9], grads[10], grads[11])
```

```python
import functools

import jax
import jax.numpy as jnp
from jax import lax
from jax.experimental import pallas as pl
from jax.experimental.pallas import tpu as pltpu
from jax.sharding import PartitionSpec as P

HEAD_DIM = 64
BF = jnp.bfloat16
F32 = jnp.float32
BLOCK = 256


def dot(left, right):
    return jnp.dot(left, right, preferred_element_type=F32)


def inner_rows(left, right):
    return lax.dot_general(left, right, (((1,), (1,)), ((), ())), preferred_element_type=F32)


def outer_rows(left, right):
    return lax.dot_general(left, right, (((0,), (0,)), ((), ())), preferred_element_type=F32)


def steps_of(size):
    steps = []
    while size > 1:
        size //= 2
        steps.append(size)
    return steps


def offsets(steps):
    found = [0]
    for step in steps:
        found = found + [item ^ step for item in found]
    return found


def swap(value, axis, step):
    size = lax.axis_size(axis)
    return lax.ppermute(value, axis, [(index, index ^ step) for index in range(size)])


def spread(value, axis, steps):
    held = value[None]
    for step in steps:
        held = jnp.concatenate([held, swap(held, axis, step)], axis=0)
    return held


def fold(parts, axis, steps):
    for step in reversed(steps):
        half = parts.shape[0] // 2
        came = swap(parts[half:].astype(BF), axis, step)
        parts = parts[:half].astype(F32) + came.astype(F32)
    return parts[0]


def natural(parts, axis, steps, dim=0):
    order = offsets(steps)
    size = len(order)
    place = [0] * size
    for spot, item in enumerate(order):
        place[item] = spot
    table = jnp.array(place, jnp.int32)
    rank = lax.axis_index(axis)
    return jnp.concatenate(
        [lax.dynamic_slice_in_dim(parts, table[item ^ rank], 1, dim) for item in range(size)], axis=dim
    )


def xored(parts, axis, steps, dim=0):
    rank = lax.axis_index(axis)
    return jnp.concatenate(
        [lax.dynamic_slice_in_dim(parts, item ^ rank, 1, dim) for item in offsets(steps)], axis=dim
    )


def trade(parts, steps, dim):
    rank = lax.axis_index("tensor")
    got = []
    for item in offsets(steps):
        piece = lax.dynamic_index_in_dim(parts, item ^ rank, dim, keepdims=False)
        got.append(swap(piece, "tensor", item) if item else piece)
    return got


def layer_norm(hidden, gain, shift):
    centre = hidden - jnp.mean(hidden, axis=-1, keepdims=True)
    inverse = lax.rsqrt(jnp.mean(centre * centre, axis=-1, keepdims=True) + 1e-05)
    normal = centre * inverse
    return (normal * gain + shift, normal, inverse)


def norm_back(grad, normal, inverse, gain):
    scaled = grad * gain
    middle = (
        scaled
        - jnp.mean(scaled, axis=-1, keepdims=True)
        - normal * jnp.mean(scaled * normal, axis=-1, keepdims=True)
    )
    return (middle * inverse, jnp.sum(grad * normal, axis=0), jnp.sum(grad, axis=0))


def gelu_slope(inner):
    return (
        0.5 * (1.0 + lax.erf(inner * 0.7071067811865476))
        + inner * jnp.exp(-0.5 * inner * inner) * 0.3989422804014327
    )


def head_mask(columns, head):
    lane = lax.broadcasted_iota(jnp.int32, (1, columns), 1)
    return (lane >= head * HEAD_DIM) & (lane < (head + 1) * HEAD_DIM)


def attend_kernel(lens, x, w, b, q, k, v, ctx, lse):
    span, columns = q.shape[1], q.shape[2]
    heads = columns // HEAD_DIM
    length = lens[pl.program_id(0)]
    scale = HEAD_DIM**-0.5
    rows = x[0]
    q[0] = (dot(rows, w[0]) + b[0:1, :].astype(F32)).astype(BF)
    k[0] = dot(rows, w[1]).astype(BF)
    v[0] = (dot(rows, w[2]) + b[1:2, :].astype(F32)).astype(BF)
    keys = k[0]
    values = v[0]
    keep = lax.broadcasted_iota(jnp.int32, (1, span), 1) < length
    block = min(BLOCK, span)

    @pl.loop(0, span // block)
    def _(index):
        at = pl.ds(pl.multiple_of(index * block, block), block)
        query = q[0, at, :]
        total = jnp.zeros((block, columns), F32)
        for head in range(heads):
            mask = head_mask(columns, head)
            mine = jnp.where(mask, query, jnp.zeros_like(query)) * jnp.asarray(scale, BF)
            scores = jnp.where(keep, inner_rows(mine, keys), -1e30)
            top = jnp.max(scores, axis=-1, keepdims=True)
            raised = jnp.exp(scores - top)
            mass = jnp.sum(raised, axis=-1, keepdims=True)
            part = dot(raised.astype(BF), values) / mass
            total = jnp.where(mask, part, total)
            column = jnp.broadcast_to(top + jnp.log(mass), (block, 128))
            lse[0, head : head + 1, at] = column.T[0:1, :]
        ctx[0, at, :] = total.astype(BF)


def attend_back_kernel(lens, q, k, v, g, lse, out, dk_sum, dv_sum):
    span, columns = q.shape[1], q.shape[2]
    heads = columns // HEAD_DIM
    length = lens[pl.program_id(0)]
    scale = HEAD_DIM**-0.5
    keys = k[0]
    values = v[0]
    keep = lax.broadcasted_iota(jnp.int32, (span, 1), 0) < length
    block = min(BLOCK, span)
    dk_sum[...] = jnp.zeros_like(dk_sum)
    dv_sum[...] = jnp.zeros_like(dv_sum)

    @pl.loop(0, span // block)
    def _(index):
        at = pl.ds(pl.multiple_of(index * block, block), block)
        query = q[0, at, :]
        grad = g[0, at, :]
        total = jnp.zeros((block, columns), F32)
        for head in range(heads):
            mask = head_mask(columns, head)
            mine = jnp.where(mask, query, jnp.zeros_like(query)) * jnp.asarray(scale, BF)
            back = jnp.where(mask, grad, jnp.zeros_like(grad))
            scores = jnp.where(keep, inner_rows(keys, mine), -1e30)
            probs = jnp.exp(scores - lse[0, head : head + 1, at])
            slope = inner_rows(values, back)
            middle = jnp.sum(probs * slope, axis=0, keepdims=True)
            turn = (probs * (slope - middle)).astype(BF)
            dv_sum[...] += dot(probs.astype(BF), back)
            dk_sum[...] += dot(turn, mine)
            part = outer_rows(turn, keys) * scale
            total = jnp.where(mask, part, total)
        out[0, at, 0:columns] = total.astype(BF)

    out[0, :, columns : 2 * columns] = dk_sum[...].astype(BF)
    out[0, :, 2 * columns : 3 * columns] = dv_sum[...].astype(BF)


def attend(lens, tokens, w_qkv, qv_bias):
    count, span, width = tokens.shape
    columns = w_qkv.shape[2]
    heads = columns // HEAD_DIM
    flat = jax.ShapeDtypeStruct((count, span, columns), BF)
    rows = pl.BlockSpec((1, span, columns), lambda i, n: (i, 0, 0))
    return pl.pallas_call(
        attend_kernel,
        out_shape=(flat, flat, flat, flat, jax.ShapeDtypeStruct((count, heads, span), F32)),
        grid_spec=pltpu.PrefetchScalarGridSpec(
            num_scalar_prefetch=1,
            grid=(count,),
            in_specs=[
                pl.BlockSpec((1, span, width), lambda i, n: (i, 0, 0)),
                pl.BlockSpec((3, width, columns), lambda i, n: (0, 0, 0)),
                pl.BlockSpec((2, columns), lambda i, n: (0, 0)),
            ],
            out_specs=[rows, rows, rows, rows, pl.BlockSpec((1, heads, span), lambda i, n: (i, 0, 0))],
        ),
        compiler_params=pltpu.CompilerParams(vmem_limit_bytes=48 * 2**20),
        cost_estimate=pl.CostEstimate(
            flops=20 * 10**9, bytes_accessed=8 * 2**20, transcendentals=count * heads * span * span
        ),
        name="attend",
    )(lens, tokens, w_qkv, qv_bias)


def attend_back(lens, query, key, value, grad, lse):
    count, span, columns = query.shape
    heads = columns // HEAD_DIM
    rows = pl.BlockSpec((1, span, columns), lambda i, n: (i, 0, 0))
    return pl.pallas_call(
        attend_back_kernel,
        out_shape=jax.ShapeDtypeStruct((count, span, 3 * columns), BF),
        grid_spec=pltpu.PrefetchScalarGridSpec(
            num_scalar_prefetch=1,
            grid=(count,),
            in_specs=[rows, rows, rows, rows, pl.BlockSpec((1, heads, span), lambda i, n: (i, 0, 0))],
            out_specs=pl.BlockSpec((1, span, 3 * columns), lambda i, n: (i, 0, 0)),
            scratch_shapes=[pltpu.VMEM((span, columns), F32), pltpu.VMEM((span, columns), F32)],
        ),
        compiler_params=pltpu.CompilerParams(vmem_limit_bytes=48 * 2**20),
        cost_estimate=pl.CostEstimate(
            flops=40 * 10**9, bytes_accessed=8 * 2**20, transcendentals=count * heads * span * span
        ),
        name="attend_back",
    )(lens, query, key, value, grad, lse)


def per_device(
    queries,
    passages,
    query_lengths,
    passage_lengths,
    w_qkv,
    qv_bias,
    w_out,
    w_in,
    in_bias,
    w_down,
    norm_gain,
    norm_shift,
    layer_bias,
    w_colbert,
    dense_cot,
    colbert_cot,
):
    groups, ranks = lax.axis_size("dp"), lax.axis_size("tensor")
    group, rank = lax.axis_index("dp"), lax.axis_index("tensor")
    all_t, all_d = steps_of(ranks), steps_of(groups)
    far_t, near_t = all_t[:-1], all_t[-1:]
    far_d, near_d = all_d[:-1], all_d[-1:]
    span, width = queries.shape
    share = span // ranks
    columns = w_qkv.shape[2]
    hidden = w_in.shape[1]
    piece = hidden // groups

    up_mine = lax.dynamic_slice_in_dim(w_in, group * piece, piece, 1).T
    down_mine = lax.dynamic_slice_in_dim(w_down, group * piece, piece, 0)
    up = spread(up_mine, "tensor", all_t).reshape(-1, width)
    down = spread(down_mine, "tensor", all_t).reshape(-1, width)
    slim = columns // groups
    out_mine = lax.dynamic_slice_in_dim(w_out, group * slim, slim, 0)
    out_all = spread(spread(out_mine, "tensor", all_t), "dp", all_d)
    out_all = natural(out_all, "dp", all_d).transpose(1, 0, 2, 3).reshape(ranks * columns, width)
    bias_all = lax.all_gather(in_bias, "tensor").reshape(ranks, groups, piece)
    bias_mine = lax.dynamic_index_in_dim(bias_all, group, 1, keepdims=False)
    bias_units = xored(bias_mine, "tensor", all_t).reshape(-1).astype(F32)

    tokens = jnp.stack([queries, passages])
    lens = jnp.stack([query_lengths[group], passage_lengths[group]])
    query, key, value, context, lse = attend(lens, tokens, w_qkv, qv_bias)
    context = context.reshape(2, ranks, share, columns)
    context_rows = jnp.concatenate(trade(context, all_t, 1), axis=-1).reshape(2 * share, ranks * columns)

    mine = lax.dynamic_index_in_dim(
        tokens.reshape(2, ranks, share, width), rank, 1, keepdims=False
    ).reshape(2 * share, width)
    first, first_normal, first_inverse = layer_norm(
        mine.astype(F32) + dot(context_rows, out_all) + layer_bias[0], norm_gain[0], norm_shift[0]
    )
    normed = spread(first.astype(BF), "dp", all_d).reshape(-1, width)
    inner = inner_rows(normed, up) + bias_units
    active = jax.nn.gelu(inner, approximate=False).astype(BF)
    feed = fold(dot(active, down).reshape(groups, 2 * share, width), "dp", all_d)
    output, out_normal, out_inverse = layer_norm(
        first + feed + layer_bias[1], norm_gain[1], norm_shift[1]
    )
    output_low = output.astype(BF)

    place = rank * share + jnp.arange(share)
    leading = jnp.concatenate([place == 0, place == 0])[:, None]
    chosen = jnp.where(leading, output, dot(output_low, w_colbert) + layer_bias[2])
    inverse = lax.rsqrt(jnp.sum(chosen * chosen, axis=-1, keepdims=True) + 1e-06)
    unit = chosen * inverse
    vectors = unit.astype(BF)
    rows_q = spread(spread(vectors[:share], "tensor", far_t), "dp", near_d).reshape(-1, width)
    rows_p = spread(spread(vectors[share:], "dp", far_d), "tensor", near_t).reshape(-1, width)
    off_zt, off_xt = jnp.array(offsets(far_t)), jnp.array(offsets(near_t))
    off_yd, off_cd = jnp.array(offsets(far_d)), jnp.array(offsets(near_d))
    count_z, count_x, count_y, count_c = len(off_zt), len(off_xt), len(off_yd), len(off_cd)
    spot = jnp.arange(share)
    place_q = jnp.broadcast_to(
        ((rank ^ off_zt)[None, :, None] * share + spot[None, None, :]), (count_c, count_z, share)
    )
    group_q = group ^ off_cd
    length_q = query_lengths[group_q]
    valid_q = ((place_q >= 1) & (place_q < length_q[:, None, None])).reshape(-1)
    lead_q = (place_q == 0).reshape(-1)
    place_p = jnp.broadcast_to(
        ((rank ^ off_xt)[:, None, None] * share + spot[None, None, :]), (count_x, count_y, share)
    )
    group_p = group ^ off_yd
    length_p = passage_lengths[group_p]
    valid_p = (place_p >= 1) & (place_p < length_p[None, :, None])
    lead_p = place_p == 0
    scale = float(width) ** 0.5
    many_q = count_c * count_z * share
    dots = inner_rows(rows_p, rows_q).reshape(count_x, count_y, share, many_q)
    raised = jnp.where(valid_p[..., None], jnp.exp(dots * scale - scale), 0.0)
    sums = jnp.sum(raised, axis=(0, 2)).reshape(count_y, count_c, count_z, share)
    order = offsets(far_t)
    for step in far_t:
        came = swap(sums, "tensor", step)
        came = jnp.stack([came[:, :, order.index(item ^ step)] for item in order], axis=2)
        sums = sums + came
    late = scale * colbert_cot[group_q][:, group_p].T
    late = jnp.broadcast_to(late[:, :, None, None], (count_y, count_c, count_z, share))
    late = jnp.where(valid_q[None], late.reshape(count_y, many_q) / sums.reshape(count_y, many_q), 0.0)
    dense = 50.0 * dense_cot[group_q][:, group_p].T
    dense = jnp.broadcast_to(dense[:, :, None], (count_y, count_c, count_z * share)).reshape(count_y, many_q)
    dense = jnp.where(lead_q[None], dense, 0.0)
    pull = raised * late[None, :, None, :] + jnp.where(lead_p[..., None], dense[None, :, None, :], 0.0)
    pull = pull.astype(BF).reshape(-1, many_q)
    grad_q = fold(
        fold(outer_rows(pull, rows_p).reshape(count_c, count_z, share, width), "dp", near_d),
        "tensor",
        far_t,
    )
    grad_p = fold(
        fold(dot(pull, rows_q).reshape(count_x, count_y, share, width), "tensor", near_t), "dp", far_d
    )
    grad_vec = jnp.concatenate([grad_q, grad_p])

    grad_chosen = inverse * (grad_vec - unit * jnp.sum(grad_vec * unit, axis=-1, keepdims=True))
    grad_proj = jnp.where(leading, 0.0, grad_chosen).astype(BF)
    grad_out = jnp.where(leading, grad_chosen, 0.0) + inner_rows(grad_proj, w_colbert)
    colbert_bias = jnp.sum(grad_proj.astype(F32), axis=0)
    left = xored(output_low.reshape(2 * share, ranks, -1), "tensor", all_t, 1).reshape(2 * share, width)
    right = xored(grad_proj.reshape(2 * share, groups, -1), "dp", all_d, 1)
    colbert = jnp.stack([outer_rows(left, right[:, index]) for index in range(groups)])
    colbert = colbert.reshape(groups, ranks, width // ranks, width // groups)
    colbert = fold(fold(colbert, "dp", all_d), "tensor", all_t).astype(BF)
    colbert = spread(spread(colbert, "tensor", all_t), "dp", all_d)
    colbert = natural(natural(colbert, "dp", all_d, 0), "tensor", all_t, 1)
    colbert = colbert.transpose(1, 2, 0, 3).reshape(width, width).astype(F32)

    grad_mid, gain_two, shift_two = norm_back(grad_out, out_normal, out_inverse, norm_gain[1])
    feed_grad = spread(grad_mid.astype(BF), "dp", all_d).reshape(-1, width)
    grad_inner = (inner_rows(feed_grad, down) * gelu_slope(inner)).astype(BF)
    back = fold(dot(grad_inner, up).reshape(groups, 2 * share, width), "dp", all_d)
    grad_hidden, gain_one, shift_one = norm_back(
        grad_mid + back, first_normal, first_inverse, norm_gain[0]
    )
    attn_grad = grad_hidden.astype(BF)
    grad_context = inner_rows(attn_grad, out_all).astype(BF).reshape(2, share, ranks, columns)
    order = offsets(all_t)
    parts = []
    for index, item in enumerate(order):
        part = grad_context[:, :, index]
        parts.append(swap(part, "tensor", item) if item else part)
    heads_grad = natural(jnp.stack(parts, axis=1), "tensor", all_t, 1).reshape(2, span, columns)

    def unit_grads(left, right):
        whole = outer_rows(left, right).reshape(ranks, piece, width)
        own = fold(whole, "tensor", all_t).astype(BF)
        return natural(spread(own, "dp", all_d), "dp", all_d).reshape(hidden, width)

    grad_down = unit_grads(active, feed_grad).astype(F32)
    grad_up = unit_grads(grad_inner, normed).astype(F32).T
    grad_in_bias = natural(jnp.sum(grad_inner.astype(F32), axis=0).reshape(ranks, piece), "tensor", all_t)

    whole = outer_rows(context_rows, attn_grad).reshape(ranks, groups, slim, width).transpose(1, 0, 2, 3)
    whole = fold(xored(whole, "dp", all_d), "dp", all_d)
    own = fold(whole, "tensor", all_t).astype(BF)
    grad_w_out = natural(spread(own, "dp", all_d), "dp", all_d).reshape(columns, width).astype(F32)

    turned = attend_back(lens, query, key, value, heads_grad, lse)
    got = trade(turned.reshape(2, ranks, share, 3 * columns), all_t, 1)
    got = jnp.concatenate(got, axis=-1).reshape(2 * share, ranks * 3 * columns)
    slice_in = width // groups
    w_mine, _ = lax.optimization_barrier(
        (lax.dynamic_slice_in_dim(w_qkv, group * slice_in, slice_in, 1), output_low)
    )
    w_mine = w_mine.transpose(0, 2, 1).reshape(3 * columns, slice_in)
    w_back = spread(spread(w_mine, "tensor", all_t), "dp", all_d).reshape(groups, -1, slice_in)
    added = jnp.stack([dot(got, w_back[index]) for index in range(groups)])
    added = natural(added, "dp", all_d).transpose(1, 0, 2).reshape(2 * share, width)
    grad_tokens = grad_hidden + added
    tall = tokens.reshape(2 * span, width)
    turned = turned.reshape(2 * span, 3 * columns)
    grad_qkv = outer_rows(tall, turned)
    sums_qkv = jnp.sum(turned.astype(F32), axis=0, keepdims=True)
    grad_qkv = jnp.concatenate([grad_qkv, jnp.broadcast_to(sums_qkv, (8, 3 * columns))])
    for step in reversed(all_d):
        low = grad_qkv.astype(BF)
        grad_qkv = low.astype(F32) + swap(low, "dp", step).astype(F32)
    grad_w_qkv = grad_qkv[:width].reshape(width, 3, columns).transpose(1, 0, 2)
    sums_qkv = grad_qkv[width].reshape(3, columns)
    grad_qv_bias = jnp.stack([sums_qkv[0], sums_qkv[2]])

    spaced = jnp.where(
        (jnp.arange(groups) == group)[None, :, None], grad_in_bias[:, None, :], 0.0
    ).reshape(-1, width)
    small = jnp.concatenate(
        [
            jnp.stack(
                [
                    gain_one,
                    gain_two,
                    shift_one,
                    shift_two,
                    jnp.sum(grad_hidden, axis=0),
                    jnp.sum(grad_mid, axis=0),
                    colbert_bias,
                ]
            ),
            spaced,
        ]
    )
    small = lax.psum(small, ("dp", "tensor"))
    grad_in_bias = lax.dynamic_index_in_dim(small[7:].reshape(ranks, hidden), rank, 0, keepdims=False)
    return (
        output_low[:share],
        output_low[share:],
        grad_tokens[:share],
        grad_tokens[share:],
        grad_w_qkv,
        grad_qv_bias,
        grad_w_out,
        grad_up,
        grad_in_bias,
        grad_down,
        small[0:2],
        small[2:4],
        small[4:7],
        colbert,
    )


def solution(mesh):
    both = P(("dp", "tensor"), None)
    return jax.shard_map(
        per_device,
        mesh=mesh,
        in_specs=(
            P("dp", None),
            P("dp", None),
            P(),
            P(),
            P(None, None, "tensor"),
            P(None, "tensor"),
            P("tensor", None),
            P(None, "tensor"),
            P("tensor"),
            P("tensor", None),
            P(),
            P(),
            P(),
            P(),
            P(),
            P(),
        ),
        out_specs=(
            both,
            both,
            both,
            both,
            P(None, None, "tensor"),
            P(None, "tensor"),
            P("tensor", None),
            P(None, "tensor"),
            P("tensor"),
            P("tensor", None),
            P(),
            P(),
            P(),
            P(),
        ),
        check_vma=False,
    )
```

```python
import functools

import jax
import jax.numpy as jnp
from jax import lax
from jax.experimental import pallas as pl
from jax.experimental.pallas import tpu as pltpu
from jax.sharding import PartitionSpec as P

HEAD_DIM = 64
BF = jnp.bfloat16
F32 = jnp.float32
BLOCK = 256


def dot(left, right):
    return jnp.dot(left, right, preferred_element_type=F32)


def inner_rows(left, right):
    return lax.dot_general(left, right, (((1,), (1,)), ((), ())), preferred_element_type=F32)


def outer_rows(left, right):
    return lax.dot_general(left, right, (((0,), (0,)), ((), ())), preferred_element_type=F32)


def steps_of(size):
    steps = []
    while size > 1:
        size //= 2
        steps.append(size)
    return steps


def offsets(steps):
    found = [0]
    for step in steps:
        found = found + [item ^ step for item in found]
    return found


def swap(value, axis, step):
    size = lax.axis_size(axis)
    return lax.ppermute(value, axis, [(index, index ^ step) for index in range(size)])


def spread(value, axis, steps):
    held = value[None]
    for step in steps:
        held = jnp.concatenate([held, swap(held, axis, step)], axis=0)
    return held


def fold(parts, axis, steps):
    for step in reversed(steps):
        half = parts.shape[0] // 2
        came = swap(parts[half:].astype(BF), axis, step)
        parts = parts[:half].astype(F32) + came.astype(F32)
    return parts[0]


def natural(parts, axis, steps, dim=0):
    order = offsets(steps)
    size = len(order)
    place = [0] * size
    for spot, item in enumerate(order):
        place[item] = spot
    table = jnp.array(place, jnp.int32)
    rank = lax.axis_index(axis)
    return jnp.concatenate(
        [lax.dynamic_slice_in_dim(parts, table[item ^ rank], 1, dim) for item in range(size)], axis=dim
    )


def xored(parts, axis, steps, dim=0):
    rank = lax.axis_index(axis)
    return jnp.concatenate(
        [lax.dynamic_slice_in_dim(parts, item ^ rank, 1, dim) for item in offsets(steps)], axis=dim
    )


def trade(parts, steps, dim):
    rank = lax.axis_index("tensor")
    got = []
    for item in offsets(steps):
        piece = lax.dynamic_index_in_dim(parts, item ^ rank, dim, keepdims=False)
        got.append(swap(piece, "tensor", item) if item else piece)
    return got


def layer_norm(hidden, gain, shift):
    centre = hidden - jnp.mean(hidden, axis=-1, keepdims=True)
    inverse = lax.rsqrt(jnp.mean(centre * centre, axis=-1, keepdims=True) + 1e-05)
    normal = centre * inverse
    return (normal * gain + shift, normal, inverse)


def norm_back(grad, normal, inverse, gain):
    scaled = grad * gain
    middle = (
        scaled
        - jnp.mean(scaled, axis=-1, keepdims=True)
        - normal * jnp.mean(scaled * normal, axis=-1, keepdims=True)
    )
    return (middle * inverse, jnp.sum(grad * normal, axis=0), jnp.sum(grad, axis=0))


def gelu_slope(inner):
    return (
        0.5 * (1.0 + lax.erf(inner * 0.7071067811865476))
        + inner * jnp.exp(-0.5 * inner * inner) * 0.3989422804014327
    )


def head_mask(columns, head):
    lane = lax.broadcasted_iota(jnp.int32, (1, columns), 1)
    return (lane >= head * HEAD_DIM) & (lane < (head + 1) * HEAD_DIM)


def attend_kernel(lens, x, w, b, q, k, v, ctx, lse):
    span, columns = q.shape[1], q.shape[2]
    heads = columns // HEAD_DIM
    length = lens[pl.program_id(0)]
    scale = HEAD_DIM**-0.5
    rows = x[0]
    q[0] = (dot(rows, w[0]) + b[0:1, :].astype(F32)).astype(BF)
    k[0] = dot(rows, w[1]).astype(BF)
    v[0] = (dot(rows, w[2]) + b[1:2, :].astype(F32)).astype(BF)
    keys = k[0]
    values = v[0]
    keep = lax.broadcasted_iota(jnp.int32, (1, span), 1) < length
    block = min(BLOCK, span)

    @pl.loop(0, span // block)
    def _(index):
        at = pl.ds(pl.multiple_of(index * block, block), block)
        query = q[0, at, :]
        total = jnp.zeros((block, columns), F32)
        for head in range(heads):
            mask = head_mask(columns, head)
            mine = jnp.where(mask, query, jnp.zeros_like(query)) * jnp.asarray(scale, BF)
            scores = jnp.where(keep, inner_rows(mine, keys), -1e30)
            top = jnp.max(scores, axis=-1, keepdims=True)
            raised = jnp.exp(scores - top)
            mass = jnp.sum(raised, axis=-1, keepdims=True)
            part = dot(raised.astype(BF), values) / mass
            total = jnp.where(mask, part, total)
            column = jnp.broadcast_to(top + jnp.log(mass), (block, 128))
            lse[0, head : head + 1, at] = column.T[0:1, :]
        ctx[0, at, :] = total.astype(BF)


def attend_back_kernel(lens, q, k, v, g, lse, out, dk_sum, dv_sum):
    span, columns = q.shape[1], q.shape[2]
    heads = columns // HEAD_DIM
    length = lens[pl.program_id(0)]
    scale = HEAD_DIM**-0.5
    keys = k[0]
    values = v[0]
    keep = lax.broadcasted_iota(jnp.int32, (span, 1), 0) < length
    block = min(BLOCK, span)
    dk_sum[...] = jnp.zeros_like(dk_sum)
    dv_sum[...] = jnp.zeros_like(dv_sum)

    @pl.loop(0, span // block)
    def _(index):
        at = pl.ds(pl.multiple_of(index * block, block), block)
        query = q[0, at, :]
        grad = g[0, at, :]
        total = jnp.zeros((block, columns), F32)
        for head in range(heads):
            mask = head_mask(columns, head)
            mine = jnp.where(mask, query, jnp.zeros_like(query)) * jnp.asarray(scale, BF)
            back = jnp.where(mask, grad, jnp.zeros_like(grad))
            scores = jnp.where(keep, inner_rows(keys, mine), -1e30)
            probs = jnp.exp(scores - lse[0, head : head + 1, at])
            slope = inner_rows(values, back)
            middle = jnp.sum(probs * slope, axis=0, keepdims=True)
            turn = (probs * (slope - middle)).astype(BF)
            dv_sum[...] += dot(probs.astype(BF), back)
            dk_sum[...] += dot(turn, mine)
            part = outer_rows(turn, keys) * scale
            total = jnp.where(mask, part, total)
        out[0, at, 0:columns] = total.astype(BF)

    out[0, :, columns : 2 * columns] = dk_sum[...].astype(BF)
    out[0, :, 2 * columns : 3 * columns] = dv_sum[...].astype(BF)


def attend(lens, tokens, w_qkv, qv_bias):
    count, span, width = tokens.shape
    columns = w_qkv.shape[2]
    heads = columns // HEAD_DIM
    flat = jax.ShapeDtypeStruct((count, span, columns), BF)
    rows = pl.BlockSpec((1, span, columns), lambda i, n: (i, 0, 0))
    return pl.pallas_call(
        attend_kernel,
        out_shape=(flat, flat, flat, flat, jax.ShapeDtypeStruct((count, heads, span), F32)),
        grid_spec=pltpu.PrefetchScalarGridSpec(
            num_scalar_prefetch=1,
            grid=(count,),
            in_specs=[
                pl.BlockSpec((1, span, width), lambda i, n: (i, 0, 0)),
                pl.BlockSpec((3, width, columns), lambda i, n: (0, 0, 0)),
                pl.BlockSpec((2, columns), lambda i, n: (0, 0)),
            ],
            out_specs=[rows, rows, rows, rows, pl.BlockSpec((1, heads, span), lambda i, n: (i, 0, 0))],
        ),
        compiler_params=pltpu.CompilerParams(vmem_limit_bytes=48 * 2**20),
        cost_estimate=pl.CostEstimate(
            flops=20 * 10**9, bytes_accessed=8 * 2**20, transcendentals=count * heads * span * span
        ),
        name="attend",
    )(lens, tokens, w_qkv, qv_bias)


def attend_back(lens, query, key, value, grad, lse):
    count, span, columns = query.shape
    heads = columns // HEAD_DIM
    rows = pl.BlockSpec((1, span, columns), lambda i, n: (i, 0, 0))
    return pl.pallas_call(
        attend_back_kernel,
        out_shape=jax.ShapeDtypeStruct((count, span, 3 * columns), BF),
        grid_spec=pltpu.PrefetchScalarGridSpec(
            num_scalar_prefetch=1,
            grid=(count,),
            in_specs=[rows, rows, rows, rows, pl.BlockSpec((1, heads, span), lambda i, n: (i, 0, 0))],
            out_specs=pl.BlockSpec((1, span, 3 * columns), lambda i, n: (i, 0, 0)),
            scratch_shapes=[pltpu.VMEM((span, columns), F32), pltpu.VMEM((span, columns), F32)],
        ),
        compiler_params=pltpu.CompilerParams(vmem_limit_bytes=48 * 2**20),
        cost_estimate=pl.CostEstimate(
            flops=40 * 10**9, bytes_accessed=8 * 2**20, transcendentals=count * heads * span * span
        ),
        name="attend_back",
    )(lens, query, key, value, grad, lse)


MESH = pl.DeviceIdType.MESH


class Lattice:
    def __init__(self, steps):
        self.steps = steps
        self.count = 1 << len(steps)

    def peer(self, level):
        axis, step = self.steps[level]
        return {axis: lax.axis_index(axis) ^ step}

    def shift(self, mask):
        found = {"dp": 0, "tensor": 0}
        for level, (axis, step) in enumerate(self.steps):
            if mask >> level & 1:
                found[axis] ^= step
        return found["dp"], found["tensor"]


def remote(src, dst, send, recv, peer):
    return pltpu.make_async_remote_copy(
        src_ref=src, dst_ref=dst, send_sem=send, recv_sem=recv, device_id=peer, device_id_type=MESH
    )


class Gather:
    def __init__(self, lattice, view, send, recv, base=0, own=None):
        self.lattice, self.view, self.send, self.recv, self.base = lattice, view, send, recv, base
        self.own = own
        self.sent = []

    def copy(self, level, mask):
        slot = self.base + (1 << level) + mask
        place = self.view(mask)
        src = self.own if mask == 0 and self.own is not None else place
        return remote(src, place, self.send.at[slot], self.recv.at[slot], self.lattice.peer(level))

    def start(self):
        for level in range(len(self.lattice.steps)):
            copy = self.copy(level, 0)
            copy.start()
            self.sent.append(copy)

    def arrive(self, mask):
        level = mask.bit_length() - 1
        slot = self.base + mask
        place = self.view(mask)
        remote(place, place, self.send.at[slot], self.recv.at[slot], self.lattice.peer(level)).wait_recv()
        for later in range(level + 1, len(self.lattice.steps)):
            copy = self.copy(later, mask)
            copy.start()
            self.sent.append(copy)

    def finish(self):
        for copy in self.sent:
            copy.wait_send()


class Scatter:
    def __init__(self, lattice, read, write, out, came, send, recv, base=0):
        self.lattice, self.read, self.write = lattice, read, write
        self.out, self.came, self.send, self.recv, self.base = out, came, send, recv, base
        self.sent = []

    def push(self, mask):
        level = mask.bit_length() - 1
        slot = self.base + mask
        copy = remote(
            self.out.at[mask - 1],
            self.came.at[mask - 1],
            self.send.at[slot],
            self.recv.at[slot],
            self.lattice.peer(level),
        )
        copy.start()
        self.sent.append(copy)

    def put(self, mask):
        self.out[mask - 1] = self.read(mask).astype(BF)
        self.push(mask)

    def level(self, level):
        for mask in reversed(range(1 << level)):
            slot = (1 << level) + mask
            place = self.came.at[slot - 1]
            remote(
                self.out.at[slot - 1],
                place,
                self.send.at[self.base + slot],
                self.recv.at[self.base + slot],
                self.lattice.peer(level),
            ).wait_recv()
            total = self.read(mask) + self.came[slot - 1].astype(F32)
            if mask and mask >= 1 << (level - 1):
                self.out[mask - 1] = total.astype(BF)
                self.push(mask)
            else:
                self.write(mask, total)

    def run(self):
        for level in reversed(range(len(self.lattice.steps))):
            self.level(level)

    def finish(self):
        for copy in self.sent:
            copy.wait_send()


def greet(peers):
    barrier = pltpu.get_barrier_semaphore()
    for peer in peers:
        pl.semaphore_signal(barrier, inc=1, device_id=peer, device_id_type=MESH)
    pl.semaphore_wait(barrier, len(peers))


def score_kernel(
    far_t, near_t, far_d, near_d,
    vec, keep, lead, late, dense, grad,
    rows_q, rows_p, raised, pull, sums, sums_in, sum_q, out_q, in_q, sum_p, out_p, in_p,
    gq_send, gq_recv, gp_send, gp_recv, s_send, s_recv, rq_send, rq_recv, rp_send, rp_recv,
):
    group, rank = lax.axis_index("dp"), lax.axis_index("tensor")
    share, width = vec.shape[0] // 2, vec.shape[1]
    count_z = 1 << len(far_t)
    count_y = 1 << len(far_d)
    lattice_q = Lattice([("tensor", step) for step in far_t] + [("dp", step) for step in near_d])
    lattice_p = Lattice([("dp", step) for step in far_d] + [("tensor", step) for step in near_t])
    zs = [item for item in offsets(far_t) if item]
    peers = [{"tensor": rank ^ item} for item in zs + near_t]
    peers += [{"dp": group ^ item} for item in far_d + near_d]
    greet(peers)

    def spot_q(mask):
        d, t = lattice_q.shift(mask)
        return pl.multiple_of((((group ^ d) % 2) * count_z + (rank ^ t) // 2) * share, share)

    def spot_p(mask):
        d, t = lattice_p.shift(mask)
        return pl.multiple_of((((rank ^ t) % 2) * count_y + (group ^ d) // 2) * share, share)

    take_q = Gather(
        lattice_q, lambda m: rows_q.at[pl.ds(spot_q(m), share)], gq_send, gq_recv, own=vec.at[pl.ds(0, share)]
    )
    take_p = Gather(
        lattice_p, lambda m: rows_p.at[pl.ds(spot_p(m), share)], gp_send, gp_recv, own=vec.at[pl.ds(share, share)]
    )
    take_q.start()
    take_p.start()
    rows_q[pl.ds(spot_q(0), share), :] = vec[0:share, :]
    rows_p[pl.ds(spot_p(0), share), :] = vec[share : 2 * share, :]
    for mask in range(1, lattice_p.count):
        take_p.arrive(mask)
    for mask in range(1, lattice_q.count):
        take_q.arrive(mask)

    scale = float(width) ** 0.5
    sums[...] = jnp.zeros_like(sums)
    for block in range(lattice_p.count):
        at = slice(block * share, (block + 1) * share)
        dots = inner_rows(rows_p[at, :], rows_q[...])
        value = jnp.where(keep[at, 0:1] > 0.0, jnp.exp(dots * scale - scale), 0.0)
        raised[at, :] = value
        which = block % count_y
        sums[which : which + 1, :] += jnp.sum(value, axis=0, keepdims=True)
    copies = []
    for index, item in enumerate(zs):
        copy = remote(sums, sums_in.at[index], s_send.at[index], s_recv.at[index], {"tensor": rank ^ item})
        copy.start()
        copies.append(copy)
    total = sums[...]
    for index, copy in enumerate(copies):
        copy.wait_recv()
        total = total + sums_in[index]
    for block in range(lattice_p.count):
        at = slice(block * share, (block + 1) * share)
        which = block % count_y
        ratio = late[which : which + 1, :] / total[which : which + 1, :]
        pull[at, :] = (
            raised[at, :] * ratio + jnp.where(lead[at, 0:1] > 0.0, dense[which : which + 1, :], 0.0)
        ).astype(BF)

    half_q = count_z * share
    half_p = count_y * share
    mine_q, mine_p = group % 2, rank % 2

    def fill_q(half):
        at = pl.ds(pl.multiple_of(half * half_q, half_q), half_q)
        sum_q[at, :] = outer_rows(pull[:, at], rows_p[...])

    def fill_p(half):
        at = pl.ds(pl.multiple_of(half * half_p, half_p), half_p)
        sum_p[at, :] = dot(pull[at, :], rows_q[...])

    def reader(ref, spot):
        return lambda m: ref[pl.ds(spot(m), share), :]

    def writer(ref, spot):
        def write(m, value):
            ref[pl.ds(spot(m), share), :] = value

        return write

    give_q = Scatter(lattice_q, reader(sum_q, spot_q), writer(sum_q, spot_q), out_q, in_q, rq_send, rq_recv)
    give_p = Scatter(lattice_p, reader(sum_p, spot_p), writer(sum_p, spot_p), out_p, in_p, rp_send, rp_recv)
    fill_q(1 - mine_q)
    for mask in reversed(range(lattice_q.count // 2, lattice_q.count)):
        give_q.put(mask)
    fill_p(1 - mine_p)
    for mask in reversed(range(lattice_p.count // 2, lattice_p.count)):
        give_p.put(mask)
    fill_q(mine_q)
    give_q.level(len(lattice_q.steps) - 1)
    fill_p(mine_p)
    give_p.run()
    for level in reversed(range(len(lattice_q.steps) - 1)):
        give_q.level(level)
    grad[0:share, :] = sum_q[pl.ds(spot_q(0), share), :]
    grad[share : 2 * share, :] = sum_p[pl.ds(spot_p(0), share), :]
    for move in (take_q, take_p, give_q, give_p):
        move.finish()
    for copy in copies:
        copy.wait_send()


def score(vec, keep, lead, late, dense):
    groups, ranks = lax.axis_size("dp"), lax.axis_size("tensor")
    all_t, all_d = steps_of(ranks), steps_of(groups)
    share, width = vec.shape[0] // 2, vec.shape[1]
    blocks_q, blocks_p = ranks, groups
    many_q, many_p = blocks_q * share, blocks_p * share
    peers = ranks // 2 - 1
    dma = pltpu.SemaphoreType.DMA
    return pl.pallas_call(
        functools.partial(score_kernel, all_t[:-1], all_t[-1:], all_d[:-1], all_d[-1:]),
        out_shape=jax.ShapeDtypeStruct(vec.shape, F32),
        in_specs=[pl.BlockSpec(memory_space=pltpu.VMEM)] * 5,
        out_specs=pl.BlockSpec(memory_space=pltpu.VMEM),
        scratch_shapes=[
            pltpu.VMEM((many_q, width), BF),
            pltpu.VMEM((many_p, width), BF),
            pltpu.VMEM((many_p, many_q), F32),
            pltpu.VMEM((many_p, many_q), BF),
            pltpu.VMEM((8, many_q), F32),
            pltpu.VMEM((peers, 8, many_q), F32),
            pltpu.VMEM((many_q, width), F32),
            pltpu.VMEM((blocks_q - 1, share, width), BF),
            pltpu.VMEM((blocks_q - 1, share, width), BF),
            pltpu.VMEM((many_p, width), F32),
            pltpu.VMEM((blocks_p - 1, share, width), BF),
            pltpu.VMEM((blocks_p - 1, share, width), BF),
            dma((blocks_q,)), dma((blocks_q,)), dma((blocks_p,)), dma((blocks_p,)),
            dma((peers,)), dma((peers,)),
            dma((blocks_q,)), dma((blocks_q,)), dma((blocks_p,)), dma((blocks_p,)),
        ],
        compiler_params=pltpu.CompilerParams(
            collective_id=1, has_side_effects=True, vmem_limit_bytes=48 * 2**20
        ),
        cost_estimate=pl.CostEstimate(flops=4 * 2**30, bytes_accessed=4 * 2**20, transcendentals=2**19),
        name="score",
    )(vec, keep, lead, late, dense)


def per_device(
    queries,
    passages,
    query_lengths,
    passage_lengths,
    w_qkv,
    qv_bias,
    w_out,
    w_in,
    in_bias,
    w_down,
    norm_gain,
    norm_shift,
    layer_bias,
    w_colbert,
    dense_cot,
    colbert_cot,
):
    groups, ranks = lax.axis_size("dp"), lax.axis_size("tensor")
    group, rank = lax.axis_index("dp"), lax.axis_index("tensor")
    all_t, all_d = steps_of(ranks), steps_of(groups)
    far_t, near_t = all_t[:-1], all_t[-1:]
    far_d, near_d = all_d[:-1], all_d[-1:]
    span, width = queries.shape
    share = span // ranks
    columns = w_qkv.shape[2]
    hidden = w_in.shape[1]
    piece = hidden // groups

    up_mine = lax.dynamic_slice_in_dim(w_in, group * piece, piece, 1).T
    down_mine = lax.dynamic_slice_in_dim(w_down, group * piece, piece, 0)
    up = spread(up_mine, "tensor", all_t).reshape(-1, width)
    down = spread(down_mine, "tensor", all_t).reshape(-1, width)
    slim = columns // groups
    out_mine = lax.dynamic_slice_in_dim(w_out, group * slim, slim, 0)
    out_all = spread(spread(out_mine, "tensor", all_t), "dp", all_d)
    out_all = natural(out_all, "dp", all_d).transpose(1, 0, 2, 3).reshape(ranks * columns, width)
    bias_all = lax.all_gather(in_bias, "tensor").reshape(ranks, groups, piece)
    bias_mine = lax.dynamic_index_in_dim(bias_all, group, 1, keepdims=False)
    bias_units = xored(bias_mine, "tensor", all_t).reshape(-1).astype(F32)

    tokens = jnp.stack([queries, passages])
    lens = jnp.stack([query_lengths[group], passage_lengths[group]])
    query, key, value, context, lse = attend(lens, tokens, w_qkv, qv_bias)
    context = context.reshape(2, ranks, share, columns)
    context_rows = jnp.concatenate(trade(context, all_t, 1), axis=-1).reshape(2 * share, ranks * columns)

    mine = lax.dynamic_index_in_dim(
        tokens.reshape(2, ranks, share, width), rank, 1, keepdims=False
    ).reshape(2 * share, width)
    first, first_normal, first_inverse = layer_norm(
        mine.astype(F32) + dot(context_rows, out_all) + layer_bias[0], norm_gain[0], norm_shift[0]
    )
    normed = spread(first.astype(BF), "dp", all_d).reshape(-1, width)
    inner = inner_rows(normed, up) + bias_units
    active = jax.nn.gelu(inner, approximate=False).astype(BF)
    feed = fold(dot(active, down).reshape(groups, 2 * share, width), "dp", all_d)
    output, out_normal, out_inverse = layer_norm(
        first + feed + layer_bias[1], norm_gain[1], norm_shift[1]
    )
    output_low = output.astype(BF)

    place = rank * share + jnp.arange(share)
    leading = jnp.concatenate([place == 0, place == 0])[:, None]
    chosen = jnp.where(leading, output, dot(output_low, w_colbert) + layer_bias[2])
    inverse = lax.rsqrt(jnp.sum(chosen * chosen, axis=-1, keepdims=True) + 1e-06)
    unit = chosen * inverse
    vectors = unit.astype(BF)
    half_t, half_d = ranks // 2, groups // 2
    spot = jnp.arange(share)
    group_q = (group // 2) * 2 + jnp.arange(2)
    rank_q = jnp.arange(half_t) * 2 + rank % 2
    place_q = jnp.broadcast_to(rank_q[None, :, None] * share + spot[None, None, :], (2, half_t, share))
    valid_q = ((place_q >= 1) & (place_q < query_lengths[group_q][:, None, None])).reshape(-1)
    lead_q = (place_q == 0).reshape(-1)
    group_p = jnp.arange(half_d) * 2 + group % 2
    rank_p = (rank // 2) * 2 + jnp.arange(2)
    place_p = jnp.broadcast_to(rank_p[:, None, None] * share + spot[None, None, :], (2, half_d, share))
    valid_p = ((place_p >= 1) & (place_p < passage_lengths[group_p][None, :, None])).reshape(-1, 1)
    lead_p = (place_p == 0).reshape(-1, 1)
    scale = float(width) ** 0.5

    def along(table):
        wide = jnp.broadcast_to(table[group_q][:, group_p].T[:, :, None], (half_d, 2, half_t * share))
        return wide.reshape(half_d, -1)

    late = jnp.where(valid_q[None], scale * along(colbert_cot), 0.0)
    dense = jnp.where(lead_q[None], 50.0 * along(dense_cot), 0.0)
    grad_vec = score(vectors, valid_p.astype(F32), lead_p.astype(F32), late, dense)

    grad_chosen = inverse * (grad_vec - unit * jnp.sum(grad_vec * unit, axis=-1, keepdims=True))
    grad_proj = jnp.where(leading, 0.0, grad_chosen).astype(BF)
    grad_out = jnp.where(leading, grad_chosen, 0.0) + inner_rows(grad_proj, w_colbert)
    colbert_bias = jnp.sum(grad_proj.astype(F32), axis=0)
    left = xored(output_low.reshape(2 * share, ranks, -1), "tensor", all_t, 1).reshape(2 * share, width)
    right = xored(grad_proj.reshape(2 * share, groups, -1), "dp", all_d, 1)
    colbert = jnp.stack([outer_rows(left, right[:, index]) for index in range(groups)])
    colbert = colbert.reshape(groups, ranks, width // ranks, width // groups)
    colbert = fold(fold(colbert, "dp", all_d), "tensor", all_t).astype(BF)
    colbert = spread(spread(colbert, "tensor", all_t), "dp", all_d)
    colbert = natural(natural(colbert, "dp", all_d, 0), "tensor", all_t, 1)
    colbert = colbert.transpose(1, 2, 0, 3).reshape(width, width).astype(F32)

    grad_mid, gain_two, shift_two = norm_back(grad_out, out_normal, out_inverse, norm_gain[1])
    feed_grad = spread(grad_mid.astype(BF), "dp", all_d).reshape(-1, width)
    grad_inner = (inner_rows(feed_grad, down) * gelu_slope(inner)).astype(BF)
    back = fold(dot(grad_inner, up).reshape(groups, 2 * share, width), "dp", all_d)
    grad_hidden, gain_one, shift_one = norm_back(
        grad_mid + back, first_normal, first_inverse, norm_gain[0]
    )
    attn_grad = grad_hidden.astype(BF)
    grad_context = inner_rows(attn_grad, out_all).astype(BF).reshape(2, share, ranks, columns)
    order = offsets(all_t)
    parts = []
    for index, item in enumerate(order):
        part = grad_context[:, :, index]
        parts.append(swap(part, "tensor", item) if item else part)
    heads_grad = natural(jnp.stack(parts, axis=1), "tensor", all_t, 1).reshape(2, span, columns)

    def unit_grads(left, right):
        whole = outer_rows(left, right).reshape(ranks, piece, width)
        own = fold(whole, "tensor", all_t).astype(BF)
        return natural(spread(own, "dp", all_d), "dp", all_d).reshape(hidden, width)

    grad_down = unit_grads(active, feed_grad).astype(F32)
    grad_up = unit_grads(grad_inner, normed).astype(F32).T
    grad_in_bias = natural(jnp.sum(grad_inner.astype(F32), axis=0).reshape(ranks, piece), "tensor", all_t)

    whole = outer_rows(context_rows, attn_grad).reshape(ranks, groups, slim, width).transpose(1, 0, 2, 3)
    whole = fold(xored(whole, "dp", all_d), "dp", all_d)
    own = fold(whole, "tensor", all_t).astype(BF)
    grad_w_out = natural(spread(own, "dp", all_d), "dp", all_d).reshape(columns, width).astype(F32)

    turned = attend_back(lens, query, key, value, heads_grad, lse)
    got = trade(turned.reshape(2, ranks, share, 3 * columns), all_t, 1)
    got = jnp.concatenate(got, axis=-1).reshape(2 * share, ranks * 3 * columns)
    slice_in = width // groups
    w_mine, _ = lax.optimization_barrier(
        (lax.dynamic_slice_in_dim(w_qkv, group * slice_in, slice_in, 1), output_low)
    )
    w_mine = w_mine.transpose(0, 2, 1).reshape(3 * columns, slice_in)
    w_back = spread(spread(w_mine, "tensor", all_t), "dp", all_d).reshape(groups, -1, slice_in)
    added = jnp.stack([dot(got, w_back[index]) for index in range(groups)])
    added = natural(added, "dp", all_d).transpose(1, 0, 2).reshape(2 * share, width)
    grad_tokens = grad_hidden + added
    tall = tokens.reshape(2 * span, width)
    turned = turned.reshape(2 * span, 3 * columns)
    grad_qkv = outer_rows(tall, turned)
    sums_qkv = jnp.sum(turned.astype(F32), axis=0, keepdims=True)
    grad_qkv = jnp.concatenate([grad_qkv, jnp.broadcast_to(sums_qkv, (8, 3 * columns))])
    for step in reversed(all_d):
        low = grad_qkv.astype(BF)
        grad_qkv = low.astype(F32) + swap(low, "dp", step).astype(F32)
    grad_w_qkv = grad_qkv[:width].reshape(width, 3, columns).transpose(1, 0, 2)
    sums_qkv = grad_qkv[width].reshape(3, columns)
    grad_qv_bias = jnp.stack([sums_qkv[0], sums_qkv[2]])

    spaced = jnp.where(
        (jnp.arange(groups) == group)[None, :, None], grad_in_bias[:, None, :], 0.0
    ).reshape(-1, width)
    small = jnp.concatenate(
        [
            jnp.stack(
                [
                    gain_one,
                    gain_two,
                    shift_one,
                    shift_two,
                    jnp.sum(grad_hidden, axis=0),
                    jnp.sum(grad_mid, axis=0),
                    colbert_bias,
                ]
            ),
            spaced,
        ]
    )
    small = lax.psum(small, ("dp", "tensor"))
    grad_in_bias = lax.dynamic_index_in_dim(small[7:].reshape(ranks, hidden), rank, 0, keepdims=False)
    return (
        output_low[:share],
        output_low[share:],
        grad_tokens[:share],
        grad_tokens[share:],
        grad_w_qkv,
        grad_qv_bias,
        grad_w_out,
        grad_up,
        grad_in_bias,
        grad_down,
        small[0:2],
        small[2:4],
        small[4:7],
        colbert,
    )


def solution(mesh):
    both = P(("dp", "tensor"), None)
    return jax.shard_map(
        per_device,
        mesh=mesh,
        in_specs=(
            P("dp", None),
            P("dp", None),
            P(),
            P(),
            P(None, None, "tensor"),
            P(None, "tensor"),
            P("tensor", None),
            P(None, "tensor"),
            P("tensor"),
            P("tensor", None),
            P(),
            P(),
            P(),
            P(),
            P(),
            P(),
        ),
        out_specs=(
            both,
            both,
            both,
            both,
            P(None, None, "tensor"),
            P(None, "tensor"),
            P("tensor", None),
            P(None, "tensor"),
            P("tensor"),
            P("tensor", None),
            P(),
            P(),
            P(),
            P(),
        ),
        check_vma=False,
    )
```

```python
import functools

import jax
import jax.numpy as jnp
from jax import lax
from jax.experimental import pallas as pl
from jax.experimental.pallas import tpu as pltpu
from jax.sharding import PartitionSpec as P

HEAD_DIM = 64
BF = jnp.bfloat16
F32 = jnp.float32
BLOCK = 256


def dot(left, right):
    return jnp.dot(left, right, preferred_element_type=F32)


def inner_rows(left, right):
    return lax.dot_general(left, right, (((1,), (1,)), ((), ())), preferred_element_type=F32)


def outer_rows(left, right):
    return lax.dot_general(left, right, (((0,), (0,)), ((), ())), preferred_element_type=F32)


def steps_of(size):
    steps = []
    while size > 1:
        size //= 2
        steps.append(size)
    return steps


def offsets(steps):
    found = [0]
    for step in steps:
        found = found + [item ^ step for item in found]
    return found


def swap(value, axis, step):
    size = lax.axis_size(axis)
    return lax.ppermute(value, axis, [(index, index ^ step) for index in range(size)])


def spread(value, axis, steps):
    held = value[None]
    for step in steps:
        held = jnp.concatenate([held, swap(held, axis, step)], axis=0)
    return held


def fold(parts, axis, steps):
    for step in reversed(steps):
        half = parts.shape[0] // 2
        came = swap(parts[half:].astype(BF), axis, step)
        parts = parts[:half].astype(F32) + came.astype(F32)
    return parts[0]


def natural(parts, axis, steps, dim=0):
    order = offsets(steps)
    size = len(order)
    place = [0] * size
    for spot, item in enumerate(order):
        place[item] = spot
    table = jnp.array(place, jnp.int32)
    rank = lax.axis_index(axis)
    return jnp.concatenate(
        [lax.dynamic_slice_in_dim(parts, table[item ^ rank], 1, dim) for item in range(size)], axis=dim
    )


def xored(parts, axis, steps, dim=0):
    rank = lax.axis_index(axis)
    return jnp.concatenate(
        [lax.dynamic_slice_in_dim(parts, item ^ rank, 1, dim) for item in offsets(steps)], axis=dim
    )


def trade(parts, steps, dim):
    rank = lax.axis_index("tensor")
    got = []
    for item in offsets(steps):
        piece = lax.dynamic_index_in_dim(parts, item ^ rank, dim, keepdims=False)
        got.append(swap(piece, "tensor", item) if item else piece)
    return got


def layer_norm(hidden, gain, shift):
    centre = hidden - jnp.mean(hidden, axis=-1, keepdims=True)
    inverse = lax.rsqrt(jnp.mean(centre * centre, axis=-1, keepdims=True) + 1e-05)
    normal = centre * inverse
    return (normal * gain + shift, normal, inverse)


def norm_back(grad, normal, inverse, gain):
    scaled = grad * gain
    middle = (
        scaled
        - jnp.mean(scaled, axis=-1, keepdims=True)
        - normal * jnp.mean(scaled * normal, axis=-1, keepdims=True)
    )
    return (middle * inverse, jnp.sum(grad * normal, axis=0), jnp.sum(grad, axis=0))


def gelu_slope(inner):
    return (
        0.5 * (1.0 + lax.erf(inner * 0.7071067811865476))
        + inner * jnp.exp(-0.5 * inner * inner) * 0.3989422804014327
    )


def head_mask(columns, head):
    lane = lax.broadcasted_iota(jnp.int32, (1, columns), 1)
    return (lane >= head * HEAD_DIM) & (lane < (head + 1) * HEAD_DIM)


MESH = pl.DeviceIdType.MESH


class Lattice:
    def __init__(self, steps):
        self.steps = steps
        self.count = 1 << len(steps)

    def peer(self, level):
        axis, step = self.steps[level]
        return {axis: lax.axis_index(axis) ^ step}

    def shift(self, mask):
        found = {"dp": 0, "tensor": 0}
        for level, (axis, step) in enumerate(self.steps):
            if mask >> level & 1:
                found[axis] ^= step
        return found["dp"], found["tensor"]


def remote(src, dst, send, recv, peer):
    return pltpu.make_async_remote_copy(
        src_ref=src, dst_ref=dst, send_sem=send, recv_sem=recv, device_id=peer, device_id_type=MESH
    )


class Gather:
    def __init__(self, lattice, view, send, recv, base=0, own=None):
        self.lattice, self.view, self.send, self.recv, self.base = lattice, view, send, recv, base
        self.own = own
        self.sent = []

    def copy(self, level, mask):
        slot = self.base + (1 << level) + mask
        place = self.view(mask)
        src = self.own if mask == 0 and self.own is not None else place
        return remote(src, place, self.send.at[slot], self.recv.at[slot], self.lattice.peer(level))

    def start(self):
        for level in range(len(self.lattice.steps)):
            copy = self.copy(level, 0)
            copy.start()
            self.sent.append(copy)

    def arrive(self, mask):
        level = mask.bit_length() - 1
        slot = self.base + mask
        place = self.view(mask)
        remote(place, place, self.send.at[slot], self.recv.at[slot], self.lattice.peer(level)).wait_recv()
        for later in range(level + 1, len(self.lattice.steps)):
            copy = self.copy(later, mask)
            copy.start()
            self.sent.append(copy)

    def finish(self):
        for copy in self.sent:
            copy.wait_send()


class Scatter:
    def __init__(self, lattice, read, write, out, came, send, recv, base=0):
        self.lattice, self.read, self.write = lattice, read, write
        self.out, self.came, self.send, self.recv, self.base = out, came, send, recv, base
        self.sent = []

    def push(self, mask):
        level = mask.bit_length() - 1
        slot = self.base + mask
        copy = remote(
            self.out.at[mask - 1],
            self.came.at[mask - 1],
            self.send.at[slot],
            self.recv.at[slot],
            self.lattice.peer(level),
        )
        copy.start()
        self.sent.append(copy)

    def put(self, mask):
        self.out[mask - 1] = self.read(mask).astype(BF)
        self.push(mask)

    def level(self, level):
        for mask in reversed(range(1 << level)):
            slot = (1 << level) + mask
            place = self.came.at[slot - 1]
            remote(
                self.out.at[slot - 1],
                place,
                self.send.at[self.base + slot],
                self.recv.at[self.base + slot],
                self.lattice.peer(level),
            ).wait_recv()
            total = self.read(mask) + self.came[slot - 1].astype(F32)
            if mask and mask >= 1 << (level - 1):
                self.out[mask - 1] = total.astype(BF)
                self.push(mask)
            else:
                self.write(mask, total)

    def run(self):
        for level in reversed(range(len(self.lattice.steps))):
            self.level(level)

    def finish(self):
        for copy in self.sent:
            copy.wait_send()


def greet(peers):
    barrier = pltpu.get_barrier_semaphore()
    for peer in peers:
        pl.semaphore_signal(barrier, inc=1, device_id=peer, device_id_type=MESH)
    pl.semaphore_wait(barrier, len(peers))


def score_kernel(
    far_t, near_t, far_d, near_d,
    vec, keep, lead, late, dense, grad,
    rows_q, rows_p, raised, pull, sums, sums_in, sum_q, out_q, in_q, sum_p, out_p, in_p,
    gq_send, gq_recv, gp_send, gp_recv, s_send, s_recv, rq_send, rq_recv, rp_send, rp_recv,
):
    group, rank = lax.axis_index("dp"), lax.axis_index("tensor")
    share, width = vec.shape[0] // 2, vec.shape[1]
    count_z = 1 << len(far_t)
    count_y = 1 << len(far_d)
    lattice_q = Lattice([("tensor", step) for step in far_t] + [("dp", step) for step in near_d])
    lattice_p = Lattice([("dp", step) for step in far_d] + [("tensor", step) for step in near_t])
    zs = [item for item in offsets(far_t) if item]
    peers = [{"tensor": rank ^ item} for item in zs + near_t]
    peers += [{"dp": group ^ item} for item in far_d + near_d]
    greet(peers)

    def spot_q(mask):
        d, t = lattice_q.shift(mask)
        return pl.multiple_of((((group ^ d) % 2) * count_z + (rank ^ t) // 2) * share, share)

    def spot_p(mask):
        d, t = lattice_p.shift(mask)
        return pl.multiple_of((((rank ^ t) % 2) * count_y + (group ^ d) // 2) * share, share)

    take_q = Gather(
        lattice_q, lambda m: rows_q.at[pl.ds(spot_q(m), share)], gq_send, gq_recv, own=vec.at[pl.ds(0, share)]
    )
    take_p = Gather(
        lattice_p, lambda m: rows_p.at[pl.ds(spot_p(m), share)], gp_send, gp_recv, own=vec.at[pl.ds(share, share)]
    )
    take_q.start()
    take_p.start()
    rows_q[pl.ds(spot_q(0), share), :] = vec[0:share, :]
    rows_p[pl.ds(spot_p(0), share), :] = vec[share : 2 * share, :]
    for mask in range(1, lattice_p.count):
        take_p.arrive(mask)
    for mask in range(1, lattice_q.count):
        take_q.arrive(mask)

    scale = float(width) ** 0.5
    sums[...] = jnp.zeros_like(sums)
    for block in range(lattice_p.count):
        at = slice(block * share, (block + 1) * share)
        dots = inner_rows(rows_p[at, :], rows_q[...])
        value = jnp.where(keep[at, 0:1] > 0.0, jnp.exp(dots * scale - scale), 0.0)
        raised[at, :] = value
        which = block % count_y
        sums[which : which + 1, :] += jnp.sum(value, axis=0, keepdims=True)
    copies = []
    for index, item in enumerate(zs):
        copy = remote(sums, sums_in.at[index], s_send.at[index], s_recv.at[index], {"tensor": rank ^ item})
        copy.start()
        copies.append(copy)
    total = sums[...]
    for index, copy in enumerate(copies):
        copy.wait_recv()
        total = total + sums_in[index]
    for block in range(lattice_p.count):
        at = slice(block * share, (block + 1) * share)
        which = block % count_y
        ratio = late[which : which + 1, :] / total[which : which + 1, :]
        pull[at, :] = (
            raised[at, :] * ratio + jnp.where(lead[at, 0:1] > 0.0, dense[which : which + 1, :], 0.0)
        ).astype(BF)

    half_q = count_z * share
    half_p = count_y * share
    mine_q, mine_p = group % 2, rank % 2

    def fill_q(half):
        at = pl.ds(pl.multiple_of(half * half_q, half_q), half_q)
        sum_q[at, :] = outer_rows(pull[:, at], rows_p[...])

    def fill_p(half):
        at = pl.ds(pl.multiple_of(half * half_p, half_p), half_p)
        sum_p[at, :] = dot(pull[at, :], rows_q[...])

    def reader(ref, spot):
        return lambda m: ref[pl.ds(spot(m), share), :]

    def writer(ref, spot):
        def write(m, value):
            ref[pl.ds(spot(m), share), :] = value

        return write

    give_q = Scatter(lattice_q, reader(sum_q, spot_q), writer(sum_q, spot_q), out_q, in_q, rq_send, rq_recv)
    give_p = Scatter(lattice_p, reader(sum_p, spot_p), writer(sum_p, spot_p), out_p, in_p, rp_send, rp_recv)
    fill_q(1 - mine_q)
    for mask in reversed(range(lattice_q.count // 2, lattice_q.count)):
        give_q.put(mask)
    fill_p(1 - mine_p)
    for mask in reversed(range(lattice_p.count // 2, lattice_p.count)):
        give_p.put(mask)
    fill_q(mine_q)
    give_q.level(len(lattice_q.steps) - 1)
    fill_p(mine_p)
    give_p.run()
    for level in reversed(range(len(lattice_q.steps) - 1)):
        give_q.level(level)
    grad[0:share, :] = sum_q[pl.ds(spot_q(0), share), :]
    grad[share : 2 * share, :] = sum_p[pl.ds(spot_p(0), share), :]
    for move in (take_q, take_p, give_q, give_p):
        move.finish()
    for copy in copies:
        copy.wait_send()


def score(vec, keep, lead, late, dense):
    groups, ranks = lax.axis_size("dp"), lax.axis_size("tensor")
    all_t, all_d = steps_of(ranks), steps_of(groups)
    share, width = vec.shape[0] // 2, vec.shape[1]
    blocks_q, blocks_p = ranks, groups
    many_q, many_p = blocks_q * share, blocks_p * share
    peers = ranks // 2 - 1
    dma = pltpu.SemaphoreType.DMA
    return pl.pallas_call(
        functools.partial(score_kernel, all_t[:-1], all_t[-1:], all_d[:-1], all_d[-1:]),
        out_shape=jax.ShapeDtypeStruct(vec.shape, F32),
        in_specs=[pl.BlockSpec(memory_space=pltpu.VMEM)] * 5,
        out_specs=pl.BlockSpec(memory_space=pltpu.VMEM),
        scratch_shapes=[
            pltpu.VMEM((many_q, width), BF),
            pltpu.VMEM((many_p, width), BF),
            pltpu.VMEM((many_p, many_q), F32),
            pltpu.VMEM((many_p, many_q), BF),
            pltpu.VMEM((8, many_q), F32),
            pltpu.VMEM((peers, 8, many_q), F32),
            pltpu.VMEM((many_q, width), F32),
            pltpu.VMEM((blocks_q - 1, share, width), BF),
            pltpu.VMEM((blocks_q - 1, share, width), BF),
            pltpu.VMEM((many_p, width), F32),
            pltpu.VMEM((blocks_p - 1, share, width), BF),
            pltpu.VMEM((blocks_p - 1, share, width), BF),
            dma((blocks_q,)), dma((blocks_q,)), dma((blocks_p,)), dma((blocks_p,)),
            dma((peers,)), dma((peers,)),
            dma((blocks_q,)), dma((blocks_q,)), dma((blocks_p,)), dma((blocks_p,)),
        ],
        compiler_params=pltpu.CompilerParams(
            collective_id=1, has_side_effects=True, vmem_limit_bytes=48 * 2**20
        ),
        cost_estimate=pl.CostEstimate(flops=4 * 2**30, bytes_accessed=4 * 2**20, transcendentals=2**19),
        name="score",
    )(vec, keep, lead, late, dense)


def forward_kernel(
    all_t, all_d, ship_bias,
    keep, x_q, x_p, w_qkv, qv_bias, w_out, up_piece, w_down, qkv_piece, bias_in, gain, shift, offset, w_colbert,
    o_q, o_k, o_v, o_lse, o_ctx, o_out, o_up, o_down, o_qkv, o_normed, o_inner, o_active,
    o_normal, o_vec, o_unit, o_low, o_spread,
    x, q, k, v, ctx, lse, ctx_rows, out_all, up, down, normed, inner, active, sums, s_out, s_in,
    first, normal, unit, vec, low, scales, wc, bias_all, bias_row,
    local, g_send, g_recv, a_send, a_recv, b_send, b_recv, n_send, n_recv, r_send, r_recv,
):
    group, rank = lax.axis_index("dp"), lax.axis_index("tensor")
    ranks, groups = 1 << len(all_t), 1 << len(all_d)
    span, width = x_q.shape
    columns = w_qkv.shape[2]
    share = span // ranks
    piece = up_piece.shape[0]
    units = up.shape[0]
    half, half3 = columns // 2, qkv_piece.shape[0]
    rows = groups * share
    heads = columns // HEAD_DIM
    scale = HEAD_DIM**-0.5

    x_copies = [pltpu.make_async_copy(src, x.at[s], local.at[s]) for s, src in enumerate((x_q, x_p))]
    for copy in x_copies:
        copy.start()
    wc_copy = pltpu.make_async_copy(w_colbert, wc, local.at[2])
    wc_copy.start()
    greet([{"tensor": rank ^ item} for item in range(1, ranks)] + [{"dp": group ^ item} for item in all_d])

    tensor = Lattice([("tensor", step) for step in all_t])
    both = Lattice([("tensor", step) for step in all_t] + [("dp", all_d[-1])])
    data = Lattice([("dp", step) for step in all_d])

    def halves(ref, size):
        def view(mask):
            d, t = both.shift(mask)
            return ref.at[rank ^ t, pl.ds(pl.multiple_of(((group ^ d) % 2) * size, size), size)]

        return view

    def unit_rows(ref):
        return lambda mask: ref.at[pl.ds(pl.multiple_of((rank ^ tensor.shift(mask)[1]) * piece, piece), piece)]

    wide, tall = both.count, tensor.count
    at_half = pl.ds(pl.multiple_of((group % 2) * half, half), half)
    at_piece = pl.ds(pl.multiple_of(group * piece, piece), piece)
    take_out = Gather(both, halves(out_all, half), g_send, g_recv, 0, own=w_out.at[at_half])
    take_up = Gather(tensor, unit_rows(up), g_send, g_recv, wide, own=up_piece)
    take_down = Gather(tensor, unit_rows(down), g_send, g_recv, wide + tall, own=w_down.at[at_piece])
    take_qkv = Gather(both, halves(o_qkv, half3), g_send, g_recv, wide + 2 * tall, own=qkv_piece)
    own_copies = [
        pltpu.make_async_copy(w_out.at[at_half], take_out.view(0), local.at[3]),
        pltpu.make_async_copy(up_piece, take_up.view(0), local.at[4]),
        pltpu.make_async_copy(w_down.at[at_piece], take_down.view(0), local.at[5]),
        pltpu.make_async_copy(qkv_piece, take_qkv.view(0), local.at[6]),
    ]
    take_out.start()
    take_up.start()
    for copy in own_copies:
        copy.start()
    pending = []
    bias_copies = []
    if ship_bias:
        bias_all[rank] = bias_in[...]
        for item in range(1, ranks):
            copy = remote(
                bias_in, bias_all.at[rank], b_send.at[item], b_recv.at[item], {"tensor": rank ^ item}
            )
            copy.start()
            bias_copies.append(copy)

    def project(s):
        x_copies[s].wait()
        tokens = x[s]
        q[s] = (dot(tokens, w_qkv[0]) + qv_bias[0:1, :].astype(F32)).astype(BF)
        k[s] = dot(tokens, w_qkv[1]).astype(BF)
        v[s] = (dot(tokens, w_qkv[2]) + qv_bias[1:2, :].astype(F32)).astype(BF)

    block = min(BLOCK, span)

    def attention(s, begin, end):
        @pl.loop(begin, end)
        def _(index):
            at = pl.ds(pl.multiple_of(index * block, block), block)
            query = q[s, at, :]
            total = jnp.zeros((block, columns), F32)
            for head in range(heads):
                mask = head_mask(columns, head)
                mine = jnp.where(mask, query, jnp.zeros_like(query)) * jnp.asarray(scale, BF)
                scores = inner_rows(mine, k[s]) + keep[s : s + 1, :]
                top = jnp.max(scores, axis=-1, keepdims=True)
                raised = jnp.exp(scores - top)
                mass = jnp.sum(raised, axis=-1, keepdims=True)
                part = dot(raised.astype(BF), v[s]) / mass
                total = jnp.where(mask, part, total)
                column = jnp.broadcast_to(top + jnp.log(mass), (block, 128))
                lse[s, head : head + 1, at] = column.T[0:1, :]
            ctx[s, at, :] = total.astype(BF)

    sends = []

    def trade_context(s):
        at = pl.ds(s * share, share)
        for item in range(1, ranks):
            peer = rank ^ item
            copy = remote(
                ctx.at[s, pl.ds(pl.multiple_of(peer * share, share), share)],
                ctx_rows.at[rank, at],
                a_send.at[s * ranks + item],
                a_recv.at[s * ranks + item],
                {"tensor": peer},
            )
            copy.start()
            sends.append(copy)
        ctx_rows[rank, s * share : (s + 1) * share, :] = ctx[s, pl.ds(pl.multiple_of(rank * share, share), share), :]

    def context_here(s):
        at = pl.ds(s * share, share)
        for item in range(1, ranks):
            place = ctx_rows.at[rank ^ item, at]
            remote(
                place, place, a_send.at[s * ranks + item], a_recv.at[s * ranks + item], {"tensor": rank ^ item}
            ).wait_recv()

    def out_going(src, dst, index):
        copy = pltpu.make_async_copy(src, dst, local.at[index])
        copy.start()
        pending.append(copy)

    project(0)
    attention(0, 0, span // block)
    trade_context(0)
    for copy in own_copies:
        copy.wait()
    for mask in range(1, tall // 2):
        take_out.arrive(mask)
    take_down.start()
    project(1)
    attention(1, 0, span // block // 2)
    for mask in range(1, tall // 2):
        take_up.arrive(mask)
    attention(1, span // block // 2, span // block)
    trade_context(1)
    for mask in range(tall // 2, wide):
        take_out.arrive(mask)
    out_going(q, o_q, 7)
    out_going(k, o_k, 8)
    out_going(v, o_v, 9)
    out_going(lse, o_lse, 10)

    normed_takes = []
    for s in range(2):
        at = slice(s * share, (s + 1) * share)
        context_here(s)
        if columns % 128 == 0:
            mix = jnp.concatenate([ctx_rows[r, at, :] for r in range(ranks)], axis=1)
            mixed = dot(mix, out_all[...].reshape(ranks * columns, width))
        else:
            mixed = dot(ctx_rows[0, at, :], out_all[0])
            for r in range(1, ranks):
                mixed = mixed + dot(ctx_rows[r, at, :], out_all[r])
        mine = x[s, pl.ds(pl.multiple_of(rank * share, share), share), :].astype(F32)
        value, plain, inverse = layer_norm(mine + mixed + offset[0:1, :], gain[0:1, :], shift[0:1, :])
        first[at, :] = value
        normal[0, at, :] = plain
        scales[0, at, :] = jnp.broadcast_to(inverse, (share, 128))
        own = pl.ds(pl.multiple_of(group * share, share), share)
        normed[s, own, :] = value.astype(BF)

        def view(mask, s=s):
            d, _ = data.shift(mask)
            return normed.at[s, pl.ds(pl.multiple_of((group ^ d) * share, share), share)]

        taking = Gather(data, view, n_send, n_recv, s * groups)
        taking.start()
        normed_takes.append(taking)
        for mask in range(1, tall // 2):
            if s == 0:
                take_down.arrive(mask)
    take_qkv.start()
    if ship_bias:
        for item in range(1, ranks):
            place = bias_all.at[rank ^ item]
            remote(place, place, b_send.at[item], b_recv.at[item], {"tensor": rank ^ item}).wait_recv()
        for r in range(ranks):
            bias_row[0:1, r * piece : (r + 1) * piece] = bias_all[r, 0:1, :].astype(F32)
    else:
        bias_row[0:1, :] = bias_in[0:1, :]
    for mask in range(tall // 2, tall):
        take_up.arrive(mask)
    for taking in normed_takes:
        for mask in range(1, groups):
            taking.arrive(mask)

    def spot(mask):
        return pl.multiple_of((group ^ data.shift(mask)[0]) * share, share)

    gives = []
    for s in range(2):

        def read(mask, s=s):
            return sums[s, pl.ds(spot(mask), share), :]

        def write(mask, value, s=s):
            sums[s, pl.ds(spot(mask), share), :] = value

        gives.append(Scatter(data, read, write, s_out.at[s], s_in.at[s], r_send, r_recv, s * groups))

    tile = min(256, units)

    def expand(s):
        at_rows = slice(s * rows, (s + 1) * rows)

        @pl.loop(0, units // tile)
        def _(index):
            at = pl.ds(pl.multiple_of(index * tile, tile), tile)
            value = inner_rows(normed[s], up[at, :]) + bias_row[0:1, at]
            phi = 0.5 * (1.0 + lax.erf(value * 0.7071067811865476))
            active[at_rows, at] = (value * phi).astype(BF)
            inner[at_rows, at] = (phi + value * jnp.exp(-0.5 * value * value) * 0.3989422804014327).astype(BF)

    def reduce(s):
        at_rows = slice(s * rows, (s + 1) * rows)

        @pl.loop(0, width // 256)
        def _(index):
            at = pl.ds(pl.multiple_of(index * 256, 256), 256)
            sums[s, :, at] = dot(active[at_rows, :], down[:, at])

        for mask in reversed(range(groups // 2, groups)):
            gives[s].put(mask)

    expand(0)
    for mask in range(tall // 2, tall):
        take_down.arrive(mask)
    reduce(0)
    for mask in range(1, tall // 2):
        take_qkv.arrive(mask)
    expand(1)
    gives[0].level(len(all_d) - 1)
    reduce(1)
    out_going(ctx_rows, o_ctx, 11)
    out_going(out_all, o_out, 12)
    out_going(up, o_up, 13)
    out_going(down, o_down, 14)
    out_going(normed, o_normed, 15)
    out_going(inner, o_inner, 16)
    out_going(active, o_active, 17)
    gives[1].level(len(all_d) - 1)
    wc_copy.wait()
    for s in range(2):
        at = slice(s * share, (s + 1) * share)
        for level in reversed(range(len(all_d) - 1)):
            gives[s].level(level)
        feed = gives[s].read(0)
        value, plain, inverse = layer_norm(first[at, :] + feed + offset[1:2, :], gain[1:2, :], shift[1:2, :])
        normal[1, at, :] = plain
        scales[1, at, :] = jnp.broadcast_to(inverse, (share, 128))
        short = value.astype(BF)
        low[at, :] = short
        place = lax.broadcasted_iota(jnp.int32, (share, 1), 0) + rank * share
        chosen = jnp.where(place == 0, value, dot(short, wc[...]) + offset[2:3, :])
        inverse = lax.rsqrt(jnp.sum(chosen * chosen, axis=-1, keepdims=True) + 1e-06)
        scales[2, at, :] = jnp.broadcast_to(inverse, (share, 128))
        unit[at, :] = chosen * inverse
        vec[at, :] = unit[at, :].astype(BF)
    out_going(normal, o_normal, 18)
    out_going(unit, o_unit, 19)
    out_going(vec, o_vec, 20)
    out_going(low, o_low, 21)
    out_going(scales, o_spread, 22)
    for mask in range(tall // 2, wide):
        take_qkv.arrive(mask)
    for move in [take_out, take_up, take_down, take_qkv] + normed_takes + gives:
        move.finish()
    for copy in sends + bias_copies:
        copy.wait_send()
    for copy in pending:
        copy.wait()


def forward(keep, queries, passages, w_qkv, qv_bias, w_out, up_piece, w_down, qkv_piece, bias_in, gain, shift, offset, w_colbert):
    groups, ranks = lax.axis_size("dp"), lax.axis_size("tensor")
    all_t, all_d = steps_of(ranks), steps_of(groups)
    span, width = queries.shape
    columns = w_qkv.shape[2]
    heads = columns // HEAD_DIM
    share = span // ranks
    piece = up_piece.shape[0]
    units = piece * ranks
    rows = groups * share
    ship_bias = bias_in.shape[0] == 16

    shapes = [
        ((2, span, columns), BF),
        ((2, span, columns), BF),
        ((2, span, columns), BF),
        ((2, heads, span), F32),
        ((ranks, 2 * share, columns), BF),
        ((ranks, columns, width), BF),
        ((units, width), BF),
        ((units, width), BF),
        ((ranks, 3 * columns, width), BF),
        ((2, rows, width), BF),
        ((2 * rows, units), BF),
        ((2 * rows, units), BF),
        ((2, 2 * share, width), F32),
        ((2 * share, width), BF),
        ((2 * share, width), F32),
        ((2 * share, width), BF),
        ((3, 2 * share, 128), F32),
    ]
    dma = pltpu.SemaphoreType.DMA
    vmem = pltpu.VMEM
    hold, leave = pl.BlockSpec(memory_space=pltpu.VMEM), pl.BlockSpec(memory_space=pl.ANY)
    n_gather = 6 * ranks
    return pl.pallas_call(
        functools.partial(forward_kernel, all_t, all_d, ship_bias),
        out_shape=[jax.ShapeDtypeStruct(*item) for item in shapes],
        in_specs=[hold, leave, leave, hold, hold, leave, leave, leave, leave, hold, hold, hold, hold, leave],
        out_specs=[leave] * len(shapes),
        scratch_shapes=[
            vmem((2, span, width), BF),
            vmem((2, span, columns), BF),
            vmem((2, span, columns), BF),
            vmem((2, span, columns), BF),
            vmem((2, span, columns), BF),
            vmem((2, heads, span), F32),
            vmem((ranks, 2 * share, columns), BF),
            vmem((ranks, columns, width), BF),
            vmem((units, width), BF),
            vmem((units, width), BF),
            vmem((2, rows, width), BF),
            vmem((2 * rows, units), BF),
            vmem((2 * rows, units), BF),
            vmem((2, rows, width), F32),
            vmem((2, groups - 1, share, width), BF),
            vmem((2, groups - 1, share, width), BF),
            vmem((2 * share, width), F32),
            vmem((2, 2 * share, width), F32),
            vmem((2 * share, width), F32),
            vmem((2 * share, width), BF),
            vmem((2 * share, width), BF),
            vmem((3, 2 * share, 128), F32),
            vmem((width, width), BF),
            vmem((ranks, 16, piece), BF),
            vmem((8, units), F32),
            dma((23,)),
            dma((n_gather,)), dma((n_gather,)),
            dma((2 * ranks,)), dma((2 * ranks,)),
            dma((ranks,)), dma((ranks,)),
            dma((2 * groups,)), dma((2 * groups,)),
            dma((2 * groups,)), dma((2 * groups,)),
        ],
        compiler_params=pltpu.CompilerParams(
            collective_id=2, has_side_effects=True, vmem_limit_bytes=58 * 2**20
        ),
        cost_estimate=pl.CostEstimate(flops=10**11, bytes_accessed=40 * 2**20, transcendentals=2**23),
        name="forward",
    )(keep, queries, passages, w_qkv, qv_bias, w_out, up_piece, w_down, qkv_piece, bias_in, gain, shift, offset, w_colbert)


class Settle:
    def __init__(self, lattice, view, came, send, recv, base=0):
        self.lattice, self.view, self.came = lattice, view, came
        self.send, self.recv, self.base = send, recv, base
        self.sent = []

    def copy(self, mask):
        return remote(
            self.view(mask),
            self.came.at[mask - 1],
            self.send.at[self.base + mask],
            self.recv.at[self.base + mask],
            self.lattice.peer(mask.bit_length() - 1),
        )

    def push(self, mask):
        copy = self.copy(mask)
        copy.start()
        self.sent.append(copy)

    def start(self):
        for mask in reversed(range(self.lattice.count // 2, self.lattice.count)):
            self.push(mask)

    def level(self, level):
        for mask in reversed(range(1 << level)):
            slot = (1 << level) + mask
            self.copy(slot).wait_recv()
            place = self.view(mask)
            place[...] = (place[...].astype(F32) + self.came[slot - 1].astype(F32)).astype(BF)
            if mask and mask >= 1 << (level - 1):
                self.push(mask)

    def finish(self):
        for copy in self.sent:
            copy.wait_send()


def backward_kernel(
    all_t, all_d,
    keep, grad_vec, h_unit, h_low, h_scales, h_normals, h_wc, h_down, h_up, h_slope, h_active, h_normed,
    h_out, h_ctx, h_q, h_k, h_v, h_lse, x_q, x_p, h_qkv, gain,
    o_tokens, o_down, o_up, o_out, o_wc, o_qkv, o_small,
    pool, slope, active, out_all, wc, ctx_rows, q, k, v, lse, g1, unit, low, proj, normals, scales, sums,
    s_out, s_in, turn, ctx_out, heads_grad, turned, turned_rows, dk_sum, dv_sum,
    g_down, g_down_in, g_up, g_up_in, g_out_in, g_wc_in, qkv_sum, qkv_low, qkv_in,
    small, small_in, stage, stage_in,
    local, n_send, n_recv, r_send, r_recv, d_send, d_recv, u_send, u_recv, w_send, w_recv, c_send, c_recv,
    a_send, a_recv, t_send, t_recv, f_send, f_recv, m_send, m_recv, y_send, y_recv, q_send, q_recv,
):
    group, rank = lax.axis_index("dp"), lax.axis_index("tensor")
    ranks, groups = 1 << len(all_t), 1 << len(all_d)
    far_d = all_d[:-1]
    span, width = x_q.shape
    columns = q.shape[2]
    share = span // ranks
    units = h_up.shape[0]
    piece = units // ranks
    half = columns // 2
    rows = groups * share
    heads = columns // HEAD_DIM
    scale = HEAD_DIM**-0.5
    flat = width // ranks // 2
    at_up, at_down = pl.ds(0, units), pl.ds(units, units)
    at_normed, at_feed = pl.ds(2 * units, 2 * rows), pl.ds(2 * units + 2 * rows, 2 * rows)
    feed_at = 2 * units + 2 * rows

    loads = []

    def load(src, dst):
        copy = pltpu.make_async_copy(src, dst, local.at[len(loads)])
        copy.start()
        loads.append(copy)
        return copy

    early = [load(grad_vec, g1), load(h_unit, unit), load(h_scales, scales), load(h_low, low), load(h_wc, wc)]
    early.append(load(h_normals, normals))
    ffn = [load(h_down, pool.at[at_down]), load(h_slope, slope), load(h_up, pool.at[at_up])]
    later = [load(h_active, active), load(h_normed, pool.at[at_normed])]
    last = [load(h_out, out_all), load(h_ctx, ctx_rows)]
    heads_in = [load(h_q, q), load(h_k, k), load(h_v, v), load(h_lse, lse)]
    greet([{"tensor": rank ^ item} for item in range(1, ranks)] + [{"dp": group ^ item} for item in all_d])

    tensor = Lattice([("tensor", step) for step in all_t])
    both = Lattice([("tensor", step) for step in all_t] + [("dp", all_d[-1])])
    data = Lattice([("dp", step) for step in all_d])

    def halves(ref, size):
        def view(mask):
            d, t = both.shift(mask)
            return ref.at[pl.ds(pl.multiple_of(((rank ^ t) * 2 + (group ^ d) % 2) * size, size), size)]

        return view

    def pieces(ref):
        return lambda mask: ref.at[pl.ds(pl.multiple_of((rank ^ tensor.shift(mask)[1]) * piece, piece), piece)]

    def spot(mask):
        return pl.multiple_of((group ^ data.shift(mask)[0]) * share, share)

    give_wc = Settle(both, halves(wc, flat), g_wc_in, c_send, c_recv)
    give_out = Settle(both, halves(out_all, half), g_out_in, w_send, w_recv)
    give_down = Settle(tensor, pieces(g_down), g_down_in, d_send, d_recv)
    give_up = Settle(tensor, pieces(g_up), g_up_in, u_send, u_recv)

    small[...] = jnp.zeros_like(small)
    for copy in early:
        copy.wait()
    takes = []
    for s in range(2):
        at = slice(s * share, (s + 1) * share)
        grad, plain = g1[at, :], unit[at, :]
        chosen = scales[2, at, 0:1] * (grad - plain * jnp.sum(grad * plain, axis=-1, keepdims=True))
        leading = lax.broadcasted_iota(jnp.int32, (share, 1), 0) + rank * share == 0
        short = jnp.where(leading, 0.0, chosen).astype(BF)
        proj[at, :] = short
        grad = jnp.where(leading, chosen, 0.0) + inner_rows(short, wc[...])
        middle, gains, shifts = norm_back(grad, normals[1, at, :], scales[1, at, 0:1], gain[1:2, :])
        g1[at, :] = middle
        small[0, 1:2, :] += gains[None, :]
        small[0, 3:4, :] += shifts[None, :]
        small[0, 5:6, :] += jnp.sum(middle, axis=0, keepdims=True)
        small[0, 6:7, :] += jnp.sum(short.astype(F32), axis=0, keepdims=True)
        own = pl.multiple_of(feed_at + s * rows + group * share, share)
        pool[pl.ds(own, share), :] = middle.astype(BF)

        def view(mask, s=s):
            place = feed_at + s * rows + (group ^ data.shift(mask)[0]) * share
            return pool.at[pl.ds(pl.multiple_of(place, share), share)]

        taking = Gather(data, view, n_send, n_recv, s * groups)
        taking.start()
        takes.append(taking)

    @pl.loop(0, width // 256)
    def _(index):
        at = pl.ds(pl.multiple_of(index * 256, 256), 256)
        wc[at, :] = outer_rows(low[:, at], proj[...]).astype(BF)

    give_wc.start()

    gives = []
    for s in range(2):

        def read(mask, s=s):
            return sums[s, pl.ds(spot(mask), share), :]

        def write(mask, value, s=s):
            sums[s, pl.ds(spot(mask), share), :] = value

        gives.append(Scatter(data, read, write, s_out.at[s], s_in.at[s], r_send, r_recv, s * groups))
    for copy in ffn:
        copy.wait()
    tile = min(256, units)

    def shrink(s):
        for mask in range(1, groups):
            takes[s].arrive(mask)
        at_rows = slice(s * rows, (s + 1) * rows)
        feed_rows = slice(feed_at + s * rows, feed_at + (s + 1) * rows)

        @pl.loop(0, units // tile)
        def _(index):
            at = pl.ds(pl.multiple_of(index * tile, tile), tile)
            down_at = pl.ds(pl.multiple_of(units + index * tile, tile), tile)
            value = inner_rows(pool[feed_rows, :], pool[down_at, :]) * slope[at_rows, at].astype(F32)
            value = value.astype(BF)
            slope[at_rows, at] = value
            small[0, 7:8, at] += jnp.sum(value.astype(F32), axis=0, keepdims=True)

        @pl.loop(0, width // 256)
        def _(index):
            at = pl.ds(pl.multiple_of(index * 256, 256), 256)
            sums[s, :, at] = dot(slope[at_rows, :], pool[at_up, at])

    def put(s):
        for mask in reversed(range(groups // 2, groups)):
            gives[s].put(mask)

    top = len(all_d) - 1
    shrink(0)
    put(0)
    give_wc.level(len(all_t))
    shrink(1)
    gives[0].level(top)
    put(1)
    for copy in later:
        copy.wait()

    @pl.loop(0, units // tile)
    def _(index):
        at = pl.ds(pl.multiple_of(index * tile, tile), tile)
        g_down[at, :] = outer_rows(active[:, at], pool[at_feed, :]).astype(BF)

    gives[1].level(top)
    give_down.start()
    give_wc.level(len(all_t) - 1)

    @pl.loop(0, units // tile)
    def _(index):
        at = pl.ds(pl.multiple_of(index * tile, tile), tile)
        g_up[at, :] = outer_rows(slope[:, at], pool[at_normed, :]).astype(BF)

    for copy in last:
        copy.wait()
    sends = []
    for s in range(2):
        at = slice(s * share, (s + 1) * share)
        for level in reversed(range(top)):
            gives[s].level(level)
        grad = g1[at, :] + gives[s].read(0)
        hidden, gains, shifts = norm_back(grad, normals[0, at, :], scales[0, at, 0:1], gain[0:1, :])
        g1[at, :] = hidden
        small[0, 0:1, :] += gains[None, :]
        small[0, 2:3, :] += shifts[None, :]
        small[0, 4:5, :] += jnp.sum(hidden, axis=0, keepdims=True)
        short = hidden.astype(BF)
        turn[at, :] = short
        if columns % 128 == 0:
            value = inner_rows(short, out_all[...]).astype(BF)
            for r in range(ranks):
                ctx_out[r, at, :] = value[:, r * columns : (r + 1) * columns]
        else:
            for r in range(ranks):
                ctx_out[r, at, :] = inner_rows(short, out_all[r * columns : (r + 1) * columns, :]).astype(BF)
        mine = pl.ds(pl.multiple_of(rank * share, share), share)
        for item in range(1, ranks):
            copy = remote(
                ctx_out.at[rank ^ item, pl.ds(s * share, share)],
                heads_grad.at[s, mine],
                a_send.at[s * ranks + item],
                a_recv.at[s * ranks + item],
                {"tensor": rank ^ item},
            )
            copy.start()
            sends.append(copy)
        heads_grad[s, mine, :] = ctx_out[rank, at, :]
    give_up.start()
    for taking in takes:
        taking.finish()
    tall = load(x_q, pool.at[pl.ds(0, span)]), load(x_p, pool.at[pl.ds(span, span)])
    at_qkv = 2 * span
    back_in = load(h_qkv, pool.at[pl.ds(at_qkv, 3 * columns * ranks)])

    for r in range(ranks):
        out_all[r * columns : (r + 1) * columns, :] = outer_rows(ctx_rows[r], turn[...]).astype(BF)
    give_out.start()

    def small_step(level):
        copy = remote(
            small.at[level], small_in.at[level], m_send.at[level], m_recv.at[level], {"tensor": rank ^ all_t[level]}
        )
        return copy

    small_copies = [small_step(level) for level in range(len(all_t))]
    small_copies[0].start()

    def small_next(level):
        small_copies[level].wait_recv()
        small[level + 1] = small[level] + small_in[level]
        if level + 1 < len(all_t):
            small_copies[level + 1].start()

    block = min(BLOCK, span)

    def attention(s, begin, end):
        @pl.loop(begin, end)
        def _(index):
            at = pl.ds(pl.multiple_of(index * block, block), block)
            query = q[s, at, :]
            grad = heads_grad[s, at, :]
            total = jnp.zeros((block, columns), F32)
            for head in range(heads):
                mask = head_mask(columns, head)
                mine = jnp.where(mask, query, jnp.zeros_like(query)) * jnp.asarray(scale, BF)
                back = jnp.where(mask, grad, jnp.zeros_like(grad))
                scores = inner_rows(k[s], mine) + keep[:, s : s + 1]
                probs = jnp.exp(scores - lse[s, head : head + 1, at])
                slant = inner_rows(v[s], back)
                middle = jnp.sum(probs * slant, axis=0, keepdims=True)
                twist = (probs * (slant - middle)).astype(BF)
                dv_sum[...] += dot(probs.astype(BF), back)
                dk_sum[...] += dot(twist, mine)
                part = outer_rows(twist, k[s]) * scale
                total = jnp.where(mask, part, total)
            turned[s, at, 0:columns] = total.astype(BF)

    def attention_start(s):
        for item in range(1, ranks):
            place = heads_grad.at[s, pl.ds(pl.multiple_of((rank ^ item) * share, share), share)]
            remote(
                place, place, a_send.at[s * ranks + item], a_recv.at[s * ranks + item], {"tensor": rank ^ item}
            ).wait_recv()
        dk_sum[...] = jnp.zeros_like(dk_sum)
        dv_sum[...] = jnp.zeros_like(dv_sum)

    def attention_end(s):
        turned[s, :, columns : 2 * columns] = dk_sum[...].astype(BF)
        turned[s, :, 2 * columns : 3 * columns] = dv_sum[...].astype(BF)
        for item in range(1, ranks):
            copy = remote(
                turned.at[s, pl.ds(pl.multiple_of((rank ^ item) * share, share), share)],
                turned_rows.at[rank, pl.ds(s * share, share)],
                t_send.at[s * ranks + item],
                t_recv.at[s * ranks + item],
                {"tensor": rank ^ item},
            )
            copy.start()
            sends.append(copy)
        turned_rows[rank, s * share : (s + 1) * share, :] = turned[
            s, pl.ds(pl.multiple_of(rank * share, share), share), :
        ]

    many = qkv_sum.shape[0]

    def qkv_grad(s):
        tokens = pool[s * span : (s + 1) * span, :]
        line = jnp.sum(turned[s].astype(F32), axis=0, keepdims=True)
        if s == 0:
            qkv_sum[0:width, :] = outer_rows(tokens, turned[s])
            qkv_sum[width:many, :] = jnp.broadcast_to(line, (many - width, 3 * columns))
        else:
            qkv_sum[0:width, :] += outer_rows(tokens, turned[s])
            qkv_sum[width:many, :] += jnp.broadcast_to(line, (many - width, 3 * columns))

    for copy in heads_in:
        copy.wait()
    attention_start(0)
    attention(0, 0, span // block // 2)
    give_wc.level(len(all_t) - 2)
    small_next(0)
    attention(0, span // block // 2, span // block)
    attention_end(0)
    give_out.level(len(all_t))
    for copy in tall:
        copy.wait()
    qkv_grad(0)
    attention_start(1)
    attention(1, 0, span // block // 2)
    for level in reversed(range(len(all_t) - 2)):
        give_wc.level(level)
    small_next(1)
    give_down.level(len(all_t) - 1)
    attention(1, span // block // 2, span // block)
    attention_end(1)
    qkv_grad(1)

    part = many // 2
    mine_half, other_half = group % 2, 1 - group % 2
    at_mine = pl.ds(pl.multiple_of(mine_half * part, part), part)
    at_other = pl.ds(pl.multiple_of(other_half * part, part), part)
    qkv_low[0] = qkv_sum[at_other, :].astype(BF)
    near = {"dp": group ^ all_d[-1]}
    qkv_copy = remote(qkv_low.at[0], qkv_in.at[0], q_send.at[0], q_recv.at[0], near)
    qkv_copy.start()

    def settle_stage(which, source, size):
        copies = []
        base = which * (len(far_d) + 1)
        for index, step in enumerate(far_d):
            src = source if index == 0 else stage.at[base + index - 1, pl.ds(0, size)]
            dst = stage_in.at[base + index, pl.ds(0, size)]
            slot = base + index
            copies.append(remote(src, dst, y_send.at[slot], y_recv.at[slot], {"dp": group ^ step}))

        def begin():
            copies[0].start()

        def end():
            value = source[...]
            for index, copy in enumerate(copies):
                copy.wait_recv()
                value = (value.astype(F32) + stage_in[base + index, 0:size, :].astype(F32)).astype(BF)
                stage[base + index, 0:size, :] = value
                if index + 1 < len(copies):
                    copies[index + 1].start()
            return stage.at[base + len(copies) - 1, pl.ds(0, size)]

        return begin, end, copies

    wc_begin, wc_end, wc_copies = settle_stage(0, give_wc.view(0), flat)
    out_begin, out_end, out_copies = settle_stage(1, give_out.view(0), half)
    wc_begin()
    for level in reversed(range(len(all_t))):
        if level < len(all_t):
            give_out.level(level)
    out_begin()
    small_next(2) if len(all_t) > 2 else None
    for level in range(3, len(all_t)):
        small_next(level)
    small_own = small.at[len(all_t)]
    small_take = Gather(data, lambda m: o_small.at[group ^ data.shift(m)[0]], f_send, f_recv, 0, own=small_own)
    small_take.start()
    small_copy = load(small_own, o_small.at[group])
    qkv_copy.wait_recv()
    sum_half = qkv_sum[at_mine, :].astype(BF).astype(F32) + qkv_in[0].astype(F32)
    qkv_low[1] = sum_half.astype(BF)
    qkv_copies = [qkv_copy]
    for index, step in enumerate(far_d):
        copy = remote(
            qkv_low.at[1 + index], qkv_in.at[1 + index], q_send.at[1 + index], q_recv.at[1 + index], {"dp": group ^ step}
        )
        qkv_copies.append(copy)
    qkv_copies[1].start()
    wc_own = wc_end()
    wc_take = Gather(both, halves(o_wc, flat), f_send, f_recv, groups, own=wc_own)
    wc_take.start()
    wc_copy = load(wc_own, wc_take.view(0))
    for level in reversed(range(len(all_t) - 1)):
        give_down.level(level)
    down_own = give_down.view(0)

    def dp_view(ref):
        return lambda m: ref.at[pl.ds(pl.multiple_of((group ^ data.shift(m)[0]) * piece, piece), piece)]

    down_take = Gather(data, dp_view(o_down), f_send, f_recv, groups + both.count, own=down_own)
    down_take.start()
    down_copy = load(down_own, down_take.view(0))
    for index in range(len(far_d)):
        qkv_copies[1 + index].wait_recv()
        qkv_low[2 + index] = (qkv_low[1 + index].astype(F32) + qkv_in[1 + index].astype(F32)).astype(BF)
        if index + 2 < len(qkv_copies):
            qkv_copies[index + 2].start()
    qkv_own = qkv_low.at[1 + len(far_d)]
    last_qkv = remote(qkv_own, o_qkv.at[at_mine], q_send.at[1 + len(far_d)], q_recv.at[1 + len(far_d)], near)
    last_qkv.start()
    qkv_copies.append(last_qkv)
    qkv_local = load(qkv_own, o_qkv.at[at_mine])
    out_own = out_end()

    def out_view(mask):
        return o_out.at[pl.ds(pl.multiple_of(((group % 2) ^ mask) * half, half), half)]

    core = Lattice([("dp", all_d[-1])])
    out_take = Gather(core, out_view, f_send, f_recv, 2 * groups + both.count, own=out_own)
    out_take.start()
    out_copy = load(out_own, out_view(0))
    for mask in range(1, both.count // 2):
        wc_take.arrive(mask)

    back_in.wait()
    for s in range(2):
        at = slice(s * share, (s + 1) * share)
        for item in range(1, ranks):
            place = turned_rows.at[rank ^ item, pl.ds(s * share, share)]
            remote(
                place, place, t_send.at[s * ranks + item], t_recv.at[s * ranks + item], {"tensor": rank ^ item}
            ).wait_recv()
        total = g1[at, :]
        for r in range(ranks):
            begin = at_qkv + r * 3 * columns
            total = total + dot(turned_rows[r, at, :], pool[begin : begin + 3 * columns, :])
        unit[at, :] = total
    tokens_copy = load(unit, o_tokens)
    for level in reversed(range(len(all_t))):
        give_up.level(level)
    up_own = give_up.view(0)
    up_take = Gather(data, dp_view(o_up), f_send, f_recv, 2 * groups + both.count + 2, own=up_own)
    up_take.start()
    up_copy = load(up_own, up_take.view(0))
    for mask in range(both.count // 2, both.count):
        wc_take.arrive(mask)
    for taking in (small_take, down_take, up_take):
        for mask in range(1, groups):
            taking.arrive(mask)
    out_take.arrive(1)
    at_theirs = o_qkv.at[at_other]
    remote(at_theirs, at_theirs, q_send.at[1 + len(far_d)], q_recv.at[1 + len(far_d)], near).wait_recv()
    for move in [give_wc, give_out, give_down, give_up, small_take, wc_take, down_take, up_take, out_take] + gives:
        move.finish()
    for copy in sends + small_copies + qkv_copies + wc_copies + out_copies:
        copy.wait_send()
    for copy in (tokens_copy, small_copy, wc_copy, down_copy, qkv_local, out_copy, up_copy):
        copy.wait()


def backward(keep, grad_vec, unit, low, scales, normals, w_colbert, down, up, slope, active, normed, out_all,
             context_rows, query, key, value, lse, queries, passages, qkv_all, gain):
    groups, ranks = lax.axis_size("dp"), lax.axis_size("tensor")
    all_t, all_d = steps_of(ranks), steps_of(groups)
    span, width = queries.shape
    columns = query.shape[2]
    heads = columns // HEAD_DIM
    share = span // ranks
    units = up.shape[0]
    piece = units // ranks
    rows = groups * share
    half, flat = columns // 2, width // ranks // 2
    pool = max(2 * units + 4 * rows, 2 * span + 3 * columns * ranks)
    many = width + 32
    far = len(all_d) - 1
    dma = pltpu.SemaphoreType.DMA
    vmem = pltpu.VMEM
    hold, leave = pl.BlockSpec(memory_space=pltpu.VMEM), pl.BlockSpec(memory_space=pl.ANY)
    shapes = [
        ((2 * share, width), F32),
        ((units // ranks * groups, width), BF),
        ((units // ranks * groups, width), BF),
        ((columns, width), BF),
        ((width, width), BF),
        ((many, 3 * columns), BF),
        ((groups, 8, width), F32),
    ]
    pair = lambda count: [dma((count,)), dma((count,))]
    return pl.pallas_call(
        functools.partial(backward_kernel, all_t, all_d),
        out_shape=[jax.ShapeDtypeStruct(*item) for item in shapes],
        in_specs=[hold] + [leave] * 20 + [hold],
        out_specs=[leave] * len(shapes),
        scratch_shapes=[
            vmem((pool, width), BF),
            vmem((2 * rows, units), BF),
            vmem((2 * rows, units), BF),
            vmem((ranks * columns, width), BF),
            vmem((width, width), BF),
            vmem((ranks, 2 * share, columns), BF),
            vmem((2, span, columns), BF),
            vmem((2, span, columns), BF),
            vmem((2, span, columns), BF),
            vmem((2, heads, span), F32),
            vmem((2 * share, width), F32),
            vmem((2 * share, width), F32),
            vmem((2 * share, width), BF),
            vmem((2 * share, width), BF),
            vmem((2, 2 * share, width), F32),
            vmem((3, 2 * share, 128), F32),
            vmem((2, rows, width), F32),
            vmem((2, groups - 1, share, width), BF),
            vmem((2, groups - 1, share, width), BF),
            vmem((2 * share, width), BF),
            vmem((ranks, 2 * share, columns), BF),
            vmem((2, span, columns), BF),
            vmem((2, span, 3 * columns), BF),
            vmem((ranks, 2 * share, 3 * columns), BF),
            vmem((span, columns), F32),
            vmem((span, columns), F32),
            vmem((units, width), BF),
            vmem((ranks - 1, piece, width), BF),
            vmem((units, width), BF),
            vmem((ranks - 1, piece, width), BF),
            vmem((2 * ranks - 1, half, width), BF),
            vmem((2 * ranks - 1, flat, width), BF),
            vmem((many, 3 * columns), F32),
            vmem((2 + far, many // 2, 3 * columns), BF),
            vmem((1 + far, many // 2, 3 * columns), BF),
            vmem((len(all_t) + 1, 8, width), F32),
            vmem((len(all_t), 8, width), F32),
            vmem((2 * (far + 1), max(half, flat), width), BF),
            vmem((2 * (far + 1), max(half, flat), width), BF),
            dma((32,)),
        ]
        + pair(2 * groups)
        + pair(2 * groups)
        + pair(ranks)
        + pair(ranks)
        + pair(2 * ranks)
        + pair(2 * ranks)
        + pair(2 * ranks)
        + pair(2 * ranks)
        + pair(3 * groups + 2 * ranks + 2)
        + pair(len(all_t))
        + pair(2 * (far + 1))
        + pair(2 + far),
        compiler_params=pltpu.CompilerParams(
            collective_id=3, has_side_effects=True, vmem_limit_bytes=62 * 2**20
        ),
        cost_estimate=pl.CostEstimate(flops=10**11, bytes_accessed=40 * 2**20, transcendentals=2**22),
        name="backward",
    )(keep, grad_vec, unit, low, scales, normals, w_colbert, down, up, slope, active, normed, out_all,
      context_rows, query, key, value, lse, queries, passages, qkv_all, gain)


def per_device(
    queries,
    passages,
    query_lengths,
    passage_lengths,
    w_qkv,
    qv_bias,
    w_out,
    w_in,
    in_bias,
    w_down,
    norm_gain,
    norm_shift,
    layer_bias,
    w_colbert,
    dense_cot,
    colbert_cot,
):
    groups, ranks = lax.axis_size("dp"), lax.axis_size("tensor")
    group, rank = lax.axis_index("dp"), lax.axis_index("tensor")
    all_t, all_d = steps_of(ranks), steps_of(groups)
    span, width = queries.shape
    share = span // ranks
    columns = w_qkv.shape[2]
    hidden = w_in.shape[1]
    piece = hidden // groups

    up_piece = lax.dynamic_slice_in_dim(w_in, group * piece, piece, 1).T
    turned = w_qkv.transpose(0, 2, 1).reshape(3 * columns, width)
    qkv_piece = lax.dynamic_slice_in_dim(turned, (group % 2) * (3 * columns // 2), 3 * columns // 2, 0)
    if piece % 128 == 0:
        bias_in = lax.dynamic_slice_in_dim(in_bias, group * piece, piece, 0)
        bias_in = jnp.broadcast_to(bias_in[None, :], (16, piece))
    else:
        bias_in = lax.all_gather(in_bias, "tensor").reshape(ranks, groups, piece)
        bias_in = lax.dynamic_index_in_dim(bias_in, group, 1, keepdims=False).reshape(1, -1).astype(F32)
    lens = jnp.stack([query_lengths[group], passage_lengths[group]])
    keep = jnp.where(jnp.arange(span)[None, :] < lens[:, None], 0.0, -1e30)
    (
        query,
        key,
        value,
        lse,
        context_rows,
        out_all,
        up,
        down,
        qkv_all,
        normed,
        inner,
        active,
        normals,
        vectors,
        unit,
        output_low,
        scales,
    ) = forward(
        keep, queries, passages, w_qkv, qv_bias, w_out, up_piece, w_down, qkv_piece, bias_in,
        norm_gain, norm_shift, layer_bias, w_colbert,
    )
    half_t, half_d = ranks // 2, groups // 2
    spot = jnp.arange(share)
    group_q = (group // 2) * 2 + jnp.arange(2)
    rank_q = jnp.arange(half_t) * 2 + rank % 2
    place_q = jnp.broadcast_to(rank_q[None, :, None] * share + spot[None, None, :], (2, half_t, share))
    valid_q = ((place_q >= 1) & (place_q < query_lengths[group_q][:, None, None])).reshape(-1)
    lead_q = (place_q == 0).reshape(-1)
    group_p = jnp.arange(half_d) * 2 + group % 2
    rank_p = (rank // 2) * 2 + jnp.arange(2)
    place_p = jnp.broadcast_to(rank_p[:, None, None] * share + spot[None, None, :], (2, half_d, share))
    valid_p = ((place_p >= 1) & (place_p < passage_lengths[group_p][None, :, None])).reshape(-1, 1)
    lead_p = (place_p == 0).reshape(-1, 1)
    scale = float(width) ** 0.5

    def along(table):
        wide = jnp.broadcast_to(table[group_q][:, group_p].T[:, :, None], (half_d, 2, half_t * share))
        return wide.reshape(half_d, -1)

    late = jnp.where(valid_q[None], scale * along(colbert_cot), 0.0)
    dense = jnp.where(lead_q[None], 50.0 * along(dense_cot), 0.0)
    grad_vec = score(vectors, valid_p.astype(F32), lead_p.astype(F32), late, dense)

    tokens, grad_down, grad_up, grad_w_out, colbert, grad_qkv, small = backward(
        keep.T, grad_vec, unit, output_low, scales, normals, w_colbert, down, up, inner, active,
        normed.reshape(-1, width), out_all.reshape(-1, width), context_rows, query, key, value, lse,
        queries, passages, qkv_all.reshape(-1, width), norm_gain,
    )
    units = piece * ranks
    grad_in_bias = small[:, 7, :units].reshape(groups, ranks, piece)
    grad_in_bias = lax.dynamic_index_in_dim(grad_in_bias, rank, 1, keepdims=False).reshape(-1)
    small = jnp.sum(small, axis=0)
    grad_qkv = grad_qkv.astype(F32)
    grad_w_qkv = grad_qkv[:width].reshape(width, 3, columns).transpose(1, 0, 2)
    line = grad_qkv[width].reshape(3, columns)
    return (
        output_low[:share],
        output_low[share:],
        tokens[:share],
        tokens[share:],
        grad_w_qkv,
        jnp.stack([line[0], line[2]]),
        grad_w_out.astype(F32),
        grad_up.astype(F32).T,
        grad_in_bias,
        grad_down.astype(F32),
        small[0:2],
        small[2:4],
        small[4:7],
        colbert.astype(F32),
    )


def solution(mesh):
    both = P(("dp", "tensor"), None)
    return jax.shard_map(
        per_device,
        mesh=mesh,
        in_specs=(
            P("dp", None),
            P("dp", None),
            P(),
            P(),
            P(None, None, "tensor"),
            P(None, "tensor"),
            P("tensor", None),
            P(None, "tensor"),
            P("tensor"),
            P("tensor", None),
            P(),
            P(),
            P(),
            P(),
            P(),
            P(),
        ),
        out_specs=(
            both,
            both,
            both,
            both,
            P(None, None, "tensor"),
            P(None, "tensor"),
            P("tensor", None),
            P(None, "tensor"),
            P("tensor"),
            P("tensor", None),
            P(),
            P(),
            P(),
            P(),
        ),
        check_vma=False,
    )
```

```python
import functools

import jax
import jax.numpy as jnp
from jax import lax
from jax.experimental import pallas as pl
from jax.experimental.pallas import tpu as pltpu
from jax.sharding import PartitionSpec as P

HEAD_DIM = 64
BF = jnp.bfloat16
F32 = jnp.float32
BLOCK = 256


def dot(left, right):
    return jnp.dot(left, right, preferred_element_type=F32)


def inner_rows(left, right):
    return lax.dot_general(left, right, (((1,), (1,)), ((), ())), preferred_element_type=F32)


def outer_rows(left, right):
    return lax.dot_general(left, right, (((0,), (0,)), ((), ())), preferred_element_type=F32)


def steps_of(size):
    steps = []
    while size > 1:
        size //= 2
        steps.append(size)
    return steps


def offsets(steps):
    found = [0]
    for step in steps:
        found = found + [item ^ step for item in found]
    return found


def swap(value, axis, step):
    size = lax.axis_size(axis)
    return lax.ppermute(value, axis, [(index, index ^ step) for index in range(size)])


def spread(value, axis, steps):
    held = value[None]
    for step in steps:
        held = jnp.concatenate([held, swap(held, axis, step)], axis=0)
    return held


def fold(parts, axis, steps):
    for step in reversed(steps):
        half = parts.shape[0] // 2
        came = swap(parts[half:].astype(BF), axis, step)
        parts = parts[:half].astype(F32) + came.astype(F32)
    return parts[0]


def natural(parts, axis, steps, dim=0):
    order = offsets(steps)
    size = len(order)
    place = [0] * size
    for spot, item in enumerate(order):
        place[item] = spot
    table = jnp.array(place, jnp.int32)
    rank = lax.axis_index(axis)
    return jnp.concatenate(
        [lax.dynamic_slice_in_dim(parts, table[item ^ rank], 1, dim) for item in range(size)], axis=dim
    )


def xored(parts, axis, steps, dim=0):
    rank = lax.axis_index(axis)
    return jnp.concatenate(
        [lax.dynamic_slice_in_dim(parts, item ^ rank, 1, dim) for item in offsets(steps)], axis=dim
    )


def trade(parts, steps, dim):
    rank = lax.axis_index("tensor")
    got = []
    for item in offsets(steps):
        piece = lax.dynamic_index_in_dim(parts, item ^ rank, dim, keepdims=False)
        got.append(swap(piece, "tensor", item) if item else piece)
    return got


def layer_norm(hidden, gain, shift):
    centre = hidden - jnp.mean(hidden, axis=-1, keepdims=True)
    inverse = lax.rsqrt(jnp.mean(centre * centre, axis=-1, keepdims=True) + 1e-05)
    normal = centre * inverse
    return (normal * gain + shift, normal, inverse)


def norm_back(grad, normal, inverse, gain):
    scaled = grad * gain
    middle = (
        scaled
        - jnp.mean(scaled, axis=-1, keepdims=True)
        - normal * jnp.mean(scaled * normal, axis=-1, keepdims=True)
    )
    return (middle * inverse, jnp.sum(grad * normal, axis=0), jnp.sum(grad, axis=0))


def gelu_slope(inner):
    return (
        0.5 * (1.0 + lax.erf(inner * 0.7071067811865476))
        + inner * jnp.exp(-0.5 * inner * inner) * 0.3989422804014327
    )


def head_mask(columns, head):
    lane = lax.broadcasted_iota(jnp.int32, (1, columns), 1)
    return (lane >= head * HEAD_DIM) & (lane < (head + 1) * HEAD_DIM)


MESH = pl.DeviceIdType.MESH


class Lattice:
    def __init__(self, steps):
        self.steps = steps
        self.count = 1 << len(steps)

    def peer(self, level):
        axis, step = self.steps[level]
        return {axis: lax.axis_index(axis) ^ step}

    def index(self, mask):
        found = 0
        for level, (axis, step) in enumerate(self.steps):
            bit = (lax.axis_index(axis) // step) % 2
            found = found + (1 - bit if mask >> level & 1 else bit) * (1 << level)
        return found

    def member(self, axis, block):
        found = lax.axis_index(axis)
        for level, (name, step) in enumerate(self.steps):
            if name == axis:
                found = found + ((block // (1 << level)) % 2 - (lax.axis_index(axis) // step) % 2) * step
        return found

    def shift(self, mask):
        found = {"dp": 0, "tensor": 0}
        for level, (axis, step) in enumerate(self.steps):
            if mask >> level & 1:
                found[axis] ^= step
        return found["dp"], found["tensor"]


def remote(src, dst, send, recv, peer):
    return pltpu.make_async_remote_copy(
        src_ref=src, dst_ref=dst, send_sem=send, recv_sem=recv, device_id=peer, device_id_type=MESH
    )


class Gather:
    def __init__(self, lattice, view, send, recv, base=0, own=None):
        self.lattice, self.view, self.send, self.recv, self.base = lattice, view, send, recv, base
        self.own = own
        self.sent = []

    def copy(self, level, mask):
        slot = self.base + (1 << level) + mask
        place = self.view(mask)
        src = self.own if mask == 0 and self.own is not None else place
        return remote(src, place, self.send.at[slot], self.recv.at[slot], self.lattice.peer(level))

    def start(self, levels=None):
        for level in range(len(self.lattice.steps)) if levels is None else levels:
            copy = self.copy(level, 0)
            copy.start()
            self.sent.append(copy)

    def arrive(self, mask):
        level = mask.bit_length() - 1
        slot = self.base + mask
        place = self.view(mask)
        remote(place, place, self.send.at[slot], self.recv.at[slot], self.lattice.peer(level)).wait_recv()
        for later in range(level + 1, len(self.lattice.steps)):
            copy = self.copy(later, mask)
            copy.start()
            self.sent.append(copy)

    def finish(self):
        for copy in self.sent:
            copy.wait_send()


class Scatter:
    def __init__(self, lattice, read, write, out, came, send, recv, base=0):
        self.lattice, self.read, self.write = lattice, read, write
        self.out, self.came, self.send, self.recv, self.base = out, came, send, recv, base
        self.sent = []

    def push(self, mask):
        level = mask.bit_length() - 1
        slot = self.base + mask
        copy = remote(
            self.out.at[mask - 1],
            self.came.at[mask - 1],
            self.send.at[slot],
            self.recv.at[slot],
            self.lattice.peer(level),
        )
        copy.start()
        self.sent.append(copy)

    def put(self, mask):
        self.out[mask - 1] = self.read(mask).astype(BF)
        self.push(mask)

    def level(self, level):
        for mask in reversed(range(1 << level)):
            slot = (1 << level) + mask
            place = self.came.at[slot - 1]
            remote(
                self.out.at[slot - 1],
                place,
                self.send.at[self.base + slot],
                self.recv.at[self.base + slot],
                self.lattice.peer(level),
            ).wait_recv()
            total = self.read(mask) + self.came[slot - 1].astype(F32)
            if mask and mask >= 1 << (level - 1):
                self.out[mask - 1] = total.astype(BF)
                self.push(mask)
            else:
                self.write(mask, total)

    def run(self):
        for level in reversed(range(len(self.lattice.steps))):
            self.level(level)

    def finish(self):
        for copy in self.sent:
            copy.wait_send()


def score_steps(all_t, all_d):
    if len(all_d) <= 2:
        rows_q = [("tensor", step) for step in all_t[1:-1]] + [("dp", step) for step in all_d]
        rows_p = [("tensor", step) for step in all_t[:1] + all_t[-1:]]
    else:
        rows_q = [("tensor", step) for step in all_t[:-1]] + [("dp", step) for step in all_d[-1:]]
        rows_p = [("dp", step) for step in all_d[:-1]] + [("tensor", step) for step in all_t[-1:]]
    return rows_q, rows_p


def score_peers(all_t, rows_p):
    return [item for item in offsets([step for step in all_t if ("tensor", step) not in rows_p]) if item]


def greet(peers):
    barrier = pltpu.get_barrier_semaphore()
    for peer in peers:
        pl.semaphore_signal(barrier, inc=1, device_id=peer, device_id_type=MESH)
    pl.semaphore_wait(barrier, len(peers))


def forward_kernel(
    all_t, all_d, ship_bias,
    len_q, len_p, dense_cot, late_cot,
    x_q, x_p, w_qkv, qv_bias, w_out, up_piece, w_down, qkv_piece, bias_in, gain, shift, offset, w_colbert,
    o_q, o_k, o_v, o_lse, o_ctx, o_out, o_up, o_down, o_qkv, o_normed, o_slope, o_active,
    o_normal, o_unit, o_low, o_spread, o_grad,
    x, q, k, v, ctx, lse, ctx_rows, out_all, up, down, normed, slope, active, sums, s_out, s_in,
    first, normal, unit, vec, low, scales, wc, bias_all, bias_row,
    rows_q, rows_p, raised, pull, mass, mass_in, out_q, in_q, sum_p, out_p, in_p, grad,
    local, g_send, g_recv, a_send, a_recv, b_send, b_recv, n_send, n_recv, r_send, r_recv,
    gq_send, gq_recv, gp_send, gp_recv, m_send, m_recv, rq_send, rq_recv, rp_send, rp_recv,
):
    group, rank = lax.axis_index("dp"), lax.axis_index("tensor")
    ranks, groups = 1 << len(all_t), 1 << len(all_d)
    span, width = x_q.shape
    columns = w_qkv.shape[2]
    share = span // ranks
    piece = up_piece.shape[0]
    units = up.shape[0]
    quarter = columns // 4
    rows = groups * share
    heads = columns // HEAD_DIM
    scale = HEAD_DIM**-0.5

    x_copies = [pltpu.make_async_copy(src, x.at[s], local.at[s]) for s, src in enumerate((x_q, x_p))]
    for copy in x_copies:
        copy.start()
    wc_copy = pltpu.make_async_copy(w_colbert, wc, local.at[2])
    wc_copy.start()
    greet([{"tensor": rank ^ item} for item in range(1, ranks)] + [{"dp": group ^ item} for item in all_d])

    tensor = Lattice([("tensor", step) for step in all_t])
    quad = Lattice([("tensor", step) for step in all_t] + [("dp", step) for step in all_d[-2:]])
    data = Lattice([("dp", step) for step in all_d])

    def quarters(ref, size):
        def view(mask):
            d, t = quad.shift(mask)
            return ref.at[rank ^ t, pl.ds(pl.multiple_of(((group ^ d) % 4) * size, size), size)]

        return view

    def unit_rows(ref):
        return lambda mask: ref.at[pl.ds(pl.multiple_of((rank ^ tensor.shift(mask)[1]) * piece, piece), piece)]

    wide, tall = quad.count, tensor.count
    far, near = list(range(len(all_t) - 1)), [len(all_t) - 1]
    at_quarter = pl.ds(pl.multiple_of((group % 4) * quarter, quarter), quarter)
    at_piece = pl.ds(pl.multiple_of(group * piece, piece), piece)
    take_out = Gather(quad, quarters(out_all, quarter), g_send, g_recv, 0, own=w_out.at[at_quarter])
    take_up = Gather(tensor, unit_rows(up), g_send, g_recv, wide, own=up_piece)
    take_down = Gather(tensor, unit_rows(down), g_send, g_recv, wide + tall, own=w_down.at[at_piece])
    cores = Lattice([("tensor", step) for step in all_t] + [("dp", all_d[-1])])
    slab = qkv_piece.shape[0]

    def slab_view(mask):
        d, t = cores.shift(mask)
        return o_qkv.at[rank ^ t, pl.ds(pl.multiple_of(((group ^ d) % 2) * slab, slab), slab)]

    take_qkv = Gather(cores, slab_view, g_send, g_recv, wide + 2 * tall, own=qkv_piece)
    own_copies = [
        pltpu.make_async_copy(w_out.at[at_quarter], take_out.view(0), local.at[3]),
        pltpu.make_async_copy(up_piece, take_up.view(0), local.at[4]),
        pltpu.make_async_copy(w_down.at[at_piece], take_down.view(0), local.at[5]),
        pltpu.make_async_copy(qkv_piece, take_qkv.view(0), local.at[6]),
    ]
    early = [tall // 4] + list(range(1, tall // 4))
    late = list(range(tall // 4 + 1, tall // 2))
    take_out.start()
    take_up.start(near)
    for copy in own_copies:
        copy.start()
    pending = []
    bias_copies = []
    if ship_bias:
        bias_all[rank] = bias_in[...]
        for item in range(1, ranks):
            copy = remote(
                bias_in, bias_all.at[rank], b_send.at[item], b_recv.at[item], {"tensor": rank ^ item}
            )
            copy.start()
            bias_copies.append(copy)

    lengths = (len_q[group], len_p[group])
    def project(s):
        x_copies[s].wait()
        tokens = x[s]
        q[s] = (dot(tokens, w_qkv[0]) + qv_bias[0:1, :].astype(F32)).astype(BF)
        k[s] = dot(tokens, w_qkv[1]).astype(BF)
        v[s] = (dot(tokens, w_qkv[2]) + qv_bias[1:2, :].astype(F32)).astype(BF)

    block = min(BLOCK, span)

    def attention(s, begin, end):
        keep = lax.broadcasted_iota(jnp.int32, (1, span), 1) < lengths[s]

        @pl.loop(begin, end)
        def _(index):
            at = pl.ds(pl.multiple_of(index * block, block), block)
            query = q[s, at, :]
            total = jnp.zeros((block, columns), F32)
            for head in range(heads):
                mask = head_mask(columns, head)
                mine = jnp.where(mask, query, jnp.zeros_like(query)) * jnp.asarray(scale, BF)
                scores = jnp.where(keep, inner_rows(mine, k[s]), -1e30)
                top = jnp.max(scores, axis=-1, keepdims=True)
                weight = jnp.exp(scores - top)
                amount = jnp.sum(weight, axis=-1, keepdims=True)
                part = dot(weight.astype(BF), v[s]) / amount
                total = jnp.where(mask, part, total)
                column = jnp.broadcast_to(top + jnp.log(amount), (block, 128))
                lse[s, head : head + 1, at] = column.T[0:1, :]
            ctx[s, at, :] = total.astype(BF)

    sends = []

    def trade_context(s):
        at = pl.ds(s * share, share)
        for item in range(1, ranks):
            peer = rank ^ item
            copy = remote(
                ctx.at[s, pl.ds(pl.multiple_of(peer * share, share), share)],
                ctx_rows.at[rank, at],
                a_send.at[s * ranks + item],
                a_recv.at[s * ranks + item],
                {"tensor": peer},
            )
            copy.start()
            sends.append(copy)
        ctx_rows[rank, s * share : (s + 1) * share, :] = ctx[s, pl.ds(pl.multiple_of(rank * share, share), share), :]

    def context_here(s):
        at = pl.ds(s * share, share)
        for item in range(1, ranks):
            place = ctx_rows.at[rank ^ item, at]
            remote(
                place, place, a_send.at[s * ranks + item], a_recv.at[s * ranks + item], {"tensor": rank ^ item}
            ).wait_recv()

    def out_going(src, dst, index):
        copy = pltpu.make_async_copy(src, dst, local.at[index])
        copy.start()
        pending.append(copy)

    def arrive(taking, masks):
        for mask in masks:
            taking.arrive(mask)

    count = span // block
    arrive(take_out, early)
    take_up.start(far)
    take_down.start(near)
    project(0)
    attention(0, 0, count // 2)
    arrive(take_up, early[:1])
    attention(0, count // 2, count)
    trade_context(0)
    for copy in own_copies:
        copy.wait()
    project(1)
    attention(1, 0, count // 2)
    arrive(take_out, late)
    attention(1, count // 2, count)
    trade_context(1)
    arrive(take_up, early[1:])
    arrive(take_out, range(tall // 2, wide))
    take_down.start(far)
    arrive(take_up, late)
    out_going(q, o_q, 7)
    out_going(k, o_k, 8)
    out_going(v, o_v, 9)
    out_going(lse, o_lse, 10)

    def to_rows(s):
        at = slice(s * share, (s + 1) * share)
        context_here(s)
        if columns % 128 == 0:
            mix = jnp.concatenate([ctx_rows[r, at, :] for r in range(ranks)], axis=1)
            mixed = dot(mix, out_all[...].reshape(ranks * columns, width))
        else:
            mixed = dot(ctx_rows[0, at, :], out_all[0])
            for r in range(1, ranks):
                mixed = mixed + dot(ctx_rows[r, at, :], out_all[r])
        mine = x[s, pl.ds(pl.multiple_of(rank * share, share), share), :].astype(F32)
        value, plain, inverse = layer_norm(mine + mixed + offset[0:1, :], gain[0:1, :], shift[0:1, :])
        first[at, :] = value
        normal[0, at, :] = plain
        scales[0, at, :] = jnp.broadcast_to(inverse, (share, 128))
        normed[s, pl.ds(pl.multiple_of(group * share, share), share), :] = value.astype(BF)

        def view(mask):
            d, _ = data.shift(mask)
            return normed.at[s, pl.ds(pl.multiple_of((group ^ d) * share, share), share)]

        taking = Gather(data, view, n_send, n_recv, s * groups)
        taking.start()
        return taking

    normed_takes = [to_rows(0)]
    normed_takes.append(to_rows(1))
    arrive(take_down, early)
    arrive(take_down, late)
    take_qkv.start()
    if ship_bias:
        for item in range(1, ranks):
            place = bias_all.at[rank ^ item]
            remote(place, place, b_send.at[item], b_recv.at[item], {"tensor": rank ^ item}).wait_recv()
        for r in range(ranks):
            bias_row[0:1, r * piece : (r + 1) * piece] = bias_all[r, 0:1, :].astype(F32)
    else:
        bias_row[0:1, :] = bias_in[0:1, :]
    arrive(take_up, range(tall // 2, tall))
    arrive(normed_takes[0], range(1, groups))

    def spot(mask):
        return pl.multiple_of((group ^ data.shift(mask)[0]) * share, share)

    gives = []
    for s in range(2):

        def read(mask, s=s):
            return sums[pl.ds(s * rows + spot(mask), share), :]

        def write(mask, value, s=s):
            sums[pl.ds(s * rows + spot(mask), share), :] = value

        gives.append(Scatter(data, read, write, s_out.at[s], s_in.at[s], r_send, r_recv, s * groups))

    tile = min(256, units)

    def expand(s):
        at_rows = slice(s * rows, (s + 1) * rows)

        @pl.loop(0, units // tile)
        def _(index):
            at = pl.ds(pl.multiple_of(index * tile, tile), tile)
            value = inner_rows(normed[s], up[at, :]) + bias_row[0:1, at]
            phi = 0.5 * (1.0 + lax.erf(value * 0.7071067811865476))
            active[at_rows, at] = (value * phi).astype(BF)
            slope[at_rows, at] = (phi + value * jnp.exp(-0.5 * value * value) * 0.3989422804014327).astype(BF)

    def reduce(s):
        at_rows = slice(s * rows, (s + 1) * rows)

        @pl.loop(0, width // 256)
        def _(index):
            at = pl.ds(pl.multiple_of(index * 256, 256), 256)
            sums[at_rows, at] = dot(active[at_rows, :], down[:, at])

        for mask in reversed(range(groups // 2, groups)):
            gives[s].put(mask)

    top = len(all_d) - 1
    expand(0)
    arrive(normed_takes[1], range(1, groups))
    expand(1)
    arrive(take_down, range(tall // 2, tall))
    reduce(0)
    arrive(take_qkv, early)
    reduce(1)
    gives[0].level(top)
    out_going(ctx_rows, o_ctx, 11)
    out_going(out_all, o_out, 12)
    out_going(up, o_up, 13)
    out_going(down, o_down, 14)
    out_going(normed, o_normed, 15)
    out_going(slope, o_slope, 16)
    out_going(active, o_active, 17)
    gives[1].level(top)
    wc_copy.wait()

    steps_q, steps_p = score_steps(all_t, all_d)
    lattice_q, lattice_p = Lattice(steps_q), Lattice(steps_p)
    levels_y = [level for level, (axis, _) in enumerate(steps_p) if axis == "dp"]
    count_y = 1 << len(levels_y)

    def spot_q(mask):
        return pl.multiple_of(lattice_q.index(mask) * share, share)

    def spot_p(mask):
        return pl.multiple_of(lattice_p.index(mask) * share, share)

    takes = (
        Gather(lattice_q, lambda m: rows_q.at[pl.ds(spot_q(m), share)], gq_send, gq_recv, own=vec.at[pl.ds(0, share)]),
        Gather(
            lattice_p, lambda m: rows_p.at[pl.ds(spot_p(m), share)], gp_send, gp_recv, own=vec.at[pl.ds(share, share)]
        ),
    )
    for s in range(2):
        at = slice(s * share, (s + 1) * share)
        for level in reversed(range(top)):
            gives[s].level(level)
        feed = gives[s].read(0)
        value, plain, inverse = layer_norm(first[at, :] + feed + offset[1:2, :], gain[1:2, :], shift[1:2, :])
        short = value.astype(BF)
        place = lax.broadcasted_iota(jnp.int32, (share, 1), 0) + rank * share
        chosen = jnp.where(place == 0, value, dot(short, wc[...]) + offset[2:3, :])
        norm = lax.rsqrt(jnp.sum(chosen * chosen, axis=-1, keepdims=True) + 1e-06)
        chosen = chosen * norm
        vec[at, :] = chosen.astype(BF)
        takes[s].start()
        unit[at, :] = chosen
        normal[1, at, :] = plain
        scales[1, at, :] = jnp.broadcast_to(inverse, (share, 128))
        scales[2, at, :] = jnp.broadcast_to(norm, (share, 128))
        low[at, :] = short
    rows_q[pl.ds(spot_q(0), share), :] = vec[0:share, :]
    rows_p[pl.ds(spot_p(0), share), :] = vec[share : 2 * share, :]
    take_q, take_p = takes
    many_q, many_p = lattice_q.count * share, lattice_p.count * share
    half_q, half_p = many_q // 2, many_p // 2
    arrive(take_q, range(1, lattice_q.count // 4))
    arrive(take_p, range(1, lattice_p.count // 2))
    arrive(take_q, [lattice_q.count // 4])
    arrive(take_q, range(lattice_q.count // 4 + 1, lattice_q.count // 2))
    out_going(normal, o_normal, 18)
    out_going(unit, o_unit, 19)
    out_going(low, o_low, 20)
    out_going(scales, o_spread, 21)

    lane = lax.broadcasted_iota(jnp.int32, (1, many_q), 1)
    block_q = lane // share
    group_q = lattice_q.member("dp", block_q)
    place_q = lattice_q.member("tensor", block_q) * share + lane % share
    temper = float(width) ** 0.5
    which_y = [sum(((y >> i) & 1) << level for i, level in enumerate(levels_y)) for y in range(count_y)]
    late_rows, dense_rows = [], []
    for y in range(count_y):
        which = lattice_p.member("dp", which_y[y])
        length, late_row, dense_row = 0, 0.0, 0.0
        for g in range(groups):
            length = jnp.where(group_q == g, len_q[g], length)
            late_row = jnp.where(group_q == g, temper * late_cot[g, which], late_row)
            dense_row = jnp.where(group_q == g, 50.0 * dense_cot[g, which], dense_row)
        late_rows.append(jnp.where((place_q >= 1) & (place_q < length), late_row, 0.0))
        dense_rows.append(jnp.where(place_q == 0, dense_row, 0.0))
    arrive(take_q, range(lattice_q.count // 2, lattice_q.count))
    arrive(take_p, range(lattice_p.count // 2, lattice_p.count))
    arrive(take_qkv, late)

    def place_p(block):
        first_place = lattice_p.member("tensor", block) * share
        return first_place + lax.broadcasted_iota(jnp.int32, (share, 1), 0)

    def part_of(block):
        return sum(((block >> level) & 1) << i for i, level in enumerate(levels_y))

    mass[...] = jnp.zeros_like(mass)
    for block in range(lattice_p.count):
        at = slice(block * share, (block + 1) * share)
        y = part_of(block)
        dots = inner_rows(rows_p[at, :], rows_q[...])
        place = place_p(block)
        counted = (place >= 1) & (place < len_p[lattice_p.member("dp", block)])
        value = jnp.where(counted, jnp.exp(dots * temper - temper), 0.0)
        raised[at, :] = value
        mass[y : y + 1, :] += jnp.sum(value, axis=0, keepdims=True)
    mass_copies = []
    for index, item in enumerate(score_peers(all_t, steps_p)):
        copy = remote(mass, mass_in.at[index], m_send.at[index], m_recv.at[index], {"tensor": rank ^ item})
        copy.start()
        mass_copies.append(copy)
    total = mass[...]
    for index, copy in enumerate(mass_copies):
        copy.wait_recv()
        total = total + mass_in[index]
    for block in range(lattice_p.count):
        at = slice(block * share, (block + 1) * share)
        y = part_of(block)
        value = raised[at, :] * (late_rows[y] / total[y : y + 1, :])
        pull[at, :] = (value + jnp.where(place_p(block) == 0, dense_rows[y], 0.0)).astype(BF)

    mine_q = (lax.axis_index(steps_q[-1][0]) // steps_q[-1][1]) % 2
    mine_p = (lax.axis_index(steps_p[-1][0]) // steps_p[-1][1]) % 2

    def fill_q(half):
        at = pl.ds(pl.multiple_of(half * half_q, half_q), half_q)
        sums[at, :] = outer_rows(pull[:, at], rows_p[...])

    def fill_p(half):
        at = pl.ds(pl.multiple_of(half * half_p, half_p), half_p)
        sum_p[at, :] = dot(pull[at, :], rows_q[...])

    def reader(ref, find):
        return lambda m: ref[pl.ds(find(m), share), :]

    def writer(ref, find):
        def write(m, value):
            ref[pl.ds(find(m), share), :] = value

        return write

    give_q = Scatter(lattice_q, reader(sums, spot_q), writer(sums, spot_q), out_q, in_q, rq_send, rq_recv)
    give_p = Scatter(lattice_p, reader(sum_p, spot_p), writer(sum_p, spot_p), out_p, in_p, rp_send, rp_recv)
    fill_q(1 - mine_q)
    for mask in reversed(range(lattice_q.count // 2, lattice_q.count)):
        give_q.put(mask)
    fill_p(1 - mine_p)
    for mask in reversed(range(lattice_p.count // 2, lattice_p.count)):
        give_p.put(mask)
    fill_q(mine_q)
    arrive(take_qkv, range(tall // 2, tall))
    give_q.level(len(steps_q) - 1)
    fill_p(mine_p)
    give_p.level(len(steps_p) - 1)
    for level in reversed(range(len(steps_q) - 1)):
        give_q.level(level)
    for level in reversed(range(len(steps_p) - 1)):
        give_p.level(level)
    grad[0:share, :] = sums[pl.ds(spot_q(0), share), :]
    grad[share : 2 * share, :] = sum_p[pl.ds(spot_p(0), share), :]
    out_going(grad, o_grad, 22)
    arrive(take_qkv, range(tall, 2 * tall))
    for move in [take_out, take_up, take_down, take_qkv, take_q, take_p, give_q, give_p] + normed_takes + gives:
        move.finish()
    for copy in sends + bias_copies + mass_copies:
        copy.wait_send()
    for copy in pending:
        copy.wait()


def forward(len_q, len_p, dense_cot, late_cot, queries, passages, w_qkv, qv_bias, w_out, up_piece, w_down, qkv_piece,
            bias_in, gain, shift, offset, w_colbert):
    groups, ranks = lax.axis_size("dp"), lax.axis_size("tensor")
    all_t, all_d = steps_of(ranks), steps_of(groups)
    span, width = queries.shape
    columns = w_qkv.shape[2]
    heads = columns // HEAD_DIM
    share = span // ranks
    piece = up_piece.shape[0]
    units = piece * ranks
    rows = groups * share
    ship_bias = bias_in.shape[0] == 16
    steps_q, steps_p = score_steps(all_t, all_d)
    blocks_q, blocks_p = 1 << len(steps_q), 1 << len(steps_p)
    many_q, many_p, peers = blocks_q * share, blocks_p * share, len(score_peers(all_t, steps_p))

    shapes = [
        ((2, span, columns), BF),
        ((2, span, columns), BF),
        ((2, span, columns), BF),
        ((2, heads, span), F32),
        ((ranks, 2 * share, columns), BF),
        ((ranks, columns, width), BF),
        ((units, width), BF),
        ((units, width), BF),
        ((ranks, 3 * columns, width), BF),
        ((2, rows, width), BF),
        ((2 * rows, units), BF),
        ((2 * rows, units), BF),
        ((2, 2 * share, width), F32),
        ((2 * share, width), F32),
        ((2 * share, width), BF),
        ((3, 2 * share, 128), F32),
        ((2 * share, width), F32),
    ]
    dma = pltpu.SemaphoreType.DMA
    vmem = pltpu.VMEM
    hold, leave = pl.BlockSpec(memory_space=pltpu.VMEM), pl.BlockSpec(memory_space=pl.ANY)
    flat = pl.BlockSpec(memory_space=pltpu.SMEM)

    def pair(count):
        return [dma((count,)), dma((count,))]

    return pl.pallas_call(
        functools.partial(forward_kernel, all_t, all_d, ship_bias),
        out_shape=[jax.ShapeDtypeStruct(*item) for item in shapes],
        in_specs=[flat] * 4
        + [leave, leave, hold, hold, leave, leave, leave, hold, hold, hold, hold, hold, leave],
        out_specs=[leave] * len(shapes),
        scratch_shapes=[
            vmem((2, span, width), BF),
            vmem((2, span, columns), BF),
            vmem((2, span, columns), BF),
            vmem((2, span, columns), BF),
            vmem((2, span, columns), BF),
            vmem((2, heads, span), F32),
            vmem((ranks, 2 * share, columns), BF),
            vmem((ranks, columns, width), BF),
            vmem((units, width), BF),
            vmem((units, width), BF),
            vmem((2, rows, width), BF),
            vmem((2 * rows, units), BF),
            vmem((2 * rows, units), BF),
            vmem((2 * rows, width), F32),
            vmem((2, groups - 1, share, width), BF),
            vmem((2, groups - 1, share, width), BF),
            vmem((2 * share, width), F32),
            vmem((2, 2 * share, width), F32),
            vmem((2 * share, width), F32),
            vmem((2 * share, width), BF),
            vmem((2 * share, width), BF),
            vmem((3, 2 * share, 128), F32),
            vmem((width, width), BF),
            vmem((ranks, 16, piece), BF),
            vmem((8, units), F32),
            vmem((many_q, width), BF),
            vmem((many_p, width), BF),
            vmem((many_p, many_q), F32),
            vmem((many_p, many_q), BF),
            vmem((8, many_q), F32),
            vmem((peers, 8, many_q), F32),
            vmem((blocks_q - 1, share, width), BF),
            vmem((blocks_q - 1, share, width), BF),
            vmem((many_p, width), F32),
            vmem((blocks_p - 1, share, width), BF),
            vmem((blocks_p - 1, share, width), BF),
            vmem((2 * share, width), F32),
            dma((23,)),
        ]
        + pair(8 * ranks)
        + pair(2 * ranks)
        + pair(ranks)
        + pair(2 * groups)
        + pair(2 * groups)
        + pair(blocks_q)
        + pair(blocks_p)
        + pair(peers)
        + pair(blocks_q)
        + pair(blocks_p),
        compiler_params=pltpu.CompilerParams(
            collective_id=2, has_side_effects=True, vmem_limit_bytes=62 * 2**20
        ),
        cost_estimate=pl.CostEstimate(flops=10**11, bytes_accessed=40 * 2**20, transcendentals=2**23),
        name="forward",
    )(len_q, len_p, dense_cot, late_cot, queries, passages, w_qkv, qv_bias, w_out, up_piece, w_down, qkv_piece,
      bias_in, gain, shift, offset, w_colbert)


class Settle:
    def __init__(self, lattice, view, came, send, recv, base=0):
        self.lattice, self.view, self.came = lattice, view, came
        self.send, self.recv, self.base = send, recv, base
        self.sent = []

    def copy(self, mask):
        return remote(
            self.view(mask),
            self.came.at[mask - 1],
            self.send.at[self.base + mask],
            self.recv.at[self.base + mask],
            self.lattice.peer(mask.bit_length() - 1),
        )

    def push(self, mask):
        copy = self.copy(mask)
        copy.start()
        self.sent.append(copy)

    def start(self):
        for mask in reversed(range(self.lattice.count // 2, self.lattice.count)):
            self.push(mask)

    def level(self, level):
        for mask in reversed(range(1 << level)):
            slot = (1 << level) + mask
            self.copy(slot).wait_recv()
            place = self.view(mask)
            place[...] = (place[...].astype(F32) + self.came[slot - 1].astype(F32)).astype(BF)
            if mask and mask >= 1 << (level - 1):
                self.push(mask)

    def finish(self):
        for copy in self.sent:
            copy.wait_send()


def backward_kernel(
    all_t, all_d,
    len_q, len_p, grad_vec, h_unit, h_low, h_scales, h_normals, h_wc, h_down, h_up, h_slope, h_active, h_normed,
    h_out, h_ctx, h_q, h_k, h_v, h_lse, x_q, x_p, h_qkv, gain,
    o_tokens, o_down, o_up, o_out, o_wc, o_qkv, o_small,
    pool, slope, active, out_all, wc, ctx_rows, q, k, v, lse, g1, unit, low, proj, normals, scales, sums,
    s_out, s_in, turn, ctx_out, heads_grad, turned, turned_rows, dk_sum, dv_sum,
    g_down, g_down_in, g_up, g_up_in, g_out_in, g_wc_in, qkv_sum, qkv_low, qkv_in,
    small, small_in, stage, stage_in,
    local, n_send, n_recv, r_send, r_recv, d_send, d_recv, u_send, u_recv, w_send, w_recv, c_send, c_recv,
    a_send, a_recv, t_send, t_recv, f_send, f_recv, m_send, m_recv, y_send, y_recv, q_send, q_recv,
):
    group, rank = lax.axis_index("dp"), lax.axis_index("tensor")
    ranks, groups = 1 << len(all_t), 1 << len(all_d)
    far_d = all_d[:-1]
    span, width = x_q.shape
    columns = q.shape[2]
    share = span // ranks
    units = h_up.shape[0]
    piece = units // ranks
    quarter = columns // 4
    rows = groups * share
    heads = columns // HEAD_DIM
    scale = HEAD_DIM**-0.5
    flat = width // ranks // 4
    at_up, at_down = pl.ds(0, units), pl.ds(units, units)
    at_normed, at_feed = pl.ds(2 * units, 2 * rows), pl.ds(2 * units + 2 * rows, 2 * rows)
    feed_at = 2 * units + 2 * rows

    loads = []

    def load(src, dst):
        copy = pltpu.make_async_copy(src, dst, local.at[len(loads)])
        copy.start()
        loads.append(copy)
        return copy

    early = [load(grad_vec, g1), load(h_unit, unit), load(h_scales, scales), load(h_low, low), load(h_wc, wc)]
    early.append(load(h_normals, normals))
    ffn = [load(h_down, pool.at[at_down]), load(h_slope, slope), load(h_up, pool.at[at_up])]
    later = [load(h_active, active), load(h_normed, pool.at[at_normed])]
    last = [load(h_out, out_all), load(h_ctx, ctx_rows)]
    heads_in = [load(h_q, q), load(h_k, k), load(h_v, v), load(h_lse, lse)]
    greet([{"tensor": rank ^ item} for item in range(1, ranks)] + [{"dp": group ^ item} for item in all_d])

    tensor = Lattice([("tensor", step) for step in all_t])
    quad = Lattice([("tensor", step) for step in all_t] + [("dp", step) for step in all_d[-2:]])
    data = Lattice([("dp", step) for step in all_d])

    def quarters(ref, size, lattice=quad):
        def view(mask):
            d, t = lattice.shift(mask)
            return ref.at[pl.ds(pl.multiple_of(((rank ^ t) * 4 + (group ^ d) % 4) * size, size), size)]

        return view

    cross = Lattice(tensor.steps[:-2] + [tensor.steps[-1], tensor.steps[-2]])

    def pieces(ref, lattice):
        return lambda mask: ref.at[pl.ds(pl.multiple_of((rank ^ lattice.shift(mask)[1]) * piece, piece), piece)]

    def spot(mask):
        return pl.multiple_of((group ^ data.shift(mask)[0]) * share, share)

    flow = Lattice([("dp", all_d[-2])] + tensor.steps + [("dp", all_d[-1])])
    give_wc = Settle(flow, quarters(wc, flat, flow), g_wc_in, c_send, c_recv)
    give_out = Settle(quad, quarters(out_all, quarter), g_out_in, w_send, w_recv)
    give_down = Settle(tensor, pieces(g_down, tensor), g_down_in, d_send, d_recv)
    give_up = Settle(cross, pieces(g_up, cross), g_up_in, u_send, u_recv)

    small[...] = jnp.zeros_like(small)
    for copy in early:
        copy.wait()
    takes = []
    for s in range(2):
        at = slice(s * share, (s + 1) * share)
        grad, plain = g1[at, :], unit[at, :]
        chosen = scales[2, at, 0:1] * (grad - plain * jnp.sum(grad * plain, axis=-1, keepdims=True))
        leading = lax.broadcasted_iota(jnp.int32, (share, 1), 0) + rank * share == 0
        short = jnp.where(leading, 0.0, chosen).astype(BF)
        proj[at, :] = short
        grad = jnp.where(leading, chosen, 0.0) + inner_rows(short, wc[...])
        middle, gains, shifts = norm_back(grad, normals[1, at, :], scales[1, at, 0:1], gain[1:2, :])
        g1[at, :] = middle
        small[0, 1:2, :] += gains[None, :]
        small[0, 3:4, :] += shifts[None, :]
        small[0, 5:6, :] += jnp.sum(middle, axis=0, keepdims=True)
        small[0, 6:7, :] += jnp.sum(short.astype(F32), axis=0, keepdims=True)
        own = pl.multiple_of(feed_at + s * rows + group * share, share)
        pool[pl.ds(own, share), :] = middle.astype(BF)

        def view(mask, s=s):
            place = feed_at + s * rows + (group ^ data.shift(mask)[0]) * share
            return pool.at[pl.ds(pl.multiple_of(place, share), share)]

        taking = Gather(data, view, n_send, n_recv, s * groups)
        taking.start()
        takes.append(taking)

    @pl.loop(0, width // 256)
    def _(index):
        at = pl.ds(pl.multiple_of(index * 256, 256), 256)
        wc[at, :] = outer_rows(low[:, at], proj[...]).astype(BF)

    give_wc.start()

    gives = []
    for s in range(2):

        def read(mask, s=s):
            return sums[s, pl.ds(spot(mask), share), :]

        def write(mask, value, s=s):
            sums[s, pl.ds(spot(mask), share), :] = value

        gives.append(Scatter(data, read, write, s_out.at[s], s_in.at[s], r_send, r_recv, s * groups))
    for copy in ffn:
        copy.wait()
    tile = min(256, units)

    def shrink(s):
        at_rows = slice(s * rows, (s + 1) * rows)
        feed_rows = slice(feed_at + s * rows, feed_at + (s + 1) * rows)

        @pl.loop(0, units // tile)
        def _(index):
            at = pl.ds(pl.multiple_of(index * tile, tile), tile)
            down_at = pl.ds(pl.multiple_of(units + index * tile, tile), tile)
            value = inner_rows(pool[feed_rows, :], pool[down_at, :]) * slope[at_rows, at].astype(F32)
            value = value.astype(BF)
            slope[at_rows, at] = value
            small[0, 7:8, at] += jnp.sum(value.astype(F32), axis=0, keepdims=True)

        @pl.loop(0, width // 256)
        def _(index):
            at = pl.ds(pl.multiple_of(index * 256, 256), 256)
            sums[s, :, at] = dot(slope[at_rows, :], pool[at_up, at])

    def put(s):
        for mask in reversed(range(groups // 2, groups)):
            gives[s].put(mask)

    top = len(all_d) - 1
    last_t = len(all_t) - 1
    quad_top = len(all_t) + 1
    blocks = list(reversed(range(ranks // 2, ranks)))
    give_wc.level(quad_top)
    for mask in range(1, groups):
        takes[0].arrive(mask)
    shrink(0)
    put(0)
    for copy in later:
        copy.wait()
    for mask in range(1, groups):
        takes[1].arrive(mask)
    gives[0].level(top)

    @pl.loop(0, units // tile)
    def _(index):
        at = pl.ds(pl.multiple_of(index * tile, tile), tile)
        g_down[at, :] = outer_rows(active[:, at], pool[at_feed, :]).astype(BF)

    for mask in blocks[:2]:
        give_down.push(mask)
    give_wc.level(last_t + 1)
    shrink(1)
    put(1)

    @pl.loop(0, units // tile)
    def _(index):
        at = pl.ds(pl.multiple_of(index * tile, tile), tile)
        g_up[at, :] = outer_rows(slope[:, at], pool[at_normed, :]).astype(BF)

    gives[1].level(top)
    for mask in blocks[:1]:
        give_up.push(mask)

    for copy in last:
        copy.wait()
    def small_step(level):
        copy = remote(
            small.at[level], small_in.at[level], m_send.at[level], m_recv.at[level], {"tensor": rank ^ all_t[level]}
        )
        return copy

    small_copies = [small_step(level) for level in range(len(all_t))]

    def small_next(level):
        small_copies[level].wait_recv()
        small[level + 1] = small[level] + small_in[level]
        if level + 1 < len(all_t):
            small_copies[level + 1].start()

    sends = []
    for s in range(2):
        at = slice(s * share, (s + 1) * share)
        for level in reversed(range(top)):
            gives[s].level(level)
        grad = g1[at, :] + gives[s].read(0)
        hidden, gains, shifts = norm_back(grad, normals[0, at, :], scales[0, at, 0:1], gain[0:1, :])
        g1[at, :] = hidden
        small[0, 0:1, :] += gains[None, :]
        small[0, 2:3, :] += shifts[None, :]
        small[0, 4:5, :] += jnp.sum(hidden, axis=0, keepdims=True)
        short = hidden.astype(BF)
        turn[at, :] = short
        if columns % 128 == 0:
            value = inner_rows(short, out_all[...]).astype(BF)
            for r in range(ranks):
                ctx_out[r, at, :] = value[:, r * columns : (r + 1) * columns]
        else:
            for r in range(ranks):
                ctx_out[r, at, :] = inner_rows(short, out_all[r * columns : (r + 1) * columns, :]).astype(BF)
        mine = pl.ds(pl.multiple_of(rank * share, share), share)
        for item in range(1, ranks):
            copy = remote(
                ctx_out.at[rank ^ item, pl.ds(s * share, share)],
                heads_grad.at[s, mine],
                a_send.at[s * ranks + item],
                a_recv.at[s * ranks + item],
                {"tensor": rank ^ item},
            )
            copy.start()
            sends.append(copy)
        heads_grad[s, mine, :] = ctx_out[rank, at, :]
        if s == 1:
            for mask in blocks[1:2]:
                give_up.push(mask)
            small_copies[0].start()
    for taking in takes:
        taking.finish()
    tall = load(x_q, pool.at[pl.ds(0, span)]), load(x_p, pool.at[pl.ds(span, span)])
    at_qkv = 2 * span
    pairs = Lattice([("dp", step) for step in all_d[-2:]])
    back_in = load(h_qkv, pool.at[pl.ds(at_qkv, 3 * columns * ranks)])

    for r in range(ranks):
        out_all[r * columns : (r + 1) * columns, :] = outer_rows(ctx_rows[r], turn[...]).astype(BF)
    give_wc.level(last_t)
    give_out.start()

    block = min(BLOCK, span)

    lengths = (len_q[group], len_p[group])

    def attention(s, begin, end):
        keep = lax.broadcasted_iota(jnp.int32, (span, 1), 0) < lengths[s]

        @pl.loop(begin, end)
        def _(index):
            at = pl.ds(pl.multiple_of(index * block, block), block)
            query = q[s, at, :]
            grad = heads_grad[s, at, :]
            total = jnp.zeros((block, columns), F32)
            for head in range(heads):
                mask = head_mask(columns, head)
                mine = jnp.where(mask, query, jnp.zeros_like(query)) * jnp.asarray(scale, BF)
                back = jnp.where(mask, grad, jnp.zeros_like(grad))
                scores = jnp.where(keep, inner_rows(k[s], mine), -1e30)
                probs = jnp.exp(scores - lse[s, head : head + 1, at])
                slant = inner_rows(v[s], back)
                middle = jnp.sum(probs * slant, axis=0, keepdims=True)
                twist = (probs * (slant - middle)).astype(BF)
                dv_sum[...] += dot(probs.astype(BF), back)
                dk_sum[...] += dot(twist, mine)
                part = outer_rows(twist, k[s]) * scale
                total = jnp.where(mask, part, total)
            turned[s, at, 0:columns] = total.astype(BF)

    def attention_start(s):
        for item in range(1, ranks):
            place = heads_grad.at[s, pl.ds(pl.multiple_of((rank ^ item) * share, share), share)]
            remote(
                place, place, a_send.at[s * ranks + item], a_recv.at[s * ranks + item], {"tensor": rank ^ item}
            ).wait_recv()
        dk_sum[...] = jnp.zeros_like(dk_sum)
        dv_sum[...] = jnp.zeros_like(dv_sum)

    def attention_end(s):
        turned[s, :, columns : 2 * columns] = dk_sum[...].astype(BF)
        turned[s, :, 2 * columns : 3 * columns] = dv_sum[...].astype(BF)
        for item in range(1, ranks):
            copy = remote(
                turned.at[s, pl.ds(pl.multiple_of((rank ^ item) * share, share), share)],
                turned_rows.at[rank, pl.ds(s * share, share)],
                t_send.at[s * ranks + item],
                t_recv.at[s * ranks + item],
                {"tensor": rank ^ item},
            )
            copy.start()
            sends.append(copy)
        turned_rows[rank, s * share : (s + 1) * share, :] = turned[
            s, pl.ds(pl.multiple_of(rank * share, share), share), :
        ]

    many = qkv_sum.shape[1]

    def qkv_grad(s):
        tokens = pool[s * span : (s + 1) * span, :]
        for i in range(3):
            part = turned[s, :, i * columns : (i + 1) * columns]
            whole = outer_rows(tokens, part)
            line = jnp.broadcast_to(jnp.sum(part.astype(F32), axis=0, keepdims=True), (many - width, columns))
            if s == 0:
                qkv_sum[i, 0:width, :] = whole
                qkv_sum[i, width:many, :] = line
            else:
                qkv_sum[i, 0:width, :] += whole
                qkv_sum[i, width:many, :] += line

    for copy in heads_in:
        copy.wait()
    count = span // block
    attention_start(0)
    attention(0, 0, count // 2)
    for mask in blocks[2:]:
        give_down.push(mask)
    for level in reversed(range(1, last_t)):
        give_wc.level(level)
    small_next(0)
    give_wc.level(0)
    for mask in blocks[2:]:
        give_up.push(mask)
    attention(0, count // 2, count)
    attention_end(0)
    for copy in tall:
        copy.wait()
    qkv_grad(0)
    attention_start(1)
    for level in range(1, len(all_t)):
        small_next(level)
    attention(1, 0, count // 2)
    small_own = small.at[len(all_t)]
    small_take = Gather(data, lambda m: o_small.at[group ^ data.shift(m)[0]], f_send, f_recv, 0, own=small_own)
    small_take.start()
    small_copy = load(small_own, o_small.at[group])
    give_up.level(last_t)
    attention(1, count // 2, count)
    attention_end(1)
    give_out.level(quad_top)

    rest = all_d[:-2]

    def settle_stage(which, source, size):
        base = which * max(1, len(rest))
        copies = []
        for index, step in enumerate(rest):
            src = source if index == 0 else stage.at[base + index - 1, pl.ds(0, size)]
            dst = stage_in.at[base + index, pl.ds(0, size)]
            copies.append(remote(src, dst, y_send.at[base + index], y_recv.at[base + index], {"dp": group ^ step}))
        for index, copy in enumerate(copies):
            copy.start()
            copy.wait_recv()
            before = source[...] if index == 0 else stage[base + index - 1, 0:size, :]
            value = before.astype(F32) + stage_in[base + index, 0:size, :].astype(F32)
            stage[base + index, 0:size, :] = value.astype(BF)
        return (stage.at[base + len(rest) - 1, pl.ds(0, size)] if rest else source), copies

    def dp_view(ref):
        return lambda m: ref.at[pl.ds(pl.multiple_of((group ^ data.shift(m)[0]) * piece, piece), piece)]

    def out_view(mask):
        d, _ = pairs.shift(mask)
        return o_out.at[pl.ds(pl.multiple_of(((group ^ d) % 4) * quarter, quarter), quarter)]

    out_base = 2 * groups + quad.count

    def rows_end(s):
        at = slice(s * share, (s + 1) * share)
        for item in range(1, ranks):
            place = turned_rows.at[rank ^ item, pl.ds(s * share, share)]
            remote(
                place, place, t_send.at[s * ranks + item], t_recv.at[s * ranks + item], {"tensor": rank ^ item}
            ).wait_recv()
        total = g1[at, :]
        for r in range(ranks):
            begin = at_qkv + r * 3 * columns
            total = total + dot(turned_rows[r, at, :], pool[begin : begin + 3 * columns, :])
        unit[at, :] = total

    back_in.wait()
    rows_end(0)
    give_up.level(last_t - 1)
    give_down.level(last_t)
    qkv_grad(1)

    part = many // 2
    at_mine = pl.ds(pl.multiple_of((group % 2) * part, part), part)
    at_other = pl.ds(pl.multiple_of((1 - group % 2) * part, part), part)
    near = {"dp": group ^ all_d[-1]}
    qkv_low[0] = qkv_sum[:, at_other, :].astype(BF)
    qkv_copies = [remote(qkv_low.at[0], qkv_in.at[0], q_send.at[0], q_recv.at[0], near)]
    qkv_copies[0].start()
    for index, step in enumerate(far_d):
        slot = 1 + index
        qkv_copies.append(
            remote(qkv_low.at[slot], qkv_in.at[slot], q_send.at[slot], q_recv.at[slot], {"dp": group ^ step})
        )
    qkv_last = len(far_d) + 1
    qkv_own = qkv_low.at[qkv_last]
    qkv_copies.append(remote(qkv_own, o_qkv.at[:, at_mine], q_send.at[qkv_last], q_recv.at[qkv_last], near))

    wc_own, wc_copies = settle_stage(0, give_wc.view(0), flat)
    wc_take = Gather(quad, quarters(o_wc, flat), f_send, f_recv, groups, own=wc_own)
    wc_take.start()
    wc_copy = load(wc_own, wc_take.view(0))
    qkv_copies[0].wait_recv()
    sum_half = qkv_sum[:, at_mine, :].astype(BF).astype(F32) + qkv_in[0].astype(F32)
    qkv_low[1] = sum_half.astype(BF)
    qkv_copies[1].start()
    for level in reversed(range(last_t - 1)):
        give_up.level(level)
    up_own = give_up.view(0)
    up_take = Gather(data, dp_view(o_up), f_send, f_recv, out_base + 4, own=up_own)
    up_take.start()
    up_copy = load(up_own, up_take.view(0))
    give_out.level(quad_top - 1)
    for mask in range(1, ranks // 2):
        wc_take.arrive(mask)
    give_down.level(last_t - 1)
    give_out.level(last_t)
    for index in range(len(far_d)):
        qkv_copies[1 + index].wait_recv()
        qkv_low[2 + index] = (qkv_low[1 + index].astype(F32) + qkv_in[1 + index].astype(F32)).astype(BF)
        qkv_copies[index + 2].start()
    qkv_local = load(qkv_own, o_qkv.at[:, at_mine])
    for mask in range(ranks // 2, quad.count):
        wc_take.arrive(mask)
    for level in reversed(range(last_t - 1)):
        give_down.level(level)
    down_own = give_down.view(0)
    down_take = Gather(data, dp_view(o_down), f_send, f_recv, groups + quad.count, own=down_own)
    down_take.start()
    down_copy = load(down_own, down_take.view(0))
    give_out.level(last_t - 1)
    rows_end(1)
    tokens_copy = load(unit, o_tokens)
    for level in reversed(range(last_t - 1)):
        give_out.level(level)
    out_own, out_copies = settle_stage(1, give_out.view(0), quarter)
    out_take = Gather(pairs, out_view, f_send, f_recv, out_base, own=out_own)
    out_take.start()
    out_copy = load(out_own, out_view(0))
    for taking in (small_take, down_take, up_take):
        for mask in range(1, groups):
            taking.arrive(mask)
    for mask in range(1, 4):
        out_take.arrive(mask)
    at_theirs = o_qkv.at[:, at_other]
    remote(at_theirs, at_theirs, q_send.at[qkv_last], q_recv.at[qkv_last], near).wait_recv()
    for move in [give_wc, give_out, give_down, give_up, small_take, wc_take, down_take, up_take, out_take] + gives:
        move.finish()
    for copy in sends + small_copies + qkv_copies + wc_copies + out_copies:
        copy.wait_send()
    for copy in (tokens_copy, small_copy, wc_copy, down_copy, qkv_local, out_copy, up_copy):
        copy.wait()


def backward(len_q, len_p, grad_vec, unit, low, scales, normals, w_colbert, down, up, slope, active, normed, out_all,
             context_rows, query, key, value, lse, queries, passages, qkv_all, gain):
    groups, ranks = lax.axis_size("dp"), lax.axis_size("tensor")
    all_t, all_d = steps_of(ranks), steps_of(groups)
    span, width = queries.shape
    columns = query.shape[2]
    heads = columns // HEAD_DIM
    share = span // ranks
    units = up.shape[0]
    piece = units // ranks
    rows = groups * share
    quarter, flat = columns // 4, width // ranks // 4
    pool = max(2 * units + 4 * rows, 2 * span + 3 * columns * ranks)
    many = width + 32
    far = len(all_d) - 1
    dma = pltpu.SemaphoreType.DMA
    vmem = pltpu.VMEM
    hold, leave = pl.BlockSpec(memory_space=pltpu.VMEM), pl.BlockSpec(memory_space=pl.ANY)
    shapes = [
        ((2 * share, width), F32),
        ((units // ranks * groups, width), BF),
        ((units // ranks * groups, width), BF),
        ((columns, width), BF),
        ((width, width), BF),
        ((3, many, columns), BF),
        ((groups, 8, width), F32),
    ]
    smem = pl.BlockSpec(memory_space=pltpu.SMEM)
    rest = max(1, len(all_d) - 2)

    def pair(count):
        return [dma((count,)), dma((count,))]

    return pl.pallas_call(
        functools.partial(backward_kernel, all_t, all_d),
        out_shape=[jax.ShapeDtypeStruct(*item) for item in shapes],
        in_specs=[smem, smem] + [leave] * 20 + [hold],
        out_specs=[leave] * len(shapes),
        scratch_shapes=[
            vmem((pool, width), BF),
            vmem((2 * rows, units), BF),
            vmem((2 * rows, units), BF),
            vmem((ranks * columns, width), BF),
            vmem((width, width), BF),
            vmem((ranks, 2 * share, columns), BF),
            vmem((2, span, columns), BF),
            vmem((2, span, columns), BF),
            vmem((2, span, columns), BF),
            vmem((2, heads, span), F32),
            vmem((2 * share, width), F32),
            vmem((2 * share, width), F32),
            vmem((2 * share, width), BF),
            vmem((2 * share, width), BF),
            vmem((2, 2 * share, width), F32),
            vmem((3, 2 * share, 128), F32),
            vmem((2, rows, width), F32),
            vmem((2, groups - 1, share, width), BF),
            vmem((2, groups - 1, share, width), BF),
            vmem((2 * share, width), BF),
            vmem((ranks, 2 * share, columns), BF),
            vmem((2, span, columns), BF),
            vmem((2, span, 3 * columns), BF),
            vmem((ranks, 2 * share, 3 * columns), BF),
            vmem((span, columns), F32),
            vmem((span, columns), F32),
            vmem((units, width), BF),
            vmem((ranks - 1, piece, width), BF),
            vmem((units, width), BF),
            vmem((ranks - 1, piece, width), BF),
            vmem((4 * ranks - 1, quarter, width), BF),
            vmem((4 * ranks - 1, flat, width), BF),
            vmem((3, many, columns), F32),
            vmem((2 + far, 3, many // 2, columns), BF),
            vmem((1 + far, 3, many // 2, columns), BF),
            vmem((len(all_t) + 1, 8, width), F32),
            vmem((len(all_t), 8, width), F32),
            vmem((2 * rest, max(quarter, flat), width), BF),
            vmem((2 * rest, max(quarter, flat), width), BF),
            dma((32,)),
        ]
        + pair(2 * groups)
        + pair(2 * groups)
        + pair(ranks)
        + pair(ranks)
        + pair(4 * ranks)
        + pair(4 * ranks)
        + pair(2 * ranks)
        + pair(2 * ranks)
        + pair(3 * groups + 4 * ranks + 4)
        + pair(len(all_t))
        + pair(2 * rest)
        + pair(2 + far),
        compiler_params=pltpu.CompilerParams(
            collective_id=3, has_side_effects=True, vmem_limit_bytes=62 * 2**20
        ),
        cost_estimate=pl.CostEstimate(flops=10**11, bytes_accessed=40 * 2**20, transcendentals=2**22),
        name="backward",
    )(len_q, len_p, grad_vec, unit, low, scales, normals, w_colbert, down, up, slope, active, normed, out_all,
      context_rows, query, key, value, lse, queries, passages, qkv_all, gain)


def finish_kernel(
    rank_of, low, tokens, down, up, out, wc, qkv, small,
    out_q, out_p, tok_q, tok_p, g_qkv, g_bias, g_out, g_up, g_in, g_down, g_gain, g_shift, g_offset, g_wc,
    v_low, v_tokens, v_down, v_up, v_out, v_wc, v_qkv, f_down, f_up, f_out, f_wc, f_qkv, load, store,
):
    share, width = out_q.shape
    copies = []

    def begin(src, dst, sem):
        copy = pltpu.make_async_copy(src, dst, sem)
        copy.start()
        return copy

    loads = [
        begin(src, dst, load.at[index])
        for index, (src, dst) in enumerate(
            ((down, v_down), (up, v_up), (wc, v_wc), (qkv, v_qkv), (out, v_out), (low, v_low), (tokens, v_tokens))
        )
    ]
    loads[0].wait()
    f_down[...] = v_down[...].astype(F32)
    copies.append(begin(f_down, g_down, store.at[4]))
    loads[1].wait()
    f_up[...] = v_up[...].astype(F32).T
    copies.append(begin(f_up, g_up, store.at[5]))
    loads[2].wait()
    f_wc[...] = v_wc[...].astype(F32)
    copies.append(begin(f_wc, g_wc, store.at[6]))
    loads[3].wait()
    f_qkv[...] = v_qkv[:, 0:width, :].astype(F32)
    copies.append(begin(f_qkv, g_qkv, store.at[7]))
    g_bias[0:1, :] = v_qkv[0, width : width + 16, :].astype(F32)[0:1, :]
    g_bias[1:2, :] = v_qkv[2, width : width + 16, :].astype(F32)[0:1, :]
    loads[4].wait()
    f_out[...] = v_out[...].astype(F32)
    copies.append(begin(f_out, g_out, store.at[8]))
    groups = small.shape[0]
    total = small[0]
    for index in range(1, groups):
        total = total + small[index]
    g_gain[...] = total[0:2]
    g_shift[...] = total[2:4]
    g_offset[...] = total[4:7]
    piece = g_in.shape[1]
    for index in range(groups):
        if piece % 128 == 0:
            at = pl.ds(pl.multiple_of(rank_of[0] * piece, piece), piece)
            g_in[index : index + 1, :] = small[index, 7:8, at]
    loads[5].wait()
    copies.append(begin(v_low.at[pl.ds(0, share)], out_q, store.at[0]))
    copies.append(begin(v_low.at[pl.ds(share, share)], out_p, store.at[1]))
    loads[6].wait()
    copies.append(begin(v_tokens.at[pl.ds(0, share)], tok_q, store.at[2]))
    copies.append(begin(v_tokens.at[pl.ds(share, share)], tok_p, store.at[3]))
    for copy in copies:
        copy.wait()


def finish(low, tokens, down, up, out, wc, qkv, small, piece):
    share, width = low.shape[0] // 2, low.shape[1]
    hidden, columns = down.shape[0], out.shape[0]
    groups = small.shape[0]
    hold, leave = pl.BlockSpec(memory_space=pltpu.VMEM), pl.BlockSpec(memory_space=pl.ANY)
    rank_of = lax.axis_index("tensor").reshape(1).astype(jnp.int32)
    shapes = [
        ((share, width), BF),
        ((share, width), BF),
        ((share, width), F32),
        ((share, width), F32),
        ((3, width, columns), F32),
        ((2, columns), F32),
        ((columns, width), F32),
        ((width, hidden), F32),
        ((groups, piece), F32),
        ((hidden, width), F32),
        ((2, width), F32),
        ((2, width), F32),
        ((3, width), F32),
        ((width, width), F32),
    ]
    vmem, dma = pltpu.VMEM, pltpu.SemaphoreType.DMA
    return pl.pallas_call(
        finish_kernel,
        out_shape=[jax.ShapeDtypeStruct(*item) for item in shapes],
        in_specs=[pl.BlockSpec(memory_space=pltpu.SMEM)] + [leave] * 7 + [hold],
        out_specs=[leave] * 5 + [hold, leave, leave, hold, leave, hold, hold, hold, leave],
        scratch_shapes=[
            vmem(low.shape, BF),
            vmem(tokens.shape, F32),
            vmem(down.shape, BF),
            vmem(up.shape, BF),
            vmem(out.shape, BF),
            vmem(wc.shape, BF),
            vmem(qkv.shape, BF),
            vmem(down.shape, F32),
            vmem((width, hidden), F32),
            vmem(out.shape, F32),
            vmem(wc.shape, F32),
            vmem((3, width, columns), F32),
            dma((7,)),
            dma((9,)),
        ],
        compiler_params=pltpu.CompilerParams(vmem_limit_bytes=62 * 2**20),
        name="finish",
    )(rank_of, low, tokens, down, up, out, wc, qkv, small)


def per_device(
    queries,
    passages,
    query_lengths,
    passage_lengths,
    w_qkv,
    qv_bias,
    w_out,
    w_in,
    in_bias,
    w_down,
    norm_gain,
    norm_shift,
    layer_bias,
    w_colbert,
    dense_cot,
    colbert_cot,
):
    groups, ranks = lax.axis_size("dp"), lax.axis_size("tensor")
    group, rank = lax.axis_index("dp"), lax.axis_index("tensor")
    width = queries.shape[1]
    columns = w_qkv.shape[2]
    piece = w_in.shape[1] // groups
    units = piece * ranks

    up_piece = lax.dynamic_slice_in_dim(w_in, group * piece, piece, 1).T
    slim = 3 * columns // 2
    turned = w_qkv.transpose(0, 2, 1).reshape(3 * columns, width)
    qkv_piece = lax.dynamic_slice_in_dim(turned, (group % 2) * slim, slim, 0)
    if piece % 128 == 0:
        bias_in = lax.dynamic_slice_in_dim(in_bias, group * piece, piece, 0)
        bias_in = jnp.broadcast_to(bias_in[None, :], (16, piece))
    else:
        bias_in = lax.all_gather(in_bias, "tensor").reshape(ranks, groups, piece)
        bias_in = lax.dynamic_index_in_dim(bias_in, group, 1, keepdims=False).reshape(1, -1).astype(F32)
    (
        query,
        key,
        value,
        lse,
        context_rows,
        out_all,
        up,
        down,
        qkv_all,
        normed,
        slope,
        active,
        normals,
        unit,
        low,
        scales,
        grad_vec,
    ) = forward(
        query_lengths, passage_lengths, dense_cot, colbert_cot, queries, passages, w_qkv, qv_bias, w_out, up_piece,
        w_down, qkv_piece, bias_in, norm_gain, norm_shift, layer_bias, w_colbert,
    )
    tokens, grad_down, grad_up, grad_out, colbert, grad_qkv, small = backward(
        query_lengths, passage_lengths, grad_vec, unit, low, scales, normals, w_colbert, down, up, slope, active,
        normed.reshape(-1, width), out_all.reshape(-1, width), context_rows, query, key, value, lse,
        queries, passages, qkv_all.reshape(-1, width), norm_gain,
    )
    results = list(finish(low, tokens, grad_down, grad_up, grad_out, colbert, grad_qkv, small, piece))
    if piece % 128:
        bias = small[:, 7, :units].reshape(groups, ranks, piece)
        results[8] = lax.dynamic_index_in_dim(bias, rank, 1, keepdims=False)
    results[8] = results[8].reshape(-1)
    return tuple(results)


def solution(mesh):
    both = P(("dp", "tensor"), None)
    return jax.shard_map(
        per_device,
        mesh=mesh,
        in_specs=(
            P("dp", None),
            P("dp", None),
            P(),
            P(),
            P(None, None, "tensor"),
            P(None, "tensor"),
            P("tensor", None),
            P(None, "tensor"),
            P("tensor"),
            P("tensor", None),
            P(),
            P(),
            P(),
            P(),
            P(),
            P(),
        ),
        out_specs=(
            both,
            both,
            both,
            both,
            P(None, None, "tensor"),
            P(None, "tensor"),
            P("tensor", None),
            P(None, "tensor"),
            P("tensor"),
            P("tensor", None),
            P(),
            P(),
            P(),
            P(),
        ),
        check_vma=False,
    )
```

```python
import functools

import jax
import jax.numpy as jnp
from jax import lax
from jax.experimental import pallas as pl
from jax.experimental.pallas import tpu as pltpu
from jax.sharding import PartitionSpec as P

HEAD_DIM = 64
BF = jnp.bfloat16
F32 = jnp.float32
BLOCK = 256


def dot(left, right):
    return jnp.dot(left, right, preferred_element_type=F32)


def inner_rows(left, right):
    return lax.dot_general(left, right, (((1,), (1,)), ((), ())), preferred_element_type=F32)


def outer_rows(left, right):
    return lax.dot_general(left, right, (((0,), (0,)), ((), ())), preferred_element_type=F32)


def steps_of(size):
    steps = []
    while size > 1:
        size //= 2
        steps.append(size)
    return steps


def offsets(steps):
    found = [0]
    for step in steps:
        found = found + [item ^ step for item in found]
    return found


def swap(value, axis, step):
    size = lax.axis_size(axis)
    return lax.ppermute(value, axis, [(index, index ^ step) for index in range(size)])


def spread(value, axis, steps):
    held = value[None]
    for step in steps:
        held = jnp.concatenate([held, swap(held, axis, step)], axis=0)
    return held


def fold(parts, axis, steps):
    for step in reversed(steps):
        half = parts.shape[0] // 2
        came = swap(parts[half:].astype(BF), axis, step)
        parts = parts[:half].astype(F32) + came.astype(F32)
    return parts[0]


def natural(parts, axis, steps, dim=0):
    order = offsets(steps)
    size = len(order)
    place = [0] * size
    for spot, item in enumerate(order):
        place[item] = spot
    table = jnp.array(place, jnp.int32)
    rank = lax.axis_index(axis)
    return jnp.concatenate(
        [lax.dynamic_slice_in_dim(parts, table[item ^ rank], 1, dim) for item in range(size)], axis=dim
    )


def xored(parts, axis, steps, dim=0):
    rank = lax.axis_index(axis)
    return jnp.concatenate(
        [lax.dynamic_slice_in_dim(parts, item ^ rank, 1, dim) for item in offsets(steps)], axis=dim
    )


def trade(parts, steps, dim):
    rank = lax.axis_index("tensor")
    got = []
    for item in offsets(steps):
        piece = lax.dynamic_index_in_dim(parts, item ^ rank, dim, keepdims=False)
        got.append(swap(piece, "tensor", item) if item else piece)
    return got


def layer_norm(hidden, gain, shift):
    centre = hidden - jnp.mean(hidden, axis=-1, keepdims=True)
    inverse = lax.rsqrt(jnp.mean(centre * centre, axis=-1, keepdims=True) + 1e-05)
    normal = centre * inverse
    return (normal * gain + shift, normal, inverse)


def norm_back(grad, normal, inverse, gain):
    scaled = grad * gain
    middle = (
        scaled
        - jnp.mean(scaled, axis=-1, keepdims=True)
        - normal * jnp.mean(scaled * normal, axis=-1, keepdims=True)
    )
    return (middle * inverse, jnp.sum(grad * normal, axis=0), jnp.sum(grad, axis=0))


def gelu_slope(inner):
    return (
        0.5 * (1.0 + lax.erf(inner * 0.7071067811865476))
        + inner * jnp.exp(-0.5 * inner * inner) * 0.3989422804014327
    )


def head_mask(columns, head):
    lane = lax.broadcasted_iota(jnp.int32, (1, columns), 1)
    return (lane >= head * HEAD_DIM) & (lane < (head + 1) * HEAD_DIM)


MESH = pl.DeviceIdType.MESH


class Lattice:
    def __init__(self, steps):
        self.steps = steps
        self.count = 1 << len(steps)

    def peer(self, level):
        axis, step = self.steps[level]
        return {axis: lax.axis_index(axis) ^ step}

    def index(self, mask):
        found = 0
        for level, (axis, step) in enumerate(self.steps):
            bit = (lax.axis_index(axis) // step) % 2
            found = found + (1 - bit if mask >> level & 1 else bit) * (1 << level)
        return found

    def member(self, axis, block):
        found = lax.axis_index(axis)
        for level, (name, step) in enumerate(self.steps):
            if name == axis:
                found = found + ((block // (1 << level)) % 2 - (lax.axis_index(axis) // step) % 2) * step
        return found

    def shift(self, mask):
        found = {"dp": 0, "tensor": 0}
        for level, (axis, step) in enumerate(self.steps):
            if mask >> level & 1:
                found[axis] ^= step
        return found["dp"], found["tensor"]


def remote(src, dst, send, recv, peer):
    return pltpu.make_async_remote_copy(
        src_ref=src, dst_ref=dst, send_sem=send, recv_sem=recv, device_id=peer, device_id_type=MESH
    )


class Gather:
    def __init__(self, lattice, view, send, recv, base=0, own=None):
        self.lattice, self.view, self.send, self.recv, self.base = lattice, view, send, recv, base
        self.own = own
        self.sent = []

    def copy(self, level, mask):
        slot = self.base + (1 << level) + mask
        place = self.view(mask)
        src = self.own if mask == 0 and self.own is not None else place
        return remote(src, place, self.send.at[slot], self.recv.at[slot], self.lattice.peer(level))

    def start(self, levels=None):
        for level in range(len(self.lattice.steps)) if levels is None else levels:
            copy = self.copy(level, 0)
            copy.start()
            self.sent.append(copy)

    def arrive(self, mask):
        level = mask.bit_length() - 1
        slot = self.base + mask
        place = self.view(mask)
        remote(place, place, self.send.at[slot], self.recv.at[slot], self.lattice.peer(level)).wait_recv()
        for later in range(level + 1, len(self.lattice.steps)):
            copy = self.copy(later, mask)
            copy.start()
            self.sent.append(copy)

    def finish(self):
        for copy in self.sent:
            copy.wait_send()


class Scatter:
    def __init__(self, lattice, read, write, out, came, send, recv, base=0):
        self.lattice, self.read, self.write = lattice, read, write
        self.out, self.came, self.send, self.recv, self.base = out, came, send, recv, base
        self.sent = []

    def push(self, mask):
        level = mask.bit_length() - 1
        slot = self.base + mask
        copy = remote(
            self.out.at[mask - 1],
            self.came.at[mask - 1],
            self.send.at[slot],
            self.recv.at[slot],
            self.lattice.peer(level),
        )
        copy.start()
        self.sent.append(copy)

    def put(self, mask):
        self.out[mask - 1] = self.read(mask).astype(BF)
        self.push(mask)

    def level(self, level):
        for mask in reversed(range(1 << level)):
            slot = (1 << level) + mask
            place = self.came.at[slot - 1]
            remote(
                self.out.at[slot - 1],
                place,
                self.send.at[self.base + slot],
                self.recv.at[self.base + slot],
                self.lattice.peer(level),
            ).wait_recv()
            total = self.read(mask) + self.came[slot - 1].astype(F32)
            if mask and mask >= 1 << (level - 1):
                self.out[mask - 1] = total.astype(BF)
                self.push(mask)
            else:
                self.write(mask, total)

    def run(self):
        for level in reversed(range(len(self.lattice.steps))):
            self.level(level)

    def finish(self):
        for copy in self.sent:
            copy.wait_send()


def score_steps(all_t, all_d):
    if len(all_d) <= 2:
        rows_q = [("tensor", step) for step in all_t[1:-1]] + [("dp", step) for step in all_d]
        rows_p = [("tensor", step) for step in all_t[:1] + all_t[-1:]]
    else:
        rows_q = [("tensor", step) for step in all_t[:-1]] + [("dp", step) for step in all_d[-1:]]
        rows_p = [("dp", step) for step in all_d[:-1]] + [("tensor", step) for step in all_t[-1:]]
    return rows_q, rows_p


def score_peers(all_t, rows_p):
    return [item for item in offsets([step for step in all_t if ("tensor", step) not in rows_p]) if item]


def greet(peers):
    barrier = pltpu.get_barrier_semaphore()
    for peer in peers:
        pl.semaphore_signal(barrier, inc=1, device_id=peer, device_id_type=MESH)
    pl.semaphore_wait(barrier, len(peers))


def forward_kernel(
    all_t, all_d, ship_bias,
    len_q, len_p, dense_cot, late_cot,
    x_q, x_p, w_qkv, qv_bias, w_out, up_piece, w_down, qkv_piece, bias_in, gain, shift, offset, w_colbert,
    o_q, o_k, o_v, o_lse, o_ctx, o_out, o_up, o_down, o_qkv, o_normed, o_slope, o_active,
    o_normal, o_unit, o_low, o_spread, o_grad,
    x, q, k, v, ctx, lse, ctx_rows, out_all, up, down, normed, slope, active, sums, s_out, s_in,
    first, normal, unit, vec, low, scales, wc, bias_all, bias_row,
    rows_q, rows_p, raised, pull, mass, mass_in, out_q, in_q, sum_p, out_p, in_p, grad,
    local, g_send, g_recv, a_send, a_recv, b_send, b_recv, n_send, n_recv, r_send, r_recv,
    gq_send, gq_recv, gp_send, gp_recv, m_send, m_recv, rq_send, rq_recv, rp_send, rp_recv,
):
    group, rank = lax.axis_index("dp"), lax.axis_index("tensor")
    ranks, groups = 1 << len(all_t), 1 << len(all_d)
    span, width = x_q.shape
    columns = w_qkv.shape[2]
    share = span // ranks
    piece = up_piece.shape[0]
    units = up.shape[0]
    quarter = columns // 4
    rows = groups * share
    heads = columns // HEAD_DIM
    scale = HEAD_DIM**-0.5

    x_copies = [pltpu.make_async_copy(src, x.at[s], local.at[s]) for s, src in enumerate((x_q, x_p))]
    for copy in x_copies:
        copy.start()
    wc_copy = pltpu.make_async_copy(w_colbert, wc, local.at[2])
    wc_copy.start()
    greet([{"tensor": rank ^ item} for item in range(1, ranks)] + [{"dp": group ^ item} for item in all_d])

    tensor = Lattice([("tensor", step) for step in all_t])
    quad = Lattice([("tensor", step) for step in all_t] + [("dp", step) for step in all_d[-2:]])
    data = Lattice([("dp", step) for step in all_d])

    def quarters(ref, size):
        def view(mask):
            d, t = quad.shift(mask)
            return ref.at[rank ^ t, pl.ds(pl.multiple_of(((group ^ d) % 4) * size, size), size)]

        return view

    def unit_rows(ref):
        return lambda mask: ref.at[pl.ds(pl.multiple_of((rank ^ tensor.shift(mask)[1]) * piece, piece), piece)]

    wide, tall = quad.count, tensor.count
    far, near = list(range(len(all_t) - 1)), [len(all_t) - 1]
    at_quarter = pl.ds(pl.multiple_of((group % 4) * quarter, quarter), quarter)
    at_piece = pl.ds(pl.multiple_of(group * piece, piece), piece)
    take_out = Gather(quad, quarters(out_all, quarter), g_send, g_recv, 0, own=w_out.at[at_quarter])
    take_up = Gather(tensor, unit_rows(up), g_send, g_recv, wide, own=up_piece)
    take_down = Gather(tensor, unit_rows(down), g_send, g_recv, wide + tall, own=w_down.at[at_piece])
    cores = Lattice([("tensor", step) for step in all_t] + [("dp", all_d[-1])])
    slab = qkv_piece.shape[0]

    def slab_view(mask):
        d, t = cores.shift(mask)
        return o_qkv.at[rank ^ t, pl.ds(pl.multiple_of(((group ^ d) % 2) * slab, slab), slab)]

    take_qkv = Gather(cores, slab_view, g_send, g_recv, wide + 2 * tall, own=qkv_piece)
    own_copies = [
        pltpu.make_async_copy(w_out.at[at_quarter], take_out.view(0), local.at[3]),
        pltpu.make_async_copy(up_piece, take_up.view(0), local.at[4]),
        pltpu.make_async_copy(w_down.at[at_piece], take_down.view(0), local.at[5]),
        pltpu.make_async_copy(qkv_piece, take_qkv.view(0), local.at[6]),
    ]
    early = [tall // 4] + list(range(1, tall // 4))
    late = list(range(tall // 4 + 1, tall // 2))
    take_out.start()
    take_up.start(near)
    for copy in own_copies:
        copy.start()
    pending = []
    bias_copies = []
    if ship_bias:
        bias_all[rank] = bias_in[...]
        for item in range(1, ranks):
            copy = remote(
                bias_in, bias_all.at[rank], b_send.at[item], b_recv.at[item], {"tensor": rank ^ item}
            )
            copy.start()
            bias_copies.append(copy)

    lengths = (len_q[group], len_p[group])
    def project(s):
        x_copies[s].wait()
        tokens = x[s]
        q[s] = (dot(tokens, w_qkv[0]) + qv_bias[0:1, :].astype(F32)).astype(BF)
        k[s] = dot(tokens, w_qkv[1]).astype(BF)
        v[s] = (dot(tokens, w_qkv[2]) + qv_bias[1:2, :].astype(F32)).astype(BF)

    block = min(BLOCK, span)

    def attention(s, begin, end):
        keep = lax.broadcasted_iota(jnp.int32, (1, span), 1) < lengths[s]

        @pl.loop(begin, end)
        def _(index):
            at = pl.ds(pl.multiple_of(index * block, block), block)
            query = q[s, at, :]
            total = jnp.zeros((block, columns), F32)
            for head in range(heads):
                mask = head_mask(columns, head)
                mine = jnp.where(mask, query, jnp.zeros_like(query)) * jnp.asarray(scale, BF)
                scores = jnp.where(keep, inner_rows(mine, k[s]), -1e30)
                top = jnp.max(scores, axis=-1, keepdims=True)
                weight = jnp.exp(scores - top)
                amount = jnp.sum(weight, axis=-1, keepdims=True)
                part = dot(weight.astype(BF), v[s]) / amount
                total = jnp.where(mask, part, total)
                column = jnp.broadcast_to(top + jnp.log(amount), (block, 128))
                lse[s, head : head + 1, at] = column.T[0:1, :]
            ctx[s, at, :] = total.astype(BF)

    sends = []

    def trade_context(s):
        at = pl.ds(s * share, share)
        for item in range(1, ranks):
            peer = rank ^ item
            copy = remote(
                ctx.at[s, pl.ds(pl.multiple_of(peer * share, share), share)],
                ctx_rows.at[rank, at],
                a_send.at[s * ranks + item],
                a_recv.at[s * ranks + item],
                {"tensor": peer},
            )
            copy.start()
            sends.append(copy)
        ctx_rows[rank, s * share : (s + 1) * share, :] = ctx[s, pl.ds(pl.multiple_of(rank * share, share), share), :]

    def context_here(s):
        at = pl.ds(s * share, share)
        for item in range(1, ranks):
            place = ctx_rows.at[rank ^ item, at]
            remote(
                place, place, a_send.at[s * ranks + item], a_recv.at[s * ranks + item], {"tensor": rank ^ item}
            ).wait_recv()

    def out_going(src, dst, index):
        copy = pltpu.make_async_copy(src, dst, local.at[index])
        copy.start()
        pending.append(copy)

    def arrive(taking, masks):
        for mask in masks:
            taking.arrive(mask)

    count = span // block
    take_down.start(near)
    project(0)
    arrive(take_out, early)
    take_up.start(far)
    arrive(take_out, late)
    attention(0, 0, count)
    trade_context(0)
    for copy in own_copies:
        copy.wait()
    project(1)
    arrive(take_up, early[:1])
    attention(1, 0, count // 2)
    arrive(take_up, early[1:])
    attention(1, count // 2, count)
    take_down.start(far)
    arrive(take_out, range(tall // 2, wide))
    arrive(take_up, late)
    trade_context(1)
    out_going(q, o_q, 7)
    out_going(k, o_k, 8)
    out_going(v, o_v, 9)
    out_going(lse, o_lse, 10)

    def to_rows(s):
        at = slice(s * share, (s + 1) * share)
        context_here(s)
        if columns % 128 == 0:
            mix = jnp.concatenate([ctx_rows[r, at, :] for r in range(ranks)], axis=1)
            mixed = dot(mix, out_all[...].reshape(ranks * columns, width))
        else:
            mixed = dot(ctx_rows[0, at, :], out_all[0])
            for r in range(1, ranks):
                mixed = mixed + dot(ctx_rows[r, at, :], out_all[r])
        mine = x[s, pl.ds(pl.multiple_of(rank * share, share), share), :].astype(F32)
        value, plain, inverse = layer_norm(mine + mixed + offset[0:1, :], gain[0:1, :], shift[0:1, :])
        first[at, :] = value
        normal[0, at, :] = plain
        scales[0, at, :] = jnp.broadcast_to(inverse, (share, 128))
        normed[s, pl.ds(pl.multiple_of(group * share, share), share), :] = value.astype(BF)

        def view(mask):
            d, _ = data.shift(mask)
            return normed.at[s, pl.ds(pl.multiple_of((group ^ d) * share, share), share)]

        taking = Gather(data, view, n_send, n_recv, s * groups)
        taking.start()
        return taking

    normed_takes = [to_rows(0)]
    arrive(take_down, early)
    normed_takes.append(to_rows(1))
    arrive(take_up, range(tall // 2, tall))
    arrive(take_down, late)
    take_qkv.start()
    if ship_bias:
        for item in range(1, ranks):
            place = bias_all.at[rank ^ item]
            remote(place, place, b_send.at[item], b_recv.at[item], {"tensor": rank ^ item}).wait_recv()
        for r in range(ranks):
            bias_row[0:1, r * piece : (r + 1) * piece] = bias_all[r, 0:1, :].astype(F32)
    else:
        bias_row[0:1, :] = bias_in[0:1, :]
    arrive(normed_takes[0], range(1, groups))

    def spot(mask):
        return pl.multiple_of((group ^ data.shift(mask)[0]) * share, share)

    gives = []
    for s in range(2):

        def read(mask, s=s):
            return sums[pl.ds(s * rows + spot(mask), share), :]

        def write(mask, value, s=s):
            sums[pl.ds(s * rows + spot(mask), share), :] = value

        gives.append(Scatter(data, read, write, s_out.at[s], s_in.at[s], r_send, r_recv, s * groups))

    tile = min(256, units)

    def expand(s):
        at_rows = slice(s * rows, (s + 1) * rows)

        @pl.loop(0, units // tile)
        def _(index):
            at = pl.ds(pl.multiple_of(index * tile, tile), tile)
            value = inner_rows(normed[s], up[at, :]) + bias_row[0:1, at]
            phi = 0.5 * (1.0 + lax.erf(value * 0.7071067811865476))
            active[at_rows, at] = (value * phi).astype(BF)
            slope[at_rows, at] = (phi + value * jnp.exp(-0.5 * value * value) * 0.3989422804014327).astype(BF)

    def reduce(s):
        at_rows = slice(s * rows, (s + 1) * rows)

        @pl.loop(0, width // 256)
        def _(index):
            at = pl.ds(pl.multiple_of(index * 256, 256), 256)
            sums[at_rows, at] = dot(active[at_rows, :], down[:, at])

        for mask in reversed(range(groups // 2, groups)):
            gives[s].put(mask)

    top = len(all_d) - 1
    expand(0)
    arrive(normed_takes[1], range(1, groups))
    expand(1)
    arrive(take_down, range(tall // 2, tall))
    reduce(0)
    arrive(take_qkv, early)
    reduce(1)
    gives[0].level(top)
    out_going(ctx_rows, o_ctx, 11)
    out_going(out_all, o_out, 12)
    out_going(up, o_up, 13)
    out_going(down, o_down, 14)
    out_going(normed, o_normed, 15)
    out_going(slope, o_slope, 16)
    out_going(active, o_active, 17)
    gives[1].level(top)
    wc_copy.wait()

    steps_q, steps_p = score_steps(all_t, all_d)
    lattice_q, lattice_p = Lattice(steps_q), Lattice(steps_p)
    levels_y = [level for level, (axis, _) in enumerate(steps_p) if axis == "dp"]
    count_y = 1 << len(levels_y)

    def spot_q(mask):
        return pl.multiple_of(lattice_q.index(mask) * share, share)

    def spot_p(mask):
        return pl.multiple_of(lattice_p.index(mask) * share, share)

    takes = (
        Gather(lattice_q, lambda m: rows_q.at[pl.ds(spot_q(m), share)], gq_send, gq_recv, own=vec.at[pl.ds(0, share)]),
        Gather(
            lattice_p, lambda m: rows_p.at[pl.ds(spot_p(m), share)], gp_send, gp_recv, own=vec.at[pl.ds(share, share)]
        ),
    )
    for s in range(2):
        at = slice(s * share, (s + 1) * share)
        for level in reversed(range(top)):
            gives[s].level(level)
        feed = gives[s].read(0)
        value, plain, inverse = layer_norm(first[at, :] + feed + offset[1:2, :], gain[1:2, :], shift[1:2, :])
        short = value.astype(BF)
        place = lax.broadcasted_iota(jnp.int32, (share, 1), 0) + rank * share
        chosen = jnp.where(place == 0, value, dot(short, wc[...]) + offset[2:3, :])
        norm = lax.rsqrt(jnp.sum(chosen * chosen, axis=-1, keepdims=True) + 1e-06)
        chosen = chosen * norm
        vec[at, :] = chosen.astype(BF)
        takes[s].start()
        unit[at, :] = chosen
        normal[1, at, :] = plain
        scales[1, at, :] = jnp.broadcast_to(inverse, (share, 128))
        scales[2, at, :] = jnp.broadcast_to(norm, (share, 128))
        low[at, :] = short
    rows_q[pl.ds(spot_q(0), share), :] = vec[0:share, :]
    rows_p[pl.ds(spot_p(0), share), :] = vec[share : 2 * share, :]
    take_q, take_p = takes
    many_q, many_p = lattice_q.count * share, lattice_p.count * share
    half_q, half_p = many_q // 2, many_p // 2
    arrive(take_q, range(1, lattice_q.count // 4))
    arrive(take_p, range(1, lattice_p.count // 2))
    arrive(take_q, [lattice_q.count // 4])
    arrive(take_q, range(lattice_q.count // 4 + 1, lattice_q.count // 2))
    out_going(normal, o_normal, 18)
    out_going(unit, o_unit, 19)
    out_going(low, o_low, 20)
    out_going(scales, o_spread, 21)

    lane = lax.broadcasted_iota(jnp.int32, (1, many_q), 1)
    block_q = lane // share
    group_q = lattice_q.member("dp", block_q)
    place_q = lattice_q.member("tensor", block_q) * share + lane % share
    temper = float(width) ** 0.5
    which_y = [sum(((y >> i) & 1) << level for i, level in enumerate(levels_y)) for y in range(count_y)]
    late_rows, dense_rows = [], []
    for y in range(count_y):
        which = lattice_p.member("dp", which_y[y])
        length, late_row, dense_row = 0, 0.0, 0.0
        for g in range(groups):
            length = jnp.where(group_q == g, len_q[g], length)
            late_row = jnp.where(group_q == g, temper * late_cot[g, which], late_row)
            dense_row = jnp.where(group_q == g, 50.0 * dense_cot[g, which], dense_row)
        late_rows.append(jnp.where((place_q >= 1) & (place_q < length), late_row, 0.0))
        dense_rows.append(jnp.where(place_q == 0, dense_row, 0.0))
    arrive(take_q, range(lattice_q.count // 2, lattice_q.count))
    arrive(take_p, range(lattice_p.count // 2, lattice_p.count))
    arrive(take_qkv, late)

    def place_p(block):
        first_place = lattice_p.member("tensor", block) * share
        return first_place + lax.broadcasted_iota(jnp.int32, (share, 1), 0)

    def part_of(block):
        return sum(((block >> level) & 1) << i for i, level in enumerate(levels_y))

    mass[...] = jnp.zeros_like(mass)
    for block in range(lattice_p.count):
        at = slice(block * share, (block + 1) * share)
        y = part_of(block)
        dots = inner_rows(rows_p[at, :], rows_q[...])
        place = place_p(block)
        counted = (place >= 1) & (place < len_p[lattice_p.member("dp", block)])
        value = jnp.where(counted, jnp.exp(dots * temper - temper), 0.0)
        raised[at, :] = value
        mass[y : y + 1, :] += jnp.sum(value, axis=0, keepdims=True)
    mass_copies = []
    for index, item in enumerate(score_peers(all_t, steps_p)):
        copy = remote(mass, mass_in.at[index], m_send.at[index], m_recv.at[index], {"tensor": rank ^ item})
        copy.start()
        mass_copies.append(copy)
    total = mass[...]
    for index, copy in enumerate(mass_copies):
        copy.wait_recv()
        total = total + mass_in[index]
    for block in range(lattice_p.count):
        at = slice(block * share, (block + 1) * share)
        y = part_of(block)
        value = raised[at, :] * (late_rows[y] / total[y : y + 1, :])
        pull[at, :] = (value + jnp.where(place_p(block) == 0, dense_rows[y], 0.0)).astype(BF)

    mine_q = (lax.axis_index(steps_q[-1][0]) // steps_q[-1][1]) % 2
    mine_p = (lax.axis_index(steps_p[-1][0]) // steps_p[-1][1]) % 2

    def fill_q(half):
        at = pl.ds(pl.multiple_of(half * half_q, half_q), half_q)
        sums[at, :] = outer_rows(pull[:, at], rows_p[...])

    def fill_p(half):
        at = pl.ds(pl.multiple_of(half * half_p, half_p), half_p)
        sum_p[at, :] = dot(pull[at, :], rows_q[...])

    def reader(ref, find):
        return lambda m: ref[pl.ds(find(m), share), :]

    def writer(ref, find):
        def write(m, value):
            ref[pl.ds(find(m), share), :] = value

        return write

    give_q = Scatter(lattice_q, reader(sums, spot_q), writer(sums, spot_q), out_q, in_q, rq_send, rq_recv)
    give_p = Scatter(lattice_p, reader(sum_p, spot_p), writer(sum_p, spot_p), out_p, in_p, rp_send, rp_recv)
    fill_q(1 - mine_q)
    for mask in reversed(range(lattice_q.count // 2, lattice_q.count)):
        give_q.put(mask)
    fill_p(1 - mine_p)
    for mask in reversed(range(lattice_p.count // 2, lattice_p.count)):
        give_p.put(mask)
    fill_q(mine_q)
    arrive(take_qkv, range(tall // 2, tall))
    give_q.level(len(steps_q) - 1)
    fill_p(mine_p)
    give_p.level(len(steps_p) - 1)
    for level in reversed(range(len(steps_q) - 1)):
        give_q.level(level)
    for level in reversed(range(len(steps_p) - 1)):
        give_p.level(level)
    grad[0:share, :] = sums[pl.ds(spot_q(0), share), :]
    grad[share : 2 * share, :] = sum_p[pl.ds(spot_p(0), share), :]
    out_going(grad, o_grad, 22)
    arrive(take_qkv, range(tall, 2 * tall))
    for move in [take_out, take_up, take_down, take_qkv, take_q, take_p, give_q, give_p] + normed_takes + gives:
        move.finish()
    for copy in sends + bias_copies + mass_copies:
        copy.wait_send()
    for copy in pending:
        copy.wait()


def forward(len_q, len_p, dense_cot, late_cot, queries, passages, w_qkv, qv_bias, w_out, up_piece, w_down, qkv_piece,
            bias_in, gain, shift, offset, w_colbert):
    groups, ranks = lax.axis_size("dp"), lax.axis_size("tensor")
    all_t, all_d = steps_of(ranks), steps_of(groups)
    span, width = queries.shape
    columns = w_qkv.shape[2]
    heads = columns // HEAD_DIM
    share = span // ranks
    piece = up_piece.shape[0]
    units = piece * ranks
    rows = groups * share
    ship_bias = bias_in.shape[0] == 16
    steps_q, steps_p = score_steps(all_t, all_d)
    blocks_q, blocks_p = 1 << len(steps_q), 1 << len(steps_p)
    many_q, many_p, peers = blocks_q * share, blocks_p * share, len(score_peers(all_t, steps_p))

    shapes = [
        ((2, span, columns), BF),
        ((2, span, columns), BF),
        ((2, span, columns), BF),
        ((2, heads, span), F32),
        ((ranks, 2 * share, columns), BF),
        ((ranks, columns, width), BF),
        ((units, width), BF),
        ((units, width), BF),
        ((ranks, 3 * columns, width), BF),
        ((2, rows, width), BF),
        ((2 * rows, units), BF),
        ((2 * rows, units), BF),
        ((2, 2 * share, width), F32),
        ((2 * share, width), F32),
        ((2 * share, width), BF),
        ((3, 2 * share, 128), F32),
        ((2 * share, width), F32),
    ]
    dma = pltpu.SemaphoreType.DMA
    vmem = pltpu.VMEM
    hold, leave = pl.BlockSpec(memory_space=pltpu.VMEM), pl.BlockSpec(memory_space=pl.ANY)
    flat = pl.BlockSpec(memory_space=pltpu.SMEM)

    def pair(count):
        return [dma((count,)), dma((count,))]

    return pl.pallas_call(
        functools.partial(forward_kernel, all_t, all_d, ship_bias),
        out_shape=[jax.ShapeDtypeStruct(*item) for item in shapes],
        in_specs=[flat] * 4
        + [leave, leave, hold, hold, leave, leave, leave, hold, hold, hold, hold, hold, leave],
        out_specs=[leave] * len(shapes),
        scratch_shapes=[
            vmem((2, span, width), BF),
            vmem((2, span, columns), BF),
            vmem((2, span, columns), BF),
            vmem((2, span, columns), BF),
            vmem((2, span, columns), BF),
            vmem((2, heads, span), F32),
            vmem((ranks, 2 * share, columns), BF),
            vmem((ranks, columns, width), BF),
            vmem((units, width), BF),
            vmem((units, width), BF),
            vmem((2, rows, width), BF),
            vmem((2 * rows, units), BF),
            vmem((2 * rows, units), BF),
            vmem((2 * rows, width), F32),
            vmem((2, groups - 1, share, width), BF),
            vmem((2, groups - 1, share, width), BF),
            vmem((2 * share, width), F32),
            vmem((2, 2 * share, width), F32),
            vmem((2 * share, width), F32),
            vmem((2 * share, width), BF),
            vmem((2 * share, width), BF),
            vmem((3, 2 * share, 128), F32),
            vmem((width, width), BF),
            vmem((ranks, 16, piece), BF),
            vmem((8, units), F32),
            vmem((many_q, width), BF),
            vmem((many_p, width), BF),
            vmem((many_p, many_q), F32),
            vmem((many_p, many_q), BF),
            vmem((8, many_q), F32),
            vmem((peers, 8, many_q), F32),
            vmem((blocks_q - 1, share, width), BF),
            vmem((blocks_q - 1, share, width), BF),
            vmem((many_p, width), F32),
            vmem((blocks_p - 1, share, width), BF),
            vmem((blocks_p - 1, share, width), BF),
            vmem((2 * share, width), F32),
            dma((23,)),
        ]
        + pair(8 * ranks)
        + pair(2 * ranks)
        + pair(ranks)
        + pair(2 * groups)
        + pair(2 * groups)
        + pair(blocks_q)
        + pair(blocks_p)
        + pair(peers)
        + pair(blocks_q)
        + pair(blocks_p),
        compiler_params=pltpu.CompilerParams(
            collective_id=2, has_side_effects=True, vmem_limit_bytes=62 * 2**20
        ),
        cost_estimate=pl.CostEstimate(flops=10**11, bytes_accessed=40 * 2**20, transcendentals=2**23),
        name="forward",
    )(len_q, len_p, dense_cot, late_cot, queries, passages, w_qkv, qv_bias, w_out, up_piece, w_down, qkv_piece,
      bias_in, gain, shift, offset, w_colbert)


class Settle:
    def __init__(self, lattice, view, came, send, recv, base=0):
        self.lattice, self.view, self.came = lattice, view, came
        self.send, self.recv, self.base = send, recv, base
        self.sent = []

    def copy(self, mask):
        return remote(
            self.view(mask),
            self.came.at[mask - 1],
            self.send.at[self.base + mask],
            self.recv.at[self.base + mask],
            self.lattice.peer(mask.bit_length() - 1),
        )

    def push(self, mask):
        copy = self.copy(mask)
        copy.start()
        self.sent.append(copy)

    def start(self):
        for mask in reversed(range(self.lattice.count // 2, self.lattice.count)):
            self.push(mask)

    def level(self, level):
        for mask in reversed(range(1 << level)):
            slot = (1 << level) + mask
            self.copy(slot).wait_recv()
            place = self.view(mask)
            place[...] = (place[...].astype(F32) + self.came[slot - 1].astype(F32)).astype(BF)
            if mask and mask >= 1 << (level - 1):
                self.push(mask)

    def finish(self):
        for copy in self.sent:
            copy.wait_send()


def backward_kernel(
    all_t, all_d,
    len_q, len_p, grad_vec, h_unit, h_low, h_scales, h_normals, h_wc, h_down, h_up, h_slope, h_active, h_normed,
    h_out, h_ctx, h_q, h_k, h_v, h_lse, x_q, x_p, h_qkv, gain,
    o_tokens, o_down, o_up, o_out, o_wc, o_qkv, o_small,
    pool, slope, active, out_all, wc, ctx_rows, q, k, v, lse, g1, unit, low, proj, normals, scales, sums,
    s_out, s_in, turn, ctx_out, heads_grad, turned, turned_rows, dk_sum, dv_sum,
    g_down, g_down_in, g_up, g_up_in, g_out_in, g_wc_in, qkv_sum, qkv_low, qkv_in,
    small, small_in, stage, stage_in,
    local, n_send, n_recv, r_send, r_recv, d_send, d_recv, u_send, u_recv, w_send, w_recv, c_send, c_recv,
    a_send, a_recv, t_send, t_recv, f_send, f_recv, m_send, m_recv, y_send, y_recv, q_send, q_recv,
):
    group, rank = lax.axis_index("dp"), lax.axis_index("tensor")
    ranks, groups = 1 << len(all_t), 1 << len(all_d)
    far_d = all_d[:-1]
    span, width = x_q.shape
    columns = q.shape[2]
    share = span // ranks
    units = h_up.shape[0]
    piece = units // ranks
    quarter = columns // 4
    rows = groups * share
    heads = columns // HEAD_DIM
    scale = HEAD_DIM**-0.5
    flat = width // ranks // 4
    at_up, at_down = pl.ds(0, units), pl.ds(units, units)
    at_normed, at_feed = pl.ds(2 * units, 2 * rows), pl.ds(2 * units + 2 * rows, 2 * rows)
    feed_at = 2 * units + 2 * rows

    loads = []

    def load(src, dst):
        copy = pltpu.make_async_copy(src, dst, local.at[len(loads)])
        copy.start()
        loads.append(copy)
        return copy

    early = [load(grad_vec, g1), load(h_unit, unit), load(h_scales, scales), load(h_low, low), load(h_wc, wc)]
    early.append(load(h_normals, normals))
    ffn = [load(h_down, pool.at[at_down]), load(h_slope, slope), load(h_up, pool.at[at_up])]
    later = [load(h_active, active), load(h_normed, pool.at[at_normed])]
    last = [load(h_out, out_all), load(h_ctx, ctx_rows)]
    heads_in = [load(h_q, q), load(h_k, k), load(h_v, v), load(h_lse, lse)]
    greet([{"tensor": rank ^ item} for item in range(1, ranks)] + [{"dp": group ^ item} for item in all_d])

    tensor = Lattice([("tensor", step) for step in all_t])
    quad = Lattice([("tensor", step) for step in all_t] + [("dp", step) for step in all_d[-2:]])
    data = Lattice([("dp", step) for step in all_d])

    def quarters(ref, size, lattice=quad):
        def view(mask):
            d, t = lattice.shift(mask)
            return ref.at[pl.ds(pl.multiple_of(((rank ^ t) * 4 + (group ^ d) % 4) * size, size), size)]

        return view

    cross = Lattice(tensor.steps[:-2] + [tensor.steps[-1], tensor.steps[-2]])

    def pieces(ref, lattice):
        return lambda mask: ref.at[pl.ds(pl.multiple_of((rank ^ lattice.shift(mask)[1]) * piece, piece), piece)]

    def spot(mask):
        return pl.multiple_of((group ^ data.shift(mask)[0]) * share, share)

    flow = Lattice([("dp", all_d[-2])] + tensor.steps + [("dp", all_d[-1])])
    give_wc = Settle(flow, quarters(wc, flat, flow), g_wc_in, c_send, c_recv)
    give_out = Settle(quad, quarters(out_all, quarter), g_out_in, w_send, w_recv)
    give_down = Settle(tensor, pieces(g_down, tensor), g_down_in, d_send, d_recv)
    give_up = Settle(cross, pieces(g_up, cross), g_up_in, u_send, u_recv)

    small[...] = jnp.zeros_like(small)
    for copy in early:
        copy.wait()
    takes = []
    for s in range(2):
        at = slice(s * share, (s + 1) * share)
        grad, plain = g1[at, :], unit[at, :]
        chosen = scales[2, at, 0:1] * (grad - plain * jnp.sum(grad * plain, axis=-1, keepdims=True))
        leading = lax.broadcasted_iota(jnp.int32, (share, 1), 0) + rank * share == 0
        short = jnp.where(leading, 0.0, chosen).astype(BF)
        proj[at, :] = short
        grad = jnp.where(leading, chosen, 0.0) + inner_rows(short, wc[...])
        middle, gains, shifts = norm_back(grad, normals[1, at, :], scales[1, at, 0:1], gain[1:2, :])
        g1[at, :] = middle
        small[0, 1:2, :] += gains[None, :]
        small[0, 3:4, :] += shifts[None, :]
        small[0, 5:6, :] += jnp.sum(middle, axis=0, keepdims=True)
        small[0, 6:7, :] += jnp.sum(short.astype(F32), axis=0, keepdims=True)
        own = pl.multiple_of(feed_at + s * rows + group * share, share)
        pool[pl.ds(own, share), :] = middle.astype(BF)

        def view(mask, s=s):
            place = feed_at + s * rows + (group ^ data.shift(mask)[0]) * share
            return pool.at[pl.ds(pl.multiple_of(place, share), share)]

        taking = Gather(data, view, n_send, n_recv, s * groups)
        taking.start()
        takes.append(taking)

    @pl.loop(0, width // 256)
    def _(index):
        at = pl.ds(pl.multiple_of(index * 256, 256), 256)
        wc[at, :] = outer_rows(low[:, at], proj[...]).astype(BF)

    give_wc.start()

    gives = []
    for s in range(2):

        def read(mask, s=s):
            return sums[s, pl.ds(spot(mask), share), :]

        def write(mask, value, s=s):
            sums[s, pl.ds(spot(mask), share), :] = value

        gives.append(Scatter(data, read, write, s_out.at[s], s_in.at[s], r_send, r_recv, s * groups))
    for copy in ffn:
        copy.wait()
    tile = min(256, units)

    def shrink(s):
        at_rows = slice(s * rows, (s + 1) * rows)
        feed_rows = slice(feed_at + s * rows, feed_at + (s + 1) * rows)

        @pl.loop(0, units // tile)
        def _(index):
            at = pl.ds(pl.multiple_of(index * tile, tile), tile)
            down_at = pl.ds(pl.multiple_of(units + index * tile, tile), tile)
            value = inner_rows(pool[feed_rows, :], pool[down_at, :]) * slope[at_rows, at].astype(F32)
            value = value.astype(BF)
            slope[at_rows, at] = value
            small[0, 7:8, at] += jnp.sum(value.astype(F32), axis=0, keepdims=True)

        @pl.loop(0, width // 256)
        def _(index):
            at = pl.ds(pl.multiple_of(index * 256, 256), 256)
            sums[s, :, at] = dot(slope[at_rows, :], pool[at_up, at])

    def put(s):
        for mask in reversed(range(groups // 2, groups)):
            gives[s].put(mask)

    top = len(all_d) - 1
    last_t = len(all_t) - 1
    quad_top = len(all_t) + 1
    blocks = list(reversed(range(ranks // 2, ranks)))
    give_wc.level(quad_top)
    for mask in range(1, groups):
        takes[0].arrive(mask)
    shrink(0)
    put(0)
    for copy in later:
        copy.wait()
    for mask in range(1, groups):
        takes[1].arrive(mask)
    gives[0].level(top)

    @pl.loop(0, units // tile)
    def _(index):
        at = pl.ds(pl.multiple_of(index * tile, tile), tile)
        g_down[at, :] = outer_rows(active[:, at], pool[at_feed, :]).astype(BF)

    for mask in blocks[:2]:
        give_down.push(mask)
    give_wc.level(last_t + 1)
    shrink(1)
    put(1)

    @pl.loop(0, units // tile)
    def _(index):
        at = pl.ds(pl.multiple_of(index * tile, tile), tile)
        g_up[at, :] = outer_rows(slope[:, at], pool[at_normed, :]).astype(BF)

    gives[1].level(top)
    for mask in blocks[:1]:
        give_up.push(mask)

    for copy in last:
        copy.wait()
    def small_step(level):
        copy = remote(
            small.at[level], small_in.at[level], m_send.at[level], m_recv.at[level], {"tensor": rank ^ all_t[level]}
        )
        return copy

    small_copies = [small_step(level) for level in range(len(all_t))]

    def small_next(level):
        small_copies[level].wait_recv()
        small[level + 1] = small[level] + small_in[level]
        if level + 1 < len(all_t):
            small_copies[level + 1].start()

    sends = []
    for s in range(2):
        at = slice(s * share, (s + 1) * share)
        for level in reversed(range(top)):
            gives[s].level(level)
        grad = g1[at, :] + gives[s].read(0)
        hidden, gains, shifts = norm_back(grad, normals[0, at, :], scales[0, at, 0:1], gain[0:1, :])
        g1[at, :] = hidden
        small[0, 0:1, :] += gains[None, :]
        small[0, 2:3, :] += shifts[None, :]
        small[0, 4:5, :] += jnp.sum(hidden, axis=0, keepdims=True)
        short = hidden.astype(BF)
        turn[at, :] = short
        if columns % 128 == 0:
            value = inner_rows(short, out_all[...]).astype(BF)
            for r in range(ranks):
                ctx_out[r, at, :] = value[:, r * columns : (r + 1) * columns]
        else:
            for r in range(ranks):
                ctx_out[r, at, :] = inner_rows(short, out_all[r * columns : (r + 1) * columns, :]).astype(BF)
        mine = pl.ds(pl.multiple_of(rank * share, share), share)
        for item in range(1, ranks):
            copy = remote(
                ctx_out.at[rank ^ item, pl.ds(s * share, share)],
                heads_grad.at[s, mine],
                a_send.at[s * ranks + item],
                a_recv.at[s * ranks + item],
                {"tensor": rank ^ item},
            )
            copy.start()
            sends.append(copy)
        heads_grad[s, mine, :] = ctx_out[rank, at, :]
        if s == 1:
            for mask in blocks[1:2]:
                give_up.push(mask)
            small_copies[0].start()
    for taking in takes:
        taking.finish()
    tall = load(x_q, pool.at[pl.ds(0, span)]), load(x_p, pool.at[pl.ds(span, span)])
    at_qkv = 2 * span
    pairs = Lattice([("dp", step) for step in all_d[-2:]])
    back_in = load(h_qkv, pool.at[pl.ds(at_qkv, 3 * columns * ranks)])

    for r in range(ranks):
        out_all[r * columns : (r + 1) * columns, :] = outer_rows(ctx_rows[r], turn[...]).astype(BF)
    give_wc.level(last_t)
    give_out.start()

    block = min(BLOCK, span)

    lengths = (len_q[group], len_p[group])

    def attention(s, begin, end):
        keep = lax.broadcasted_iota(jnp.int32, (span, 1), 0) < lengths[s]

        @pl.loop(begin, end)
        def _(index):
            at = pl.ds(pl.multiple_of(index * block, block), block)
            query = q[s, at, :]
            grad = heads_grad[s, at, :]
            total = jnp.zeros((block, columns), F32)
            for head in range(heads):
                mask = head_mask(columns, head)
                mine = jnp.where(mask, query, jnp.zeros_like(query)) * jnp.asarray(scale, BF)
                back = jnp.where(mask, grad, jnp.zeros_like(grad))
                scores = jnp.where(keep, inner_rows(k[s], mine), -1e30)
                probs = jnp.exp(scores - lse[s, head : head + 1, at])
                slant = inner_rows(v[s], back)
                middle = jnp.sum(probs * slant, axis=0, keepdims=True)
                twist = (probs * (slant - middle)).astype(BF)
                dv_sum[...] += dot(probs.astype(BF), back)
                dk_sum[...] += dot(twist, mine)
                part = outer_rows(twist, k[s]) * scale
                total = jnp.where(mask, part, total)
            turned[s, at, 0:columns] = total.astype(BF)

    def attention_start(s):
        for item in range(1, ranks):
            place = heads_grad.at[s, pl.ds(pl.multiple_of((rank ^ item) * share, share), share)]
            remote(
                place, place, a_send.at[s * ranks + item], a_recv.at[s * ranks + item], {"tensor": rank ^ item}
            ).wait_recv()
        dk_sum[...] = jnp.zeros_like(dk_sum)
        dv_sum[...] = jnp.zeros_like(dv_sum)

    def attention_end(s):
        turned[s, :, columns : 2 * columns] = dk_sum[...].astype(BF)
        turned[s, :, 2 * columns : 3 * columns] = dv_sum[...].astype(BF)
        for item in range(1, ranks):
            copy = remote(
                turned.at[s, pl.ds(pl.multiple_of((rank ^ item) * share, share), share)],
                turned_rows.at[rank, pl.ds(s * share, share)],
                t_send.at[s * ranks + item],
                t_recv.at[s * ranks + item],
                {"tensor": rank ^ item},
            )
            copy.start()
            sends.append(copy)
        turned_rows[rank, s * share : (s + 1) * share, :] = turned[
            s, pl.ds(pl.multiple_of(rank * share, share), share), :
        ]

    many = qkv_sum.shape[1]

    def qkv_grad(s):
        tokens = pool[s * span : (s + 1) * span, :]
        for i in range(3):
            part = turned[s, :, i * columns : (i + 1) * columns]
            whole = outer_rows(tokens, part)
            line = jnp.broadcast_to(jnp.sum(part.astype(F32), axis=0, keepdims=True), (many - width, columns))
            if s == 0:
                qkv_sum[i, 0:width, :] = whole
                qkv_sum[i, width:many, :] = line
            else:
                qkv_sum[i, 0:width, :] += whole
                qkv_sum[i, width:many, :] += line

    for copy in heads_in:
        copy.wait()
    count = span // block
    attention_start(0)
    attention(0, 0, count // 2)
    for mask in blocks[2:]:
        give_down.push(mask)
    for level in reversed(range(1, last_t)):
        give_wc.level(level)
    small_next(0)
    give_wc.level(0)
    for mask in blocks[2:]:
        give_up.push(mask)
    attention(0, count // 2, count)
    attention_end(0)
    for copy in tall:
        copy.wait()
    qkv_grad(0)
    attention_start(1)
    for level in range(1, len(all_t)):
        small_next(level)
    attention(1, 0, count // 2)
    small_own = small.at[len(all_t)]
    small_take = Gather(data, lambda m: o_small.at[group ^ data.shift(m)[0]], f_send, f_recv, 0, own=small_own)
    small_take.start()
    small_copy = load(small_own, o_small.at[group])
    give_up.level(last_t)
    attention(1, count // 2, count)
    attention_end(1)
    give_out.level(quad_top)

    rest = all_d[:-2]

    def settle_stage(which, source, size):
        base = which * max(1, len(rest))
        copies = []
        for index, step in enumerate(rest):
            src = source if index == 0 else stage.at[base + index - 1, pl.ds(0, size)]
            dst = stage_in.at[base + index, pl.ds(0, size)]
            copies.append(remote(src, dst, y_send.at[base + index], y_recv.at[base + index], {"dp": group ^ step}))
        for index, copy in enumerate(copies):
            copy.start()
            copy.wait_recv()
            before = source[...] if index == 0 else stage[base + index - 1, 0:size, :]
            value = before.astype(F32) + stage_in[base + index, 0:size, :].astype(F32)
            stage[base + index, 0:size, :] = value.astype(BF)
        return (stage.at[base + len(rest) - 1, pl.ds(0, size)] if rest else source), copies

    def dp_view(ref):
        return lambda m: ref.at[pl.ds(pl.multiple_of((group ^ data.shift(m)[0]) * piece, piece), piece)]

    def out_view(mask):
        d, _ = pairs.shift(mask)
        return o_out.at[pl.ds(pl.multiple_of(((group ^ d) % 4) * quarter, quarter), quarter)]

    out_base = 2 * groups + quad.count

    def rows_end(s):
        at = slice(s * share, (s + 1) * share)
        for item in range(1, ranks):
            place = turned_rows.at[rank ^ item, pl.ds(s * share, share)]
            remote(
                place, place, t_send.at[s * ranks + item], t_recv.at[s * ranks + item], {"tensor": rank ^ item}
            ).wait_recv()
        total = g1[at, :]
        for r in range(ranks):
            begin = at_qkv + r * 3 * columns
            total = total + dot(turned_rows[r, at, :], pool[begin : begin + 3 * columns, :])
        unit[at, :] = total

    back_in.wait()
    rows_end(0)
    give_up.level(last_t - 1)
    give_down.level(last_t)
    qkv_grad(1)

    part = many // 2
    at_mine = pl.ds(pl.multiple_of((group % 2) * part, part), part)
    at_other = pl.ds(pl.multiple_of((1 - group % 2) * part, part), part)
    near = {"dp": group ^ all_d[-1]}
    qkv_low[0] = qkv_sum[:, at_other, :].astype(BF)
    qkv_copies = [remote(qkv_low.at[0], qkv_in.at[0], q_send.at[0], q_recv.at[0], near)]
    qkv_copies[0].start()
    for index, step in enumerate(far_d):
        slot = 1 + index
        qkv_copies.append(
            remote(qkv_low.at[slot], qkv_in.at[slot], q_send.at[slot], q_recv.at[slot], {"dp": group ^ step})
        )
    qkv_last = len(far_d) + 1
    qkv_own = qkv_low.at[qkv_last]
    qkv_copies.append(remote(qkv_own, o_qkv.at[:, at_mine], q_send.at[qkv_last], q_recv.at[qkv_last], near))

    wc_own, wc_copies = settle_stage(0, give_wc.view(0), flat)
    wc_take = Gather(quad, quarters(o_wc, flat), f_send, f_recv, groups, own=wc_own)
    wc_take.start()
    wc_copy = load(wc_own, wc_take.view(0))
    qkv_copies[0].wait_recv()
    sum_half = qkv_sum[:, at_mine, :].astype(BF).astype(F32) + qkv_in[0].astype(F32)
    qkv_low[1] = sum_half.astype(BF)
    qkv_copies[1].start()
    for level in reversed(range(last_t - 1)):
        give_up.level(level)
    up_own = give_up.view(0)
    up_take = Gather(data, dp_view(o_up), f_send, f_recv, out_base + 4, own=up_own)
    up_take.start()
    up_copy = load(up_own, up_take.view(0))
    give_out.level(quad_top - 1)
    for mask in range(1, ranks // 2):
        wc_take.arrive(mask)
    give_down.level(last_t - 1)
    give_out.level(last_t)
    for index in range(len(far_d)):
        qkv_copies[1 + index].wait_recv()
        qkv_low[2 + index] = (qkv_low[1 + index].astype(F32) + qkv_in[1 + index].astype(F32)).astype(BF)
        qkv_copies[index + 2].start()
    qkv_local = load(qkv_own, o_qkv.at[:, at_mine])
    for mask in range(ranks // 2, quad.count):
        wc_take.arrive(mask)
    for level in reversed(range(last_t - 1)):
        give_down.level(level)
    down_own = give_down.view(0)
    down_take = Gather(data, dp_view(o_down), f_send, f_recv, groups + quad.count, own=down_own)
    down_take.start()
    down_copy = load(down_own, down_take.view(0))
    give_out.level(last_t - 1)
    rows_end(1)
    tokens_copy = load(unit, o_tokens)
    for level in reversed(range(last_t - 1)):
        give_out.level(level)
    out_own, out_copies = settle_stage(1, give_out.view(0), quarter)
    out_take = Gather(pairs, out_view, f_send, f_recv, out_base, own=out_own)
    out_take.start()
    out_copy = load(out_own, out_view(0))
    for taking in (small_take, down_take, up_take):
        for mask in range(1, groups):
            taking.arrive(mask)
    for mask in range(1, 4):
        out_take.arrive(mask)
    at_theirs = o_qkv.at[:, at_other]
    remote(at_theirs, at_theirs, q_send.at[qkv_last], q_recv.at[qkv_last], near).wait_recv()
    for move in [give_wc, give_out, give_down, give_up, small_take, wc_take, down_take, up_take, out_take] + gives:
        move.finish()
    for copy in sends + small_copies + qkv_copies + wc_copies + out_copies:
        copy.wait_send()
    for copy in (tokens_copy, small_copy, wc_copy, down_copy, qkv_local, out_copy, up_copy):
        copy.wait()


def backward(len_q, len_p, grad_vec, unit, low, scales, normals, w_colbert, down, up, slope, active, normed, out_all,
             context_rows, query, key, value, lse, queries, passages, qkv_all, gain):
    groups, ranks = lax.axis_size("dp"), lax.axis_size("tensor")
    all_t, all_d = steps_of(ranks), steps_of(groups)
    span, width = queries.shape
    columns = query.shape[2]
    heads = columns // HEAD_DIM
    share = span // ranks
    units = up.shape[0]
    piece = units // ranks
    rows = groups * share
    quarter, flat = columns // 4, width // ranks // 4
    pool = max(2 * units + 4 * rows, 2 * span + 3 * columns * ranks)
    many = width + 32
    far = len(all_d) - 1
    dma = pltpu.SemaphoreType.DMA
    vmem = pltpu.VMEM
    hold, leave = pl.BlockSpec(memory_space=pltpu.VMEM), pl.BlockSpec(memory_space=pl.ANY)
    shapes = [
        ((2 * share, width), F32),
        ((units // ranks * groups, width), BF),
        ((units // ranks * groups, width), BF),
        ((columns, width), BF),
        ((width, width), BF),
        ((3, many, columns), BF),
        ((groups, 8, width), F32),
    ]
    smem = pl.BlockSpec(memory_space=pltpu.SMEM)
    rest = max(1, len(all_d) - 2)

    def pair(count):
        return [dma((count,)), dma((count,))]

    return pl.pallas_call(
        functools.partial(backward_kernel, all_t, all_d),
        out_shape=[jax.ShapeDtypeStruct(*item) for item in shapes],
        in_specs=[smem, smem] + [leave] * 20 + [hold],
        out_specs=[leave] * len(shapes),
        scratch_shapes=[
            vmem((pool, width), BF),
            vmem((2 * rows, units), BF),
            vmem((2 * rows, units), BF),
            vmem((ranks * columns, width), BF),
            vmem((width, width), BF),
            vmem((ranks, 2 * share, columns), BF),
            vmem((2, span, columns), BF),
            vmem((2, span, columns), BF),
            vmem((2, span, columns), BF),
            vmem((2, heads, span), F32),
            vmem((2 * share, width), F32),
            vmem((2 * share, width), F32),
            vmem((2 * share, width), BF),
            vmem((2 * share, width), BF),
            vmem((2, 2 * share, width), F32),
            vmem((3, 2 * share, 128), F32),
            vmem((2, rows, width), F32),
            vmem((2, groups - 1, share, width), BF),
            vmem((2, groups - 1, share, width), BF),
            vmem((2 * share, width), BF),
            vmem((ranks, 2 * share, columns), BF),
            vmem((2, span, columns), BF),
            vmem((2, span, 3 * columns), BF),
            vmem((ranks, 2 * share, 3 * columns), BF),
            vmem((span, columns), F32),
            vmem((span, columns), F32),
            vmem((units, width), BF),
            vmem((ranks - 1, piece, width), BF),
            vmem((units, width), BF),
            vmem((ranks - 1, piece, width), BF),
            vmem((4 * ranks - 1, quarter, width), BF),
            vmem((4 * ranks - 1, flat, width), BF),
            vmem((3, many, columns), F32),
            vmem((2 + far, 3, many // 2, columns), BF),
            vmem((1 + far, 3, many // 2, columns), BF),
            vmem((len(all_t) + 1, 8, width), F32),
            vmem((len(all_t), 8, width), F32),
            vmem((2 * rest, max(quarter, flat), width), BF),
            vmem((2 * rest, max(quarter, flat), width), BF),
            dma((32,)),
        ]
        + pair(2 * groups)
        + pair(2 * groups)
        + pair(ranks)
        + pair(ranks)
        + pair(4 * ranks)
        + pair(4 * ranks)
        + pair(2 * ranks)
        + pair(2 * ranks)
        + pair(3 * groups + 4 * ranks + 4)
        + pair(len(all_t))
        + pair(2 * rest)
        + pair(2 + far),
        compiler_params=pltpu.CompilerParams(
            collective_id=3, has_side_effects=True, vmem_limit_bytes=62 * 2**20
        ),
        cost_estimate=pl.CostEstimate(flops=10**11, bytes_accessed=40 * 2**20, transcendentals=2**22),
        name="backward",
    )(len_q, len_p, grad_vec, unit, low, scales, normals, w_colbert, down, up, slope, active, normed, out_all,
      context_rows, query, key, value, lse, queries, passages, qkv_all, gain)


def finish_kernel(
    rank_of, low, tokens, down, up, out, wc, qkv, small,
    out_q, out_p, tok_q, tok_p, g_qkv, g_bias, g_out, g_up, g_in, g_down, g_gain, g_shift, g_offset, g_wc,
    v_low, v_tokens, v_down, v_up, v_out, v_wc, v_qkv, f_down, f_up, f_out, f_wc, f_qkv, load, store,
):
    share, width = out_q.shape
    copies = []

    def begin(src, dst, sem):
        copy = pltpu.make_async_copy(src, dst, sem)
        copy.start()
        return copy

    loads = [
        begin(src, dst, load.at[index])
        for index, (src, dst) in enumerate(
            ((down, v_down), (up, v_up), (wc, v_wc), (qkv, v_qkv), (out, v_out), (low, v_low), (tokens, v_tokens))
        )
    ]
    loads[0].wait()
    f_down[...] = v_down[...].astype(F32)
    copies.append(begin(f_down, g_down, store.at[4]))
    loads[1].wait()
    f_up[...] = v_up[...].astype(F32).T
    copies.append(begin(f_up, g_up, store.at[5]))
    loads[2].wait()
    f_wc[...] = v_wc[...].astype(F32)
    copies.append(begin(f_wc, g_wc, store.at[6]))
    loads[3].wait()
    f_qkv[...] = v_qkv[:, 0:width, :].astype(F32)
    copies.append(begin(f_qkv, g_qkv, store.at[7]))
    g_bias[0:1, :] = v_qkv[0, width : width + 16, :].astype(F32)[0:1, :]
    g_bias[1:2, :] = v_qkv[2, width : width + 16, :].astype(F32)[0:1, :]
    loads[4].wait()
    f_out[...] = v_out[...].astype(F32)
    copies.append(begin(f_out, g_out, store.at[8]))
    groups = small.shape[0]
    total = small[0]
    for index in range(1, groups):
        total = total + small[index]
    g_gain[...] = total[0:2]
    g_shift[...] = total[2:4]
    g_offset[...] = total[4:7]
    piece = g_in.shape[1]
    for index in range(groups):
        if piece % 128 == 0:
            at = pl.ds(pl.multiple_of(rank_of[0] * piece, piece), piece)
            g_in[index : index + 1, :] = small[index, 7:8, at]
    loads[5].wait()
    copies.append(begin(v_low.at[pl.ds(0, share)], out_q, store.at[0]))
    copies.append(begin(v_low.at[pl.ds(share, share)], out_p, store.at[1]))
    loads[6].wait()
    copies.append(begin(v_tokens.at[pl.ds(0, share)], tok_q, store.at[2]))
    copies.append(begin(v_tokens.at[pl.ds(share, share)], tok_p, store.at[3]))
    for copy in copies:
        copy.wait()


def finish(low, tokens, down, up, out, wc, qkv, small, piece):
    share, width = low.shape[0] // 2, low.shape[1]
    hidden, columns = down.shape[0], out.shape[0]
    groups = small.shape[0]
    hold, leave = pl.BlockSpec(memory_space=pltpu.VMEM), pl.BlockSpec(memory_space=pl.ANY)
    rank_of = lax.axis_index("tensor").reshape(1).astype(jnp.int32)
    shapes = [
        ((share, width), BF),
        ((share, width), BF),
        ((share, width), F32),
        ((share, width), F32),
        ((3, width, columns), F32),
        ((2, columns), F32),
        ((columns, width), F32),
        ((width, hidden), F32),
        ((groups, piece), F32),
        ((hidden, width), F32),
        ((2, width), F32),
        ((2, width), F32),
        ((3, width), F32),
        ((width, width), F32),
    ]
    vmem, dma = pltpu.VMEM, pltpu.SemaphoreType.DMA
    return pl.pallas_call(
        finish_kernel,
        out_shape=[jax.ShapeDtypeStruct(*item) for item in shapes],
        in_specs=[pl.BlockSpec(memory_space=pltpu.SMEM)] + [leave] * 7 + [hold],
        out_specs=[leave] * 5 + [hold, leave, leave, hold, leave, hold, hold, hold, leave],
        scratch_shapes=[
            vmem(low.shape, BF),
            vmem(tokens.shape, F32),
            vmem(down.shape, BF),
            vmem(up.shape, BF),
            vmem(out.shape, BF),
            vmem(wc.shape, BF),
            vmem(qkv.shape, BF),
            vmem(down.shape, F32),
            vmem((width, hidden), F32),
            vmem(out.shape, F32),
            vmem(wc.shape, F32),
            vmem((3, width, columns), F32),
            dma((7,)),
            dma((9,)),
        ],
        compiler_params=pltpu.CompilerParams(vmem_limit_bytes=62 * 2**20),
        name="finish",
    )(rank_of, low, tokens, down, up, out, wc, qkv, small)


def per_device(
    queries,
    passages,
    query_lengths,
    passage_lengths,
    w_qkv,
    qv_bias,
    w_out,
    w_in,
    in_bias,
    w_down,
    norm_gain,
    norm_shift,
    layer_bias,
    w_colbert,
    dense_cot,
    colbert_cot,
):
    groups, ranks = lax.axis_size("dp"), lax.axis_size("tensor")
    group, rank = lax.axis_index("dp"), lax.axis_index("tensor")
    width = queries.shape[1]
    columns = w_qkv.shape[2]
    piece = w_in.shape[1] // groups
    units = piece * ranks

    up_piece = lax.dynamic_slice_in_dim(w_in, group * piece, piece, 1).T
    slim = 3 * columns // 2
    turned = w_qkv.transpose(0, 2, 1).reshape(3 * columns, width)
    qkv_piece = lax.dynamic_slice_in_dim(turned, (group % 2) * slim, slim, 0)
    if piece % 128 == 0:
        bias_in = lax.dynamic_slice_in_dim(in_bias, group * piece, piece, 0)
        bias_in = jnp.broadcast_to(bias_in[None, :], (16, piece))
    else:
        bias_in = lax.all_gather(in_bias, "tensor").reshape(ranks, groups, piece)
        bias_in = lax.dynamic_index_in_dim(bias_in, group, 1, keepdims=False).reshape(1, -1).astype(F32)
    (
        query,
        key,
        value,
        lse,
        context_rows,
        out_all,
        up,
        down,
        qkv_all,
        normed,
        slope,
        active,
        normals,
        unit,
        low,
        scales,
        grad_vec,
    ) = forward(
        query_lengths, passage_lengths, dense_cot, colbert_cot, queries, passages, w_qkv, qv_bias, w_out, up_piece,
        w_down, qkv_piece, bias_in, norm_gain, norm_shift, layer_bias, w_colbert,
    )
    tokens, grad_down, grad_up, grad_out, colbert, grad_qkv, small = backward(
        query_lengths, passage_lengths, grad_vec, unit, low, scales, normals, w_colbert, down, up, slope, active,
        normed.reshape(-1, width), out_all.reshape(-1, width), context_rows, query, key, value, lse,
        queries, passages, qkv_all.reshape(-1, width), norm_gain,
    )
    results = list(finish(low, tokens, grad_down, grad_up, grad_out, colbert, grad_qkv, small, piece))
    if piece % 128:
        bias = small[:, 7, :units].reshape(groups, ranks, piece)
        results[8] = lax.dynamic_index_in_dim(bias, rank, 1, keepdims=False)
    results[8] = results[8].reshape(-1)
    return tuple(results)


def solution(mesh):
    both = P(("dp", "tensor"), None)
    return jax.shard_map(
        per_device,
        mesh=mesh,
        in_specs=(
            P("dp", None),
            P("dp", None),
            P(),
            P(),
            P(None, None, "tensor"),
            P(None, "tensor"),
            P("tensor", None),
            P(None, "tensor"),
            P("tensor"),
            P("tensor", None),
            P(),
            P(),
            P(),
            P(),
            P(),
            P(),
        ),
        out_specs=(
            both,
            both,
            both,
            both,
            P(None, None, "tensor"),
            P(None, "tensor"),
            P("tensor", None),
            P(None, "tensor"),
            P("tensor"),
            P("tensor", None),
            P(),
            P(),
            P(),
            P(),
        ),
        check_vma=False,
    )
```

```python
import functools

import jax
import jax.numpy as jnp
from jax import lax
from jax.experimental import pallas as pl
from jax.experimental.pallas import tpu as pltpu
from jax.sharding import PartitionSpec as P

HEAD_DIM = 64
BF = jnp.bfloat16
F32 = jnp.float32
BLOCK = 256


def dot(left, right):
    return jnp.dot(left, right, preferred_element_type=F32)


def inner_rows(left, right):
    return lax.dot_general(left, right, (((1,), (1,)), ((), ())), preferred_element_type=F32)


def outer_rows(left, right):
    return lax.dot_general(left, right, (((0,), (0,)), ((), ())), preferred_element_type=F32)


def steps_of(size):
    steps = []
    while size > 1:
        size //= 2
        steps.append(size)
    return steps


def offsets(steps):
    found = [0]
    for step in steps:
        found = found + [item ^ step for item in found]
    return found


def swap(value, axis, step):
    size = lax.axis_size(axis)
    return lax.ppermute(value, axis, [(index, index ^ step) for index in range(size)])


def spread(value, axis, steps):
    held = value[None]
    for step in steps:
        held = jnp.concatenate([held, swap(held, axis, step)], axis=0)
    return held


def fold(parts, axis, steps):
    for step in reversed(steps):
        half = parts.shape[0] // 2
        came = swap(parts[half:].astype(BF), axis, step)
        parts = parts[:half].astype(F32) + came.astype(F32)
    return parts[0]


def natural(parts, axis, steps, dim=0):
    order = offsets(steps)
    size = len(order)
    place = [0] * size
    for spot, item in enumerate(order):
        place[item] = spot
    table = jnp.array(place, jnp.int32)
    rank = lax.axis_index(axis)
    return jnp.concatenate(
        [lax.dynamic_slice_in_dim(parts, table[item ^ rank], 1, dim) for item in range(size)], axis=dim
    )


def xored(parts, axis, steps, dim=0):
    rank = lax.axis_index(axis)
    return jnp.concatenate(
        [lax.dynamic_slice_in_dim(parts, item ^ rank, 1, dim) for item in offsets(steps)], axis=dim
    )


def trade(parts, steps, dim):
    rank = lax.axis_index("tensor")
    got = []
    for item in offsets(steps):
        piece = lax.dynamic_index_in_dim(parts, item ^ rank, dim, keepdims=False)
        got.append(swap(piece, "tensor", item) if item else piece)
    return got


def layer_norm(hidden, gain, shift):
    centre = hidden - jnp.mean(hidden, axis=-1, keepdims=True)
    inverse = lax.rsqrt(jnp.mean(centre * centre, axis=-1, keepdims=True) + 1e-05)
    normal = centre * inverse
    return (normal * gain + shift, normal, inverse)


def norm_back(grad, normal, inverse, gain):
    scaled = grad * gain
    middle = (
        scaled
        - jnp.mean(scaled, axis=-1, keepdims=True)
        - normal * jnp.mean(scaled * normal, axis=-1, keepdims=True)
    )
    return (middle * inverse, jnp.sum(grad * normal, axis=0), jnp.sum(grad, axis=0))


def gelu_slope(inner):
    return (
        0.5 * (1.0 + lax.erf(inner * 0.7071067811865476))
        + inner * jnp.exp(-0.5 * inner * inner) * 0.3989422804014327
    )


def head_mask(columns, head):
    lane = lax.broadcasted_iota(jnp.int32, (1, columns), 1)
    return (lane >= head * HEAD_DIM) & (lane < (head + 1) * HEAD_DIM)


MESH = pl.DeviceIdType.MESH


class Lattice:
    def __init__(self, steps):
        self.steps = steps
        self.count = 1 << len(steps)

    def peer(self, level):
        axis, step = self.steps[level]
        return {axis: lax.axis_index(axis) ^ step}

    def index(self, mask):
        found = 0
        for level, (axis, step) in enumerate(self.steps):
            bit = (lax.axis_index(axis) // step) % 2
            found = found + (1 - bit if mask >> level & 1 else bit) * (1 << level)
        return found

    def member(self, axis, block):
        found = lax.axis_index(axis)
        for level, (name, step) in enumerate(self.steps):
            if name == axis:
                found = found + ((block // (1 << level)) % 2 - (lax.axis_index(axis) // step) % 2) * step
        return found

    def shift(self, mask):
        found = {"dp": 0, "tensor": 0}
        for level, (axis, step) in enumerate(self.steps):
            if mask >> level & 1:
                found[axis] ^= step
        return found["dp"], found["tensor"]


def remote(src, dst, send, recv, peer):
    return pltpu.make_async_remote_copy(
        src_ref=src, dst_ref=dst, send_sem=send, recv_sem=recv, device_id=peer, device_id_type=MESH
    )


class Gather:
    def __init__(self, lattice, view, send, recv, base=0, own=None):
        self.lattice, self.view, self.send, self.recv, self.base = lattice, view, send, recv, base
        self.own = own
        self.sent = []

    def copy(self, level, mask):
        slot = self.base + (1 << level) + mask
        place = self.view(mask)
        src = self.own if mask == 0 and self.own is not None else place
        return remote(src, place, self.send.at[slot], self.recv.at[slot], self.lattice.peer(level))

    def start(self, levels=None):
        for level in range(len(self.lattice.steps)) if levels is None else levels:
            copy = self.copy(level, 0)
            copy.start()
            self.sent.append(copy)

    def arrive(self, mask):
        level = mask.bit_length() - 1
        slot = self.base + mask
        place = self.view(mask)
        remote(place, place, self.send.at[slot], self.recv.at[slot], self.lattice.peer(level)).wait_recv()
        for later in range(level + 1, len(self.lattice.steps)):
            copy = self.copy(later, mask)
            copy.start()
            self.sent.append(copy)

    def finish(self):
        for copy in self.sent:
            copy.wait_send()


class Scatter:
    def __init__(self, lattice, read, write, out, came, send, recv, base=0):
        self.lattice, self.read, self.write = lattice, read, write
        self.out, self.came, self.send, self.recv, self.base = out, came, send, recv, base
        self.sent = []

    def push(self, mask):
        level = mask.bit_length() - 1
        slot = self.base + mask
        copy = remote(
            self.out.at[mask - 1],
            self.came.at[mask - 1],
            self.send.at[slot],
            self.recv.at[slot],
            self.lattice.peer(level),
        )
        copy.start()
        self.sent.append(copy)

    def put(self, mask):
        self.out[mask - 1] = self.read(mask).astype(BF)
        self.push(mask)

    def level(self, level):
        for mask in reversed(range(1 << level)):
            slot = (1 << level) + mask
            place = self.came.at[slot - 1]
            remote(
                self.out.at[slot - 1],
                place,
                self.send.at[self.base + slot],
                self.recv.at[self.base + slot],
                self.lattice.peer(level),
            ).wait_recv()
            total = self.read(mask) + self.came[slot - 1].astype(F32)
            if mask and mask >= 1 << (level - 1):
                self.out[mask - 1] = total.astype(BF)
                self.push(mask)
            else:
                self.write(mask, total)

    def run(self):
        for level in reversed(range(len(self.lattice.steps))):
            self.level(level)

    def finish(self):
        for copy in self.sent:
            copy.wait_send()


def score_steps(all_t, all_d):
    if len(all_d) <= 2:
        rows_q = [("tensor", step) for step in all_t[1:-1]] + [("dp", step) for step in all_d]
        rows_p = [("tensor", step) for step in all_t[:1] + all_t[-1:]]
    else:
        rows_q = [("tensor", step) for step in all_t[:-1]] + [("dp", step) for step in all_d[-1:]]
        rows_p = [("dp", step) for step in all_d[:-1]] + [("tensor", step) for step in all_t[-1:]]
    return rows_q, rows_p


def score_peers(all_t, rows_p):
    return [item for item in offsets([step for step in all_t if ("tensor", step) not in rows_p]) if item]


def greet(peers):
    barrier = pltpu.get_barrier_semaphore()
    for peer in peers:
        pl.semaphore_signal(barrier, inc=1, device_id=peer, device_id_type=MESH)
    pl.semaphore_wait(barrier, len(peers))


def forward_kernel(
    all_t, all_d, ship_bias,
    len_q, len_p, dense_cot, late_cot,
    x_q, x_p, w_qkv, qv_bias, w_out, up_piece, w_down, qkv_piece, bias_in, gain, shift, offset, w_colbert,
    o_q, o_k, o_v, o_lse, o_ctx, o_out, o_up, o_down, o_qkv, o_normed, o_slope, o_active,
    o_normal, o_unit, o_low, o_spread, o_grad,
    x, q, k, v, ctx, lse, ctx_rows, out_all, up, down, normed, slope, active, sums, s_out, s_in,
    first, normal, unit, vec, low, scales, wc, bias_all, bias_row, w_cols, w_turn,
    rows_q, rows_p, raised, pull, mass, mass_in, out_q, in_q, sum_p, out_p, in_p, grad,
    local, g_send, g_recv, a_send, a_recv, b_send, b_recv, n_send, n_recv, r_send, r_recv,
    gq_send, gq_recv, gp_send, gp_recv, m_send, m_recv, rq_send, rq_recv, rp_send, rp_recv,
):
    group, rank = lax.axis_index("dp"), lax.axis_index("tensor")
    ranks, groups = 1 << len(all_t), 1 << len(all_d)
    span, width = x_q.shape
    columns = w_qkv.shape[2]
    share = span // ranks
    units = up.shape[0]
    piece = units // ranks
    turn_up, turn_qkv = up_piece.shape[0] != piece, qkv_piece.shape[0] != 3 * columns // 2
    quarter = columns // 4
    rows = groups * share
    heads = columns // HEAD_DIM
    scale = HEAD_DIM**-0.5

    x_copies = [pltpu.make_async_copy(src, x.at[s], local.at[s]) for s, src in enumerate((x_q, x_p))]
    for copy in x_copies:
        copy.start()
    if turn_up:
        up_copy = pltpu.make_async_copy(
            up_piece.at[:, pl.ds(pl.multiple_of(group * piece, piece), piece)], w_cols, local.at[4]
        )
        up_copy.start()
    wc_copy = pltpu.make_async_copy(w_colbert, wc, local.at[2])
    wc_copy.start()
    greet([{"tensor": rank ^ item} for item in range(1, ranks)] + [{"dp": group ^ item} for item in all_d])

    tensor = Lattice([("tensor", step) for step in all_t])
    quad = Lattice([("tensor", step) for step in all_t] + [("dp", step) for step in all_d[-2:]])
    data = Lattice([("dp", step) for step in all_d])

    def quarters(ref, size):
        def view(mask):
            d, t = quad.shift(mask)
            return ref.at[rank ^ t, pl.ds(pl.multiple_of(((group ^ d) % 4) * size, size), size)]

        return view

    def unit_rows(ref):
        return lambda mask: ref.at[pl.ds(pl.multiple_of((rank ^ tensor.shift(mask)[1]) * piece, piece), piece)]

    wide, tall = quad.count, tensor.count
    far, near = list(range(len(all_t) - 1)), [len(all_t) - 1]
    at_quarter = pl.ds(pl.multiple_of((group % 4) * quarter, quarter), quarter)
    at_piece = pl.ds(pl.multiple_of(group * piece, piece), piece)
    take_out = Gather(quad, quarters(out_all, quarter), g_send, g_recv, 0, own=w_out.at[at_quarter])
    take_up = Gather(tensor, unit_rows(up), g_send, g_recv, wide, own=None if turn_up else up_piece)
    take_down = Gather(tensor, unit_rows(down), g_send, g_recv, wide + tall, own=w_down.at[at_piece])
    cores = Lattice([("tensor", step) for step in all_t] + [("dp", all_d[-1])])
    slab = 3 * columns // 2
    qkv_own = w_turn.at[pl.ds(pl.multiple_of((group % 2) * slab, slab), slab)] if turn_qkv else qkv_piece

    def slab_view(mask):
        d, t = cores.shift(mask)
        return o_qkv.at[rank ^ t, pl.ds(pl.multiple_of(((group ^ d) % 2) * slab, slab), slab)]

    take_qkv = Gather(cores, slab_view, g_send, g_recv, wide + 2 * tall, own=qkv_own)
    own_copies = [
        pltpu.make_async_copy(w_out.at[at_quarter], take_out.view(0), local.at[3]),
        pltpu.make_async_copy(w_down.at[at_piece], take_down.view(0), local.at[5]),
    ]
    if not turn_up:
        own_copies.append(pltpu.make_async_copy(up_piece, take_up.view(0), local.at[4]))
    early = [tall // 4] + list(range(1, tall // 4))
    late = list(range(tall // 4 + 1, tall // 2))
    take_out.start()
    if turn_up:
        up_copy.wait()
        take_up.view(0)[...] = w_cols[...].T
    take_up.start(near)
    for copy in own_copies:
        copy.start()
    pending = []
    bias_copies = []
    if ship_bias:
        bias_all[rank] = bias_in[...]
        for item in range(1, ranks):
            copy = remote(
                bias_in, bias_all.at[rank], b_send.at[item], b_recv.at[item], {"tensor": rank ^ item}
            )
            copy.start()
            bias_copies.append(copy)

    lengths = (len_q[group], len_p[group])
    def project(s):
        x_copies[s].wait()
        tokens = x[s]
        q[s] = (dot(tokens, w_qkv[0]) + qv_bias[0:1, :].astype(F32)).astype(BF)
        k[s] = dot(tokens, w_qkv[1]).astype(BF)
        v[s] = (dot(tokens, w_qkv[2]) + qv_bias[1:2, :].astype(F32)).astype(BF)

    block = min(BLOCK, span)

    def attention(s, begin, end):
        keep = lax.broadcasted_iota(jnp.int32, (1, span), 1) < lengths[s]

        @pl.loop(begin, end)
        def _(index):
            at = pl.ds(pl.multiple_of(index * block, block), block)
            query = q[s, at, :]
            total = jnp.zeros((block, columns), F32)
            for head in range(heads):
                mask = head_mask(columns, head)
                mine = jnp.where(mask, query, jnp.zeros_like(query)) * jnp.asarray(scale, BF)
                scores = jnp.where(keep, inner_rows(mine, k[s]), -1e30)
                top = jnp.max(scores, axis=-1, keepdims=True)
                weight = jnp.exp(scores - top)
                amount = jnp.sum(weight, axis=-1, keepdims=True)
                part = dot(weight.astype(BF), v[s]) / amount
                total = jnp.where(mask, part, total)
                column = jnp.broadcast_to(top + jnp.log(amount), (block, 128))
                lse[s, head : head + 1, at] = column.T[0:1, :]
            ctx[s, at, :] = total.astype(BF)

    sends = []

    def trade_context(s):
        at = pl.ds(s * share, share)
        for item in range(1, ranks):
            peer = rank ^ item
            copy = remote(
                ctx.at[s, pl.ds(pl.multiple_of(peer * share, share), share)],
                ctx_rows.at[rank, at],
                a_send.at[s * ranks + item],
                a_recv.at[s * ranks + item],
                {"tensor": peer},
            )
            copy.start()
            sends.append(copy)
        ctx_rows[rank, s * share : (s + 1) * share, :] = ctx[s, pl.ds(pl.multiple_of(rank * share, share), share), :]

    def context_here(s):
        at = pl.ds(s * share, share)
        for item in range(1, ranks):
            place = ctx_rows.at[rank ^ item, at]
            remote(
                place, place, a_send.at[s * ranks + item], a_recv.at[s * ranks + item], {"tensor": rank ^ item}
            ).wait_recv()

    def out_going(src, dst, index):
        copy = pltpu.make_async_copy(src, dst, local.at[index])
        copy.start()
        pending.append(copy)

    def arrive(taking, masks):
        for mask in masks:
            taking.arrive(mask)

    count = span // block
    take_down.start(near)
    project(0)
    arrive(take_out, early)
    take_up.start(far)
    arrive(take_out, late)
    attention(0, 0, count)
    trade_context(0)
    for copy in own_copies:
        copy.wait()
    project(1)
    arrive(take_up, early[:1])
    attention(1, 0, count // 2)
    arrive(take_up, early[1:])
    attention(1, count // 2, count)
    take_down.start(far)
    arrive(take_out, range(tall // 2, wide))
    if turn_qkv:
        for i in range(3):
            w_turn[i * columns : (i + 1) * columns, :] = w_qkv[i].T
    arrive(take_up, late)
    trade_context(1)
    out_going(q, o_q, 7)
    out_going(k, o_k, 8)
    out_going(v, o_v, 9)
    out_going(lse, o_lse, 10)

    def to_rows(s):
        at = slice(s * share, (s + 1) * share)
        context_here(s)
        if columns % 128 == 0:
            mix = jnp.concatenate([ctx_rows[r, at, :] for r in range(ranks)], axis=1)
            mixed = dot(mix, out_all[...].reshape(ranks * columns, width))
        else:
            mixed = dot(ctx_rows[0, at, :], out_all[0])
            for r in range(1, ranks):
                mixed = mixed + dot(ctx_rows[r, at, :], out_all[r])
        mine = x[s, pl.ds(pl.multiple_of(rank * share, share), share), :].astype(F32)
        value, plain, inverse = layer_norm(mine + mixed + offset[0:1, :], gain[0:1, :], shift[0:1, :])
        first[at, :] = value
        normal[0, at, :] = plain
        scales[0, at, :] = jnp.broadcast_to(inverse, (share, 128))
        normed[s, pl.ds(pl.multiple_of(group * share, share), share), :] = value.astype(BF)

        def view(mask):
            d, _ = data.shift(mask)
            return normed.at[s, pl.ds(pl.multiple_of((group ^ d) * share, share), share)]

        taking = Gather(data, view, n_send, n_recv, s * groups)
        taking.start()
        return taking

    normed_takes = [to_rows(0)]
    arrive(take_down, early)
    normed_takes.append(to_rows(1))
    arrive(take_up, range(tall // 2, tall))
    arrive(take_down, late)
    take_qkv.start()
    out_going(qkv_own, take_qkv.view(0), 6)
    if ship_bias:
        for item in range(1, ranks):
            place = bias_all.at[rank ^ item]
            remote(place, place, b_send.at[item], b_recv.at[item], {"tensor": rank ^ item}).wait_recv()
        for r in range(ranks):
            bias_row[0:1, r * piece : (r + 1) * piece] = bias_all[r, 0:1, :].astype(F32)
    else:
        bias_row[0:1, :] = bias_in[0:1, :]
    arrive(normed_takes[0], range(1, groups))

    def spot(mask):
        return pl.multiple_of((group ^ data.shift(mask)[0]) * share, share)

    gives = []
    for s in range(2):

        def read(mask, s=s):
            return sums[pl.ds(s * rows + spot(mask), share), :]

        def write(mask, value, s=s):
            sums[pl.ds(s * rows + spot(mask), share), :] = value

        gives.append(Scatter(data, read, write, s_out.at[s], s_in.at[s], r_send, r_recv, s * groups))

    tile = min(512, units)

    def expand(s):
        at_rows = slice(s * rows, (s + 1) * rows)

        @pl.loop(0, units // tile)
        def _(index):
            at = pl.ds(pl.multiple_of(index * tile, tile), tile)
            value = inner_rows(normed[s], up[at, :]) + bias_row[0:1, at]
            phi = 0.5 * (1.0 + lax.erf(value * 0.7071067811865476))
            active[at_rows, at] = (value * phi).astype(BF)
            slope[at_rows, at] = (phi + value * jnp.exp(-0.5 * value * value) * 0.3989422804014327).astype(BF)

    def reduce(s):
        at_rows = slice(s * rows, (s + 1) * rows)

        @pl.loop(0, width // 512)
        def _(index):
            at = pl.ds(pl.multiple_of(index * 512, 512), 512)
            sums[at_rows, at] = dot(active[at_rows, :], down[:, at])

        for mask in reversed(range(groups // 2, groups)):
            gives[s].put(mask)

    top = len(all_d) - 1
    expand(0)
    arrive(normed_takes[1], range(1, groups))
    expand(1)
    arrive(take_down, range(tall // 2, tall))
    reduce(0)
    arrive(take_qkv, early)
    reduce(1)
    gives[0].level(top)
    out_going(ctx_rows, o_ctx, 11)
    out_going(out_all, o_out, 12)
    out_going(up, o_up, 13)
    out_going(down, o_down, 14)
    out_going(normed, o_normed, 15)
    out_going(slope, o_slope, 16)
    out_going(active, o_active, 17)
    gives[1].level(top)
    wc_copy.wait()

    steps_q, steps_p = score_steps(all_t, all_d)
    lattice_q, lattice_p = Lattice(steps_q), Lattice(steps_p)
    levels_y = [level for level, (axis, _) in enumerate(steps_p) if axis == "dp"]
    count_y = 1 << len(levels_y)

    def spot_q(mask):
        return pl.multiple_of(lattice_q.index(mask) * share, share)

    def spot_p(mask):
        return pl.multiple_of(lattice_p.index(mask) * share, share)

    takes = (
        Gather(lattice_q, lambda m: rows_q.at[pl.ds(spot_q(m), share)], gq_send, gq_recv, own=vec.at[pl.ds(0, share)]),
        Gather(
            lattice_p, lambda m: rows_p.at[pl.ds(spot_p(m), share)], gp_send, gp_recv, own=vec.at[pl.ds(share, share)]
        ),
    )
    for s in range(2):
        at = slice(s * share, (s + 1) * share)
        for level in reversed(range(top)):
            gives[s].level(level)
        feed = gives[s].read(0)
        value, plain, inverse = layer_norm(first[at, :] + feed + offset[1:2, :], gain[1:2, :], shift[1:2, :])
        short = value.astype(BF)
        place = lax.broadcasted_iota(jnp.int32, (share, 1), 0) + rank * share
        chosen = jnp.where(place == 0, value, dot(short, wc[...]) + offset[2:3, :])
        norm = lax.rsqrt(jnp.sum(chosen * chosen, axis=-1, keepdims=True) + 1e-06)
        chosen = chosen * norm
        vec[at, :] = chosen.astype(BF)
        takes[s].start()
        unit[at, :] = chosen
        normal[1, at, :] = plain
        scales[1, at, :] = jnp.broadcast_to(inverse, (share, 128))
        scales[2, at, :] = jnp.broadcast_to(norm, (share, 128))
        low[at, :] = short
    rows_q[pl.ds(spot_q(0), share), :] = vec[0:share, :]
    rows_p[pl.ds(spot_p(0), share), :] = vec[share : 2 * share, :]
    take_q, take_p = takes
    many_q, many_p = lattice_q.count * share, lattice_p.count * share
    half_q, half_p = many_q // 2, many_p // 2
    arrive(take_q, range(1, lattice_q.count // 4))
    arrive(take_p, range(1, lattice_p.count // 2))
    arrive(take_q, [lattice_q.count // 4])
    arrive(take_q, range(lattice_q.count // 4 + 1, lattice_q.count // 2))
    out_going(normal, o_normal, 18)
    out_going(unit, o_unit, 19)
    out_going(low, o_low, 20)
    out_going(scales, o_spread, 21)

    lane = lax.broadcasted_iota(jnp.int32, (1, many_q), 1)
    block_q = lane // share
    group_q = lattice_q.member("dp", block_q)
    place_q = lattice_q.member("tensor", block_q) * share + lane % share
    temper = float(width) ** 0.5
    which_y = [sum(((y >> i) & 1) << level for i, level in enumerate(levels_y)) for y in range(count_y)]
    late_rows, dense_rows = [], []
    for y in range(count_y):
        which = lattice_p.member("dp", which_y[y])
        length, late_row, dense_row = 0, 0.0, 0.0
        for g in range(groups):
            length = jnp.where(group_q == g, len_q[g], length)
            late_row = jnp.where(group_q == g, temper * late_cot[g, which], late_row)
            dense_row = jnp.where(group_q == g, 50.0 * dense_cot[g, which], dense_row)
        late_rows.append(jnp.where((place_q >= 1) & (place_q < length), late_row, 0.0))
        dense_rows.append(jnp.where(place_q == 0, dense_row, 0.0))
    arrive(take_q, range(lattice_q.count // 2, lattice_q.count))
    arrive(take_p, range(lattice_p.count // 2, lattice_p.count))
    arrive(take_qkv, late)

    def place_p(block):
        first_place = lattice_p.member("tensor", block) * share
        return first_place + lax.broadcasted_iota(jnp.int32, (share, 1), 0)

    def part_of(block):
        return sum(((block >> level) & 1) << i for i, level in enumerate(levels_y))

    mass[...] = jnp.zeros_like(mass)
    for block in range(lattice_p.count):
        at = slice(block * share, (block + 1) * share)
        y = part_of(block)
        dots = inner_rows(rows_p[at, :], rows_q[...])
        place = place_p(block)
        counted = (place >= 1) & (place < len_p[lattice_p.member("dp", block)])
        value = jnp.where(counted, jnp.exp(dots * temper - temper), 0.0)
        raised[at, :] = value
        mass[y : y + 1, :] += jnp.sum(value, axis=0, keepdims=True)
    mass_copies = []
    for index, item in enumerate(score_peers(all_t, steps_p)):
        copy = remote(mass, mass_in.at[index], m_send.at[index], m_recv.at[index], {"tensor": rank ^ item})
        copy.start()
        mass_copies.append(copy)
    total = mass[...]
    for index, copy in enumerate(mass_copies):
        copy.wait_recv()
        total = total + mass_in[index]
    for block in range(lattice_p.count):
        at = slice(block * share, (block + 1) * share)
        y = part_of(block)
        value = raised[at, :] * (late_rows[y] / total[y : y + 1, :])
        pull[at, :] = (value + jnp.where(place_p(block) == 0, dense_rows[y], 0.0)).astype(BF)

    mine_q = (lax.axis_index(steps_q[-1][0]) // steps_q[-1][1]) % 2
    mine_p = (lax.axis_index(steps_p[-1][0]) // steps_p[-1][1]) % 2

    def fill_q(half):
        at = pl.ds(pl.multiple_of(half * half_q, half_q), half_q)
        sums[at, :] = outer_rows(pull[:, at], rows_p[...])

    def fill_p(half):
        at = pl.ds(pl.multiple_of(half * half_p, half_p), half_p)
        sum_p[at, :] = dot(pull[at, :], rows_q[...])

    def reader(ref, find):
        return lambda m: ref[pl.ds(find(m), share), :]

    def writer(ref, find):
        def write(m, value):
            ref[pl.ds(find(m), share), :] = value

        return write

    give_q = Scatter(lattice_q, reader(sums, spot_q), writer(sums, spot_q), out_q, in_q, rq_send, rq_recv)
    give_p = Scatter(lattice_p, reader(sum_p, spot_p), writer(sum_p, spot_p), out_p, in_p, rp_send, rp_recv)
    fill_q(1 - mine_q)
    for mask in reversed(range(lattice_q.count // 2, lattice_q.count)):
        give_q.put(mask)
    fill_p(1 - mine_p)
    for mask in reversed(range(lattice_p.count // 2, lattice_p.count)):
        give_p.put(mask)
    fill_q(mine_q)
    arrive(take_qkv, range(tall // 2, tall))
    give_q.level(len(steps_q) - 1)
    fill_p(mine_p)
    give_p.level(len(steps_p) - 1)
    for level in reversed(range(len(steps_q) - 1)):
        give_q.level(level)
    for level in reversed(range(len(steps_p) - 1)):
        give_p.level(level)
    grad[0:share, :] = sums[pl.ds(spot_q(0), share), :]
    grad[share : 2 * share, :] = sum_p[pl.ds(spot_p(0), share), :]
    out_going(grad, o_grad, 22)
    arrive(take_qkv, range(tall, 2 * tall))
    for move in [take_out, take_up, take_down, take_qkv, take_q, take_p, give_q, give_p] + normed_takes + gives:
        move.finish()
    for copy in sends + bias_copies + mass_copies:
        copy.wait_send()
    for copy in pending:
        copy.wait()


def forward(len_q, len_p, dense_cot, late_cot, queries, passages, w_qkv, qv_bias, w_out, up_piece, w_down, qkv_piece,
            bias_in, gain, shift, offset, w_colbert):
    groups, ranks = lax.axis_size("dp"), lax.axis_size("tensor")
    all_t, all_d = steps_of(ranks), steps_of(groups)
    span, width = queries.shape
    columns = w_qkv.shape[2]
    heads = columns // HEAD_DIM
    share = span // ranks
    piece = w_down.shape[0] // groups
    units = piece * ranks
    rows = groups * share
    ship_bias = bias_in.shape[0] == 16
    steps_q, steps_p = score_steps(all_t, all_d)
    blocks_q, blocks_p = 1 << len(steps_q), 1 << len(steps_p)
    many_q, many_p, peers = blocks_q * share, blocks_p * share, len(score_peers(all_t, steps_p))

    shapes = [
        ((2, span, columns), BF),
        ((2, span, columns), BF),
        ((2, span, columns), BF),
        ((2, heads, span), F32),
        ((ranks, 2 * share, columns), BF),
        ((ranks, columns, width), BF),
        ((units, width), BF),
        ((units, width), BF),
        ((ranks, 3 * columns, width), BF),
        ((2, rows, width), BF),
        ((2 * rows, units), BF),
        ((2 * rows, units), BF),
        ((2, 2 * share, width), F32),
        ((2 * share, width), F32),
        ((2 * share, width), BF),
        ((3, 2 * share, 128), F32),
        ((2 * share, width), F32),
    ]
    dma = pltpu.SemaphoreType.DMA
    vmem = pltpu.VMEM
    hold, leave = pl.BlockSpec(memory_space=pltpu.VMEM), pl.BlockSpec(memory_space=pl.ANY)
    flat = pl.BlockSpec(memory_space=pltpu.SMEM)

    def pair(count):
        return [dma((count,)), dma((count,))]

    return pl.pallas_call(
        functools.partial(forward_kernel, all_t, all_d, ship_bias),
        out_shape=[jax.ShapeDtypeStruct(*item) for item in shapes],
        in_specs=[flat] * 4
        + [leave, leave, hold, hold, leave, leave, leave, leave, hold, hold, hold, hold, leave],
        out_specs=[leave] * len(shapes),
        scratch_shapes=[
            vmem((2, span, width), BF),
            vmem((2, span, columns), BF),
            vmem((2, span, columns), BF),
            vmem((2, span, columns), BF),
            vmem((2, span, columns), BF),
            vmem((2, heads, span), F32),
            vmem((ranks, 2 * share, columns), BF),
            vmem((ranks, columns, width), BF),
            vmem((units, width), BF),
            vmem((units, width), BF),
            vmem((2, rows, width), BF),
            vmem((2 * rows, units), BF),
            vmem((2 * rows, units), BF),
            vmem((2 * rows, width), F32),
            vmem((2, groups - 1, share, width), BF),
            vmem((2, groups - 1, share, width), BF),
            vmem((2 * share, width), F32),
            vmem((2, 2 * share, width), F32),
            vmem((2 * share, width), F32),
            vmem((2 * share, width), BF),
            vmem((2 * share, width), BF),
            vmem((3, 2 * share, 128), F32),
            vmem((width, width), BF),
            vmem((ranks, 16, piece), BF),
            vmem((8, units), F32),
            vmem((width, piece), BF),
            vmem((3 * columns, width) if columns % 128 == 0 else (16, 128), BF),
            vmem((many_q, width), BF),
            vmem((many_p, width), BF),
            vmem((many_p, many_q), F32),
            vmem((many_p, many_q), BF),
            vmem((8, many_q), F32),
            vmem((peers, 8, many_q), F32),
            vmem((blocks_q - 1, share, width), BF),
            vmem((blocks_q - 1, share, width), BF),
            vmem((many_p, width), F32),
            vmem((blocks_p - 1, share, width), BF),
            vmem((blocks_p - 1, share, width), BF),
            vmem((2 * share, width), F32),
            dma((23,)),
        ]
        + pair(8 * ranks)
        + pair(2 * ranks)
        + pair(ranks)
        + pair(2 * groups)
        + pair(2 * groups)
        + pair(blocks_q)
        + pair(blocks_p)
        + pair(peers)
        + pair(blocks_q)
        + pair(blocks_p),
        compiler_params=pltpu.CompilerParams(
            collective_id=2, has_side_effects=True, vmem_limit_bytes=62 * 2**20
        ),
        cost_estimate=pl.CostEstimate(flops=10**11, bytes_accessed=40 * 2**20, transcendentals=2**23),
        name="forward",
    )(len_q, len_p, dense_cot, late_cot, queries, passages, w_qkv, qv_bias, w_out, up_piece, w_down, qkv_piece,
      bias_in, gain, shift, offset, w_colbert)


class Settle:
    def __init__(self, lattice, view, came, send, recv, base=0):
        self.lattice, self.view, self.came = lattice, view, came
        self.send, self.recv, self.base = send, recv, base
        self.sent = []

    def copy(self, mask):
        return remote(
            self.view(mask),
            self.came.at[mask - 1],
            self.send.at[self.base + mask],
            self.recv.at[self.base + mask],
            self.lattice.peer(mask.bit_length() - 1),
        )

    def push(self, mask):
        copy = self.copy(mask)
        copy.start()
        self.sent.append(copy)

    def start(self):
        for mask in reversed(range(self.lattice.count // 2, self.lattice.count)):
            self.push(mask)

    def level(self, level):
        for mask in reversed(range(1 << level)):
            slot = (1 << level) + mask
            self.copy(slot).wait_recv()
            place = self.view(mask)
            place[...] = (place[...].astype(F32) + self.came[slot - 1].astype(F32)).astype(BF)
            if mask and mask >= 1 << (level - 1):
                self.push(mask)

    def finish(self):
        for copy in self.sent:
            copy.wait_send()


def backward_kernel(
    all_t, all_d,
    len_q, len_p, grad_vec, h_unit, h_low, h_scales, h_normals, h_wc, h_down, h_up, h_slope, h_active, h_normed,
    h_out, h_ctx, h_q, h_k, h_v, h_lse, x_q, x_p, h_qkv, gain,
    o_tokens, o_down, o_up, o_out, o_wc, o_qkv, o_small,
    pool, slope, active, out_all, wc, ctx_rows, q, k, v, lse, g1, unit, low, proj, normals, scales, sums,
    s_out, s_in, turn, ctx_out, heads_grad, turned, turned_rows, dk_sum, dv_sum,
    g_down, g_down_in, g_up, g_up_in, g_out_in, g_wc_in, qkv_sum, qkv_low, qkv_in,
    small, small_in, stage, stage_in,
    local, n_send, n_recv, r_send, r_recv, d_send, d_recv, u_send, u_recv, w_send, w_recv, c_send, c_recv,
    a_send, a_recv, t_send, t_recv, f_send, f_recv, m_send, m_recv, y_send, y_recv, q_send, q_recv,
):
    group, rank = lax.axis_index("dp"), lax.axis_index("tensor")
    ranks, groups = 1 << len(all_t), 1 << len(all_d)
    far_d = all_d[:-1]
    span, width = x_q.shape
    columns = q.shape[2]
    share = span // ranks
    units = h_up.shape[0]
    piece = units // ranks
    quarter = columns // 4
    rows = groups * share
    heads = columns // HEAD_DIM
    scale = HEAD_DIM**-0.5
    flat = width // ranks // 4
    at_up, at_down = pl.ds(0, units), pl.ds(units, units)
    at_normed, at_feed = pl.ds(2 * units, 2 * rows), pl.ds(2 * units + 2 * rows, 2 * rows)
    feed_at = 2 * units + 2 * rows

    loads = []

    def load(src, dst):
        copy = pltpu.make_async_copy(src, dst, local.at[len(loads)])
        copy.start()
        loads.append(copy)
        return copy

    early = [load(grad_vec, g1), load(h_unit, unit), load(h_scales, scales), load(h_low, low), load(h_wc, wc)]
    early.append(load(h_normals, normals))
    ffn = [load(h_down, pool.at[at_down]), load(h_slope, slope), load(h_up, pool.at[at_up])]
    later = [load(h_active, active), load(h_normed, pool.at[at_normed])]
    last = [load(h_out, out_all), load(h_ctx, ctx_rows)]
    heads_in = [load(h_q, q), load(h_k, k), load(h_v, v), load(h_lse, lse)]
    greet([{"tensor": rank ^ item} for item in range(1, ranks)] + [{"dp": group ^ item} for item in all_d])

    tensor = Lattice([("tensor", step) for step in all_t])
    quad = Lattice([("tensor", step) for step in all_t] + [("dp", step) for step in all_d[-2:]])
    data = Lattice([("dp", step) for step in all_d])

    def quarters(ref, size, lattice=quad):
        def view(mask):
            d, t = lattice.shift(mask)
            return ref.at[pl.ds(pl.multiple_of(((rank ^ t) * 4 + (group ^ d) % 4) * size, size), size)]

        return view

    cross = Lattice(tensor.steps[:-2] + [tensor.steps[-1], tensor.steps[-2]])

    def pieces(ref, lattice):
        return lambda mask: ref.at[pl.ds(pl.multiple_of((rank ^ lattice.shift(mask)[1]) * piece, piece), piece)]

    def spot(mask):
        return pl.multiple_of((group ^ data.shift(mask)[0]) * share, share)

    flow = Lattice([("dp", all_d[-2])] + tensor.steps + [("dp", all_d[-1])])
    give_wc = Settle(flow, quarters(wc, flat, flow), g_wc_in, c_send, c_recv)
    give_out = Settle(quad, quarters(out_all, quarter), g_out_in, w_send, w_recv)
    give_down = Settle(tensor, pieces(g_down, tensor), g_down_in, d_send, d_recv)
    give_up = Settle(cross, pieces(g_up, cross), g_up_in, u_send, u_recv)

    small[...] = jnp.zeros_like(small)
    for copy in early:
        copy.wait()
    takes = []
    for s in range(2):
        at = slice(s * share, (s + 1) * share)
        grad, plain = g1[at, :], unit[at, :]
        chosen = scales[2, at, 0:1] * (grad - plain * jnp.sum(grad * plain, axis=-1, keepdims=True))
        leading = lax.broadcasted_iota(jnp.int32, (share, 1), 0) + rank * share == 0
        short = jnp.where(leading, 0.0, chosen).astype(BF)
        proj[at, :] = short
        grad = jnp.where(leading, chosen, 0.0) + inner_rows(short, wc[...])
        middle, gains, shifts = norm_back(grad, normals[1, at, :], scales[1, at, 0:1], gain[1:2, :])
        g1[at, :] = middle
        small[0, 1:2, :] += gains[None, :]
        small[0, 3:4, :] += shifts[None, :]
        small[0, 5:6, :] += jnp.sum(middle, axis=0, keepdims=True)
        small[0, 6:7, :] += jnp.sum(short.astype(F32), axis=0, keepdims=True)
        own = pl.multiple_of(feed_at + s * rows + group * share, share)
        pool[pl.ds(own, share), :] = middle.astype(BF)

        def view(mask, s=s):
            place = feed_at + s * rows + (group ^ data.shift(mask)[0]) * share
            return pool.at[pl.ds(pl.multiple_of(place, share), share)]

        taking = Gather(data, view, n_send, n_recv, s * groups)
        taking.start()
        takes.append(taking)

    @pl.loop(0, width // 512)
    def _(index):
        at = pl.ds(pl.multiple_of(index * 512, 512), 512)
        wc[at, :] = outer_rows(low[:, at], proj[...]).astype(BF)

    give_wc.start()

    gives = []
    for s in range(2):

        def read(mask, s=s):
            return sums[s, pl.ds(spot(mask), share), :]

        def write(mask, value, s=s):
            sums[s, pl.ds(spot(mask), share), :] = value

        gives.append(Scatter(data, read, write, s_out.at[s], s_in.at[s], r_send, r_recv, s * groups))
    for copy in ffn:
        copy.wait()
    tile = min(512, units)

    def shrink(s):
        at_rows = slice(s * rows, (s + 1) * rows)
        feed_rows = slice(feed_at + s * rows, feed_at + (s + 1) * rows)

        @pl.loop(0, units // tile)
        def _(index):
            at = pl.ds(pl.multiple_of(index * tile, tile), tile)
            down_at = pl.ds(pl.multiple_of(units + index * tile, tile), tile)
            value = inner_rows(pool[feed_rows, :], pool[down_at, :]) * slope[at_rows, at].astype(F32)
            value = value.astype(BF)
            slope[at_rows, at] = value
            small[0, 7:8, at] += jnp.sum(value.astype(F32), axis=0, keepdims=True)

        @pl.loop(0, width // 512)
        def _(index):
            at = pl.ds(pl.multiple_of(index * 512, 512), 512)
            sums[s, :, at] = dot(slope[at_rows, :], pool[at_up, at])

    def put(s):
        for mask in reversed(range(groups // 2, groups)):
            gives[s].put(mask)

    top = len(all_d) - 1
    last_t = len(all_t) - 1
    quad_top = len(all_t) + 1
    blocks = list(reversed(range(ranks // 2, ranks)))
    give_wc.level(quad_top)
    for mask in range(1, groups):
        takes[0].arrive(mask)
    shrink(0)
    put(0)
    for copy in later:
        copy.wait()
    for mask in range(1, groups):
        takes[1].arrive(mask)
    gives[0].level(top)

    @pl.loop(0, units // tile)
    def _(index):
        at = pl.ds(pl.multiple_of(index * tile, tile), tile)
        g_down[at, :] = outer_rows(active[:, at], pool[at_feed, :]).astype(BF)

    for mask in blocks[:2]:
        give_down.push(mask)
    give_wc.level(last_t + 1)
    shrink(1)
    put(1)

    @pl.loop(0, units // tile)
    def _(index):
        at = pl.ds(pl.multiple_of(index * tile, tile), tile)
        g_up[at, :] = outer_rows(slope[:, at], pool[at_normed, :]).astype(BF)

    gives[1].level(top)
    for mask in blocks[:1]:
        give_up.push(mask)

    for copy in last:
        copy.wait()
    def small_step(level):
        copy = remote(
            small.at[level], small_in.at[level], m_send.at[level], m_recv.at[level], {"tensor": rank ^ all_t[level]}
        )
        return copy

    small_copies = [small_step(level) for level in range(len(all_t))]

    def small_next(level):
        small_copies[level].wait_recv()
        small[level + 1] = small[level] + small_in[level]
        if level + 1 < len(all_t):
            small_copies[level + 1].start()

    sends = []
    for s in range(2):
        at = slice(s * share, (s + 1) * share)
        for level in reversed(range(top)):
            gives[s].level(level)
        grad = g1[at, :] + gives[s].read(0)
        hidden, gains, shifts = norm_back(grad, normals[0, at, :], scales[0, at, 0:1], gain[0:1, :])
        g1[at, :] = hidden
        small[0, 0:1, :] += gains[None, :]
        small[0, 2:3, :] += shifts[None, :]
        small[0, 4:5, :] += jnp.sum(hidden, axis=0, keepdims=True)
        short = hidden.astype(BF)
        turn[at, :] = short
        if columns % 128 == 0:
            value = inner_rows(short, out_all[...]).astype(BF)
            for r in range(ranks):
                ctx_out[r, at, :] = value[:, r * columns : (r + 1) * columns]
        else:
            for r in range(ranks):
                ctx_out[r, at, :] = inner_rows(short, out_all[r * columns : (r + 1) * columns, :]).astype(BF)
        mine = pl.ds(pl.multiple_of(rank * share, share), share)
        for item in range(1, ranks):
            copy = remote(
                ctx_out.at[rank ^ item, pl.ds(s * share, share)],
                heads_grad.at[s, mine],
                a_send.at[s * ranks + item],
                a_recv.at[s * ranks + item],
                {"tensor": rank ^ item},
            )
            copy.start()
            sends.append(copy)
        heads_grad[s, mine, :] = ctx_out[rank, at, :]
        if s == 1:
            for mask in blocks[1:2]:
                give_up.push(mask)
            small_copies[0].start()
    for taking in takes:
        taking.finish()
    tall = load(x_q, pool.at[pl.ds(0, span)]), load(x_p, pool.at[pl.ds(span, span)])
    at_qkv = 2 * span
    pairs = Lattice([("dp", step) for step in all_d[-2:]])
    back_in = load(h_qkv, pool.at[pl.ds(at_qkv, 3 * columns * ranks)])

    for r in range(ranks):
        out_all[r * columns : (r + 1) * columns, :] = outer_rows(ctx_rows[r], turn[...]).astype(BF)
    give_wc.level(last_t)
    give_out.start()

    block = min(BLOCK, span)

    lengths = (len_q[group], len_p[group])

    def attention(s, begin, end):
        keep = lax.broadcasted_iota(jnp.int32, (span, 1), 0) < lengths[s]

        @pl.loop(begin, end)
        def _(index):
            at = pl.ds(pl.multiple_of(index * block, block), block)
            query = q[s, at, :]
            grad = heads_grad[s, at, :]
            total = jnp.zeros((block, columns), F32)
            for head in range(heads):
                mask = head_mask(columns, head)
                mine = jnp.where(mask, query, jnp.zeros_like(query)) * jnp.asarray(scale, BF)
                back = jnp.where(mask, grad, jnp.zeros_like(grad))
                scores = jnp.where(keep, inner_rows(k[s], mine), -1e30)
                probs = jnp.exp(scores - lse[s, head : head + 1, at])
                slant = inner_rows(v[s], back)
                middle = jnp.sum(probs * slant, axis=0, keepdims=True)
                twist = (probs * (slant - middle)).astype(BF)
                dv_sum[...] += dot(probs.astype(BF), back)
                dk_sum[...] += dot(twist, mine)
                part = outer_rows(twist, k[s]) * scale
                total = jnp.where(mask, part, total)
            turned[s, at, 0:columns] = total.astype(BF)

    def attention_start(s):
        for item in range(1, ranks):
            place = heads_grad.at[s, pl.ds(pl.multiple_of((rank ^ item) * share, share), share)]
            remote(
                place, place, a_send.at[s * ranks + item], a_recv.at[s * ranks + item], {"tensor": rank ^ item}
            ).wait_recv()
        dk_sum[...] = jnp.zeros_like(dk_sum)
        dv_sum[...] = jnp.zeros_like(dv_sum)

    def attention_end(s):
        turned[s, :, columns : 2 * columns] = dk_sum[...].astype(BF)
        turned[s, :, 2 * columns : 3 * columns] = dv_sum[...].astype(BF)
        for item in range(1, ranks):
            copy = remote(
                turned.at[s, pl.ds(pl.multiple_of((rank ^ item) * share, share), share)],
                turned_rows.at[rank, pl.ds(s * share, share)],
                t_send.at[s * ranks + item],
                t_recv.at[s * ranks + item],
                {"tensor": rank ^ item},
            )
            copy.start()
            sends.append(copy)
        turned_rows[rank, s * share : (s + 1) * share, :] = turned[
            s, pl.ds(pl.multiple_of(rank * share, share), share), :
        ]

    many = qkv_sum.shape[1]

    def qkv_grad(s):
        tokens = pool[s * span : (s + 1) * span, :]
        for i in range(3):
            part = turned[s, :, i * columns : (i + 1) * columns]
            whole = outer_rows(tokens, part)
            line = jnp.broadcast_to(jnp.sum(part.astype(F32), axis=0, keepdims=True), (many - width, columns))
            if s == 0:
                qkv_sum[i, 0:width, :] = whole
                qkv_sum[i, width:many, :] = line
            else:
                qkv_sum[i, 0:width, :] += whole
                qkv_sum[i, width:many, :] += line

    for copy in heads_in:
        copy.wait()
    count = span // block
    attention_start(0)
    attention(0, 0, count // 2)
    for mask in blocks[2:]:
        give_down.push(mask)
    for level in reversed(range(1, last_t)):
        give_wc.level(level)
    small_next(0)
    give_wc.level(0)
    for mask in blocks[2:]:
        give_up.push(mask)
    attention(0, count // 2, count)
    attention_end(0)
    for copy in tall:
        copy.wait()
    qkv_grad(0)
    attention_start(1)
    for level in range(1, len(all_t)):
        small_next(level)
    attention(1, 0, count // 2)
    small_own = small.at[len(all_t)]
    small_take = Gather(data, lambda m: o_small.at[group ^ data.shift(m)[0]], f_send, f_recv, 0, own=small_own)
    small_take.start()
    small_copy = load(small_own, o_small.at[group])
    give_up.level(last_t)
    attention(1, count // 2, count)
    attention_end(1)
    give_out.level(quad_top)

    rest = all_d[:-2]

    def settle_stage(which, source, size):
        base = which * max(1, len(rest))
        copies = []
        for index, step in enumerate(rest):
            src = source if index == 0 else stage.at[base + index - 1, pl.ds(0, size)]
            dst = stage_in.at[base + index, pl.ds(0, size)]
            copies.append(remote(src, dst, y_send.at[base + index], y_recv.at[base + index], {"dp": group ^ step}))
        for index, copy in enumerate(copies):
            copy.start()
            copy.wait_recv()
            before = source[...] if index == 0 else stage[base + index - 1, 0:size, :]
            value = before.astype(F32) + stage_in[base + index, 0:size, :].astype(F32)
            stage[base + index, 0:size, :] = value.astype(BF)
        return (stage.at[base + len(rest) - 1, pl.ds(0, size)] if rest else source), copies

    def dp_view(ref):
        return lambda m: ref.at[pl.ds(pl.multiple_of((group ^ data.shift(m)[0]) * piece, piece), piece)]

    def out_view(mask):
        d, _ = pairs.shift(mask)
        return o_out.at[pl.ds(pl.multiple_of(((group ^ d) % 4) * quarter, quarter), quarter)]

    out_base = 2 * groups + quad.count

    def rows_end(s):
        at = slice(s * share, (s + 1) * share)
        for item in range(1, ranks):
            place = turned_rows.at[rank ^ item, pl.ds(s * share, share)]
            remote(
                place, place, t_send.at[s * ranks + item], t_recv.at[s * ranks + item], {"tensor": rank ^ item}
            ).wait_recv()
        total = g1[at, :]
        for r in range(ranks):
            begin = at_qkv + r * 3 * columns
            total = total + dot(turned_rows[r, at, :], pool[begin : begin + 3 * columns, :])
        unit[at, :] = total

    back_in.wait()
    rows_end(0)
    give_up.level(last_t - 1)
    give_down.level(last_t)
    qkv_grad(1)

    part = many // 2
    at_mine = pl.ds(pl.multiple_of((group % 2) * part, part), part)
    at_other = pl.ds(pl.multiple_of((1 - group % 2) * part, part), part)
    near = {"dp": group ^ all_d[-1]}
    qkv_low[0] = qkv_sum[:, at_other, :].astype(BF)
    qkv_copies = [remote(qkv_low.at[0], qkv_in.at[0], q_send.at[0], q_recv.at[0], near)]
    qkv_copies[0].start()
    for index, step in enumerate(far_d):
        slot = 1 + index
        qkv_copies.append(
            remote(qkv_low.at[slot], qkv_in.at[slot], q_send.at[slot], q_recv.at[slot], {"dp": group ^ step})
        )
    qkv_last = len(far_d) + 1
    qkv_own = qkv_low.at[qkv_last]
    qkv_copies.append(remote(qkv_own, o_qkv.at[:, at_mine], q_send.at[qkv_last], q_recv.at[qkv_last], near))

    wc_own, wc_copies = settle_stage(0, give_wc.view(0), flat)
    wc_take = Gather(quad, quarters(o_wc, flat), f_send, f_recv, groups, own=wc_own)
    wc_take.start()
    wc_copy = load(wc_own, wc_take.view(0))
    qkv_copies[0].wait_recv()
    sum_half = qkv_sum[:, at_mine, :].astype(BF).astype(F32) + qkv_in[0].astype(F32)
    qkv_low[1] = sum_half.astype(BF)
    qkv_copies[1].start()
    for level in reversed(range(last_t - 1)):
        give_up.level(level)
    up_own = give_up.view(0)
    up_take = Gather(data, dp_view(o_up), f_send, f_recv, out_base + 4, own=up_own)
    up_take.start()
    up_copy = load(up_own, up_take.view(0))
    give_out.level(quad_top - 1)
    for mask in range(1, ranks // 2):
        wc_take.arrive(mask)
    give_down.level(last_t - 1)
    give_out.level(last_t)
    for index in range(len(far_d)):
        qkv_copies[1 + index].wait_recv()
        qkv_low[2 + index] = (qkv_low[1 + index].astype(F32) + qkv_in[1 + index].astype(F32)).astype(BF)
        qkv_copies[index + 2].start()
    qkv_local = load(qkv_own, o_qkv.at[:, at_mine])
    for mask in range(ranks // 2, quad.count):
        wc_take.arrive(mask)
    for level in reversed(range(last_t - 1)):
        give_down.level(level)
    down_own = give_down.view(0)
    down_take = Gather(data, dp_view(o_down), f_send, f_recv, groups + quad.count, own=down_own)
    down_take.start()
    down_copy = load(down_own, down_take.view(0))
    give_out.level(last_t - 1)
    rows_end(1)
    tokens_copy = load(unit, o_tokens)
    for level in reversed(range(last_t - 1)):
        give_out.level(level)
    out_own, out_copies = settle_stage(1, give_out.view(0), quarter)
    out_take = Gather(pairs, out_view, f_send, f_recv, out_base, own=out_own)
    out_take.start()
    out_copy = load(out_own, out_view(0))
    for taking in (small_take, down_take, up_take):
        for mask in range(1, groups):
            taking.arrive(mask)
    for mask in range(1, 4):
        out_take.arrive(mask)
    at_theirs = o_qkv.at[:, at_other]
    remote(at_theirs, at_theirs, q_send.at[qkv_last], q_recv.at[qkv_last], near).wait_recv()
    for move in [give_wc, give_out, give_down, give_up, small_take, wc_take, down_take, up_take, out_take] + gives:
        move.finish()
    for copy in sends + small_copies + qkv_copies + wc_copies + out_copies:
        copy.wait_send()
    for copy in (tokens_copy, small_copy, wc_copy, down_copy, qkv_local, out_copy, up_copy):
        copy.wait()


def backward(len_q, len_p, grad_vec, unit, low, scales, normals, w_colbert, down, up, slope, active, normed, out_all,
             context_rows, query, key, value, lse, queries, passages, qkv_all, gain):
    groups, ranks = lax.axis_size("dp"), lax.axis_size("tensor")
    all_t, all_d = steps_of(ranks), steps_of(groups)
    span, width = queries.shape
    columns = query.shape[2]
    heads = columns // HEAD_DIM
    share = span // ranks
    units = up.shape[0]
    piece = units // ranks
    rows = groups * share
    quarter, flat = columns // 4, width // ranks // 4
    pool = max(2 * units + 4 * rows, 2 * span + 3 * columns * ranks)
    many = width + 32
    far = len(all_d) - 1
    dma = pltpu.SemaphoreType.DMA
    vmem = pltpu.VMEM
    hold, leave = pl.BlockSpec(memory_space=pltpu.VMEM), pl.BlockSpec(memory_space=pl.ANY)
    shapes = [
        ((2 * share, width), F32),
        ((units // ranks * groups, width), BF),
        ((units // ranks * groups, width), BF),
        ((columns, width), BF),
        ((width, width), BF),
        ((3, many, columns), BF),
        ((groups, 8, width), F32),
    ]
    smem = pl.BlockSpec(memory_space=pltpu.SMEM)
    rest = max(1, len(all_d) - 2)

    def pair(count):
        return [dma((count,)), dma((count,))]

    return pl.pallas_call(
        functools.partial(backward_kernel, all_t, all_d),
        out_shape=[jax.ShapeDtypeStruct(*item) for item in shapes],
        in_specs=[smem, smem] + [leave] * 20 + [hold],
        out_specs=[leave] * len(shapes),
        scratch_shapes=[
            vmem((pool, width), BF),
            vmem((2 * rows, units), BF),
            vmem((2 * rows, units), BF),
            vmem((ranks * columns, width), BF),
            vmem((width, width), BF),
            vmem((ranks, 2 * share, columns), BF),
            vmem((2, span, columns), BF),
            vmem((2, span, columns), BF),
            vmem((2, span, columns), BF),
            vmem((2, heads, span), F32),
            vmem((2 * share, width), F32),
            vmem((2 * share, width), F32),
            vmem((2 * share, width), BF),
            vmem((2 * share, width), BF),
            vmem((2, 2 * share, width), F32),
            vmem((3, 2 * share, 128), F32),
            vmem((2, rows, width), F32),
            vmem((2, groups - 1, share, width), BF),
            vmem((2, groups - 1, share, width), BF),
            vmem((2 * share, width), BF),
            vmem((ranks, 2 * share, columns), BF),
            vmem((2, span, columns), BF),
            vmem((2, span, 3 * columns), BF),
            vmem((ranks, 2 * share, 3 * columns), BF),
            vmem((span, columns), F32),
            vmem((span, columns), F32),
            vmem((units, width), BF),
            vmem((ranks - 1, piece, width), BF),
            vmem((units, width), BF),
            vmem((ranks - 1, piece, width), BF),
            vmem((4 * ranks - 1, quarter, width), BF),
            vmem((4 * ranks - 1, flat, width), BF),
            vmem((3, many, columns), F32),
            vmem((2 + far, 3, many // 2, columns), BF),
            vmem((1 + far, 3, many // 2, columns), BF),
            vmem((len(all_t) + 1, 8, width), F32),
            vmem((len(all_t), 8, width), F32),
            vmem((2 * rest, max(quarter, flat), width), BF),
            vmem((2 * rest, max(quarter, flat), width), BF),
            dma((32,)),
        ]
        + pair(2 * groups)
        + pair(2 * groups)
        + pair(ranks)
        + pair(ranks)
        + pair(4 * ranks)
        + pair(4 * ranks)
        + pair(2 * ranks)
        + pair(2 * ranks)
        + pair(3 * groups + 4 * ranks + 4)
        + pair(len(all_t))
        + pair(2 * rest)
        + pair(2 + far),
        compiler_params=pltpu.CompilerParams(
            collective_id=3, has_side_effects=True, vmem_limit_bytes=62 * 2**20
        ),
        cost_estimate=pl.CostEstimate(flops=10**11, bytes_accessed=40 * 2**20, transcendentals=2**22),
        name="backward",
    )(len_q, len_p, grad_vec, unit, low, scales, normals, w_colbert, down, up, slope, active, normed, out_all,
      context_rows, query, key, value, lse, queries, passages, qkv_all, gain)


def finish_kernel(
    rank_of, low, tokens, down, up, out, wc, qkv, small,
    out_q, out_p, tok_q, tok_p, g_qkv, g_bias, g_out, g_up, g_in, g_down, g_gain, g_shift, g_offset, g_wc,
    v_low, v_tokens, v_down, v_up, v_out, v_wc, v_qkv, f_down, f_up, f_out, f_wc, f_qkv, load, store,
):
    share, width = out_q.shape
    copies = []

    def begin(src, dst, sem):
        copy = pltpu.make_async_copy(src, dst, sem)
        copy.start()
        return copy

    loads = [
        begin(src, dst, load.at[index])
        for index, (src, dst) in enumerate(
            ((down, v_down), (up, v_up), (wc, v_wc), (qkv, v_qkv), (out, v_out), (low, v_low), (tokens, v_tokens))
        )
    ]
    loads[0].wait()
    f_down[...] = v_down[...].astype(F32)
    copies.append(begin(f_down, g_down, store.at[4]))
    loads[1].wait()
    f_up[...] = v_up[...].astype(F32).T
    copies.append(begin(f_up, g_up, store.at[5]))
    loads[2].wait()
    f_wc[...] = v_wc[...].astype(F32)
    copies.append(begin(f_wc, g_wc, store.at[6]))
    loads[3].wait()
    f_qkv[...] = v_qkv[:, 0:width, :].astype(F32)
    copies.append(begin(f_qkv, g_qkv, store.at[7]))
    g_bias[0:1, :] = v_qkv[0, width : width + 16, :].astype(F32)[0:1, :]
    g_bias[1:2, :] = v_qkv[2, width : width + 16, :].astype(F32)[0:1, :]
    loads[4].wait()
    f_out[...] = v_out[...].astype(F32)
    copies.append(begin(f_out, g_out, store.at[8]))
    groups = small.shape[0]
    total = small[0]
    for index in range(1, groups):
        total = total + small[index]
    g_gain[...] = total[0:2]
    g_shift[...] = total[2:4]
    g_offset[...] = total[4:7]
    piece = g_in.shape[1]
    for index in range(groups):
        if piece % 128 == 0:
            at = pl.ds(pl.multiple_of(rank_of[0] * piece, piece), piece)
            g_in[index : index + 1, :] = small[index, 7:8, at]
    loads[5].wait()
    copies.append(begin(v_low.at[pl.ds(0, share)], out_q, store.at[0]))
    copies.append(begin(v_low.at[pl.ds(share, share)], out_p, store.at[1]))
    loads[6].wait()
    copies.append(begin(v_tokens.at[pl.ds(0, share)], tok_q, store.at[2]))
    copies.append(begin(v_tokens.at[pl.ds(share, share)], tok_p, store.at[3]))
    for copy in copies:
        copy.wait()


def finish(low, tokens, down, up, out, wc, qkv, small, piece):
    share, width = low.shape[0] // 2, low.shape[1]
    hidden, columns = down.shape[0], out.shape[0]
    groups = small.shape[0]
    hold, leave = pl.BlockSpec(memory_space=pltpu.VMEM), pl.BlockSpec(memory_space=pl.ANY)
    rank_of = lax.axis_index("tensor").reshape(1).astype(jnp.int32)
    shapes = [
        ((share, width), BF),
        ((share, width), BF),
        ((share, width), F32),
        ((share, width), F32),
        ((3, width, columns), F32),
        ((2, columns), F32),
        ((columns, width), F32),
        ((width, hidden), F32),
        ((groups, piece), F32),
        ((hidden, width), F32),
        ((2, width), F32),
        ((2, width), F32),
        ((3, width), F32),
        ((width, width), F32),
    ]
    vmem, dma = pltpu.VMEM, pltpu.SemaphoreType.DMA
    return pl.pallas_call(
        finish_kernel,
        out_shape=[jax.ShapeDtypeStruct(*item) for item in shapes],
        in_specs=[pl.BlockSpec(memory_space=pltpu.SMEM)] + [leave] * 7 + [hold],
        out_specs=[leave] * 5 + [hold, leave, leave, hold, leave, hold, hold, hold, leave],
        scratch_shapes=[
            vmem(low.shape, BF),
            vmem(tokens.shape, F32),
            vmem(down.shape, BF),
            vmem(up.shape, BF),
            vmem(out.shape, BF),
            vmem(wc.shape, BF),
            vmem(qkv.shape, BF),
            vmem(down.shape, F32),
            vmem((width, hidden), F32),
            vmem(out.shape, F32),
            vmem(wc.shape, F32),
            vmem((3, width, columns), F32),
            dma((7,)),
            dma((9,)),
        ],
        compiler_params=pltpu.CompilerParams(vmem_limit_bytes=62 * 2**20),
        name="finish",
    )(rank_of, low, tokens, down, up, out, wc, qkv, small)


def per_device(
    queries,
    passages,
    query_lengths,
    passage_lengths,
    w_qkv,
    qv_bias,
    w_out,
    w_in,
    in_bias,
    w_down,
    norm_gain,
    norm_shift,
    layer_bias,
    w_colbert,
    dense_cot,
    colbert_cot,
):
    groups, ranks = lax.axis_size("dp"), lax.axis_size("tensor")
    group, rank = lax.axis_index("dp"), lax.axis_index("tensor")
    width = queries.shape[1]
    columns = w_qkv.shape[2]
    piece = w_in.shape[1] // groups
    units = piece * ranks

    if piece % 128 == 0 and piece != w_in.shape[0]:
        up_piece = w_in
    else:
        up_piece = lax.dynamic_slice_in_dim(w_in, group * piece, piece, 1).T
    if columns % 128 == 0:
        qkv_piece = w_out
    else:
        slim = 3 * columns // 2
        turned = w_qkv.transpose(0, 2, 1).reshape(3 * columns, width)
        qkv_piece = lax.dynamic_slice_in_dim(turned, (group % 2) * slim, slim, 0)
    if piece % 128 == 0:
        bias_in = lax.dynamic_slice_in_dim(in_bias, group * piece, piece, 0)
        bias_in = jnp.broadcast_to(bias_in[None, :], (16, piece))
    else:
        bias_in = lax.all_gather(in_bias, "tensor").reshape(ranks, groups, piece)
        bias_in = lax.dynamic_index_in_dim(bias_in, group, 1, keepdims=False).reshape(1, -1).astype(F32)
    (
        query,
        key,
        value,
        lse,
        context_rows,
        out_all,
        up,
        down,
        qkv_all,
        normed,
        slope,
        active,
        normals,
        unit,
        low,
        scales,
        grad_vec,
    ) = forward(
        query_lengths, passage_lengths, dense_cot, colbert_cot, queries, passages, w_qkv, qv_bias, w_out, up_piece,
        w_down, qkv_piece, bias_in, norm_gain, norm_shift, layer_bias, w_colbert,
    )
    tokens, grad_down, grad_up, grad_out, colbert, grad_qkv, small = backward(
        query_lengths, passage_lengths, grad_vec, unit, low, scales, normals, w_colbert, down, up, slope, active,
        normed.reshape(-1, width), out_all.reshape(-1, width), context_rows, query, key, value, lse,
        queries, passages, qkv_all.reshape(-1, width), norm_gain,
    )
    results = list(finish(low, tokens, grad_down, grad_up, grad_out, colbert, grad_qkv, small, piece))
    if piece % 128:
        bias = small[:, 7, :units].reshape(groups, ranks, piece)
        results[8] = lax.dynamic_index_in_dim(bias, rank, 1, keepdims=False)
    results[8] = results[8].reshape(-1)
    return tuple(results)


def solution(mesh):
    both = P(("dp", "tensor"), None)
    return jax.shard_map(
        per_device,
        mesh=mesh,
        in_specs=(
            P("dp", None),
            P("dp", None),
            P(),
            P(),
            P(None, None, "tensor"),
            P(None, "tensor"),
            P("tensor", None),
            P(None, "tensor"),
            P("tensor"),
            P("tensor", None),
            P(),
            P(),
            P(),
            P(),
            P(),
            P(),
        ),
        out_specs=(
            both,
            both,
            both,
            both,
            P(None, None, "tensor"),
            P(None, "tensor"),
            P("tensor", None),
            P(None, "tensor"),
            P("tensor"),
            P("tensor", None),
            P(),
            P(),
            P(),
            P(),
        ),
        check_vma=False,
    )
```

```python
import functools

import jax
import jax.numpy as jnp
from jax import lax
from jax.experimental import pallas as pl
from jax.experimental.pallas import tpu as pltpu
from jax.sharding import PartitionSpec as P

HEAD_DIM = 64
BF = jnp.bfloat16
F32 = jnp.float32
BLOCK = 256


def dot(left, right):
    return jnp.dot(left, right, preferred_element_type=F32)


def inner_rows(left, right):
    return lax.dot_general(left, right, (((1,), (1,)), ((), ())), preferred_element_type=F32)


def outer_rows(left, right):
    return lax.dot_general(left, right, (((0,), (0,)), ((), ())), preferred_element_type=F32)


def steps_of(size):
    steps = []
    while size > 1:
        size //= 2
        steps.append(size)
    return steps


def offsets(steps):
    found = [0]
    for step in steps:
        found = found + [item ^ step for item in found]
    return found


def swap(value, axis, step):
    size = lax.axis_size(axis)
    return lax.ppermute(value, axis, [(index, index ^ step) for index in range(size)])


def spread(value, axis, steps):
    held = value[None]
    for step in steps:
        held = jnp.concatenate([held, swap(held, axis, step)], axis=0)
    return held


def fold(parts, axis, steps):
    for step in reversed(steps):
        half = parts.shape[0] // 2
        came = swap(parts[half:].astype(BF), axis, step)
        parts = parts[:half].astype(F32) + came.astype(F32)
    return parts[0]


def natural(parts, axis, steps, dim=0):
    order = offsets(steps)
    size = len(order)
    place = [0] * size
    for spot, item in enumerate(order):
        place[item] = spot
    table = jnp.array(place, jnp.int32)
    rank = lax.axis_index(axis)
    return jnp.concatenate(
        [lax.dynamic_slice_in_dim(parts, table[item ^ rank], 1, dim) for item in range(size)], axis=dim
    )


def xored(parts, axis, steps, dim=0):
    rank = lax.axis_index(axis)
    return jnp.concatenate(
        [lax.dynamic_slice_in_dim(parts, item ^ rank, 1, dim) for item in offsets(steps)], axis=dim
    )


def trade(parts, steps, dim):
    rank = lax.axis_index("tensor")
    got = []
    for item in offsets(steps):
        piece = lax.dynamic_index_in_dim(parts, item ^ rank, dim, keepdims=False)
        got.append(swap(piece, "tensor", item) if item else piece)
    return got


def layer_norm(hidden, gain, shift):
    centre = hidden - jnp.mean(hidden, axis=-1, keepdims=True)
    inverse = lax.rsqrt(jnp.mean(centre * centre, axis=-1, keepdims=True) + 1e-05)
    normal = centre * inverse
    return (normal * gain + shift, normal, inverse)


def norm_back(grad, normal, inverse, gain):
    scaled = grad * gain
    middle = (
        scaled
        - jnp.mean(scaled, axis=-1, keepdims=True)
        - normal * jnp.mean(scaled * normal, axis=-1, keepdims=True)
    )
    return (middle * inverse, jnp.sum(grad * normal, axis=0), jnp.sum(grad, axis=0))


def gelu_slope(inner):
    return (
        0.5 * (1.0 + lax.erf(inner * 0.7071067811865476))
        + inner * jnp.exp(-0.5 * inner * inner) * 0.3989422804014327
    )


def head_mask(columns, head):
    lane = lax.broadcasted_iota(jnp.int32, (1, columns), 1)
    return (lane >= head * HEAD_DIM) & (lane < (head + 1) * HEAD_DIM)


MESH = pl.DeviceIdType.MESH


class Lattice:
    def __init__(self, steps):
        self.steps = steps
        self.count = 1 << len(steps)

    def peer(self, level):
        axis, step = self.steps[level]
        return {axis: lax.axis_index(axis) ^ step}

    def index(self, mask):
        found = 0
        for level, (axis, step) in enumerate(self.steps):
            bit = (lax.axis_index(axis) // step) % 2
            found = found + (1 - bit if mask >> level & 1 else bit) * (1 << level)
        return found

    def member(self, axis, block):
        found = lax.axis_index(axis)
        for level, (name, step) in enumerate(self.steps):
            if name == axis:
                found = found + ((block // (1 << level)) % 2 - (lax.axis_index(axis) // step) % 2) * step
        return found

    def shift(self, mask):
        found = {"dp": 0, "tensor": 0}
        for level, (axis, step) in enumerate(self.steps):
            if mask >> level & 1:
                found[axis] ^= step
        return found["dp"], found["tensor"]


def remote(src, dst, send, recv, peer):
    return pltpu.make_async_remote_copy(
        src_ref=src, dst_ref=dst, send_sem=send, recv_sem=recv, device_id=peer, device_id_type=MESH
    )


class Gather:
    def __init__(self, lattice, view, send, recv, base=0, own=None):
        self.lattice, self.view, self.send, self.recv, self.base = lattice, view, send, recv, base
        self.own = own
        self.sent = []

    def copy(self, level, mask):
        slot = self.base + (1 << level) + mask
        place = self.view(mask)
        src = self.own if mask == 0 and self.own is not None else place
        return remote(src, place, self.send.at[slot], self.recv.at[slot], self.lattice.peer(level))

    def start(self, levels=None):
        for level in range(len(self.lattice.steps)) if levels is None else levels:
            copy = self.copy(level, 0)
            copy.start()
            self.sent.append(copy)

    def arrive(self, mask):
        level = mask.bit_length() - 1
        slot = self.base + mask
        place = self.view(mask)
        remote(place, place, self.send.at[slot], self.recv.at[slot], self.lattice.peer(level)).wait_recv()
        for later in range(level + 1, len(self.lattice.steps)):
            copy = self.copy(later, mask)
            copy.start()
            self.sent.append(copy)

    def finish(self):
        for copy in self.sent:
            copy.wait_send()


class Scatter:
    def __init__(self, lattice, read, write, out, came, send, recv, base=0):
        self.lattice, self.read, self.write = lattice, read, write
        self.out, self.came, self.send, self.recv, self.base = out, came, send, recv, base
        self.sent = []

    def push(self, mask):
        level = mask.bit_length() - 1
        slot = self.base + mask
        copy = remote(
            self.out.at[mask - 1],
            self.came.at[mask - 1],
            self.send.at[slot],
            self.recv.at[slot],
            self.lattice.peer(level),
        )
        copy.start()
        self.sent.append(copy)

    def put(self, mask):
        self.out[mask - 1] = self.read(mask).astype(BF)
        self.push(mask)

    def level(self, level):
        for mask in reversed(range(1 << level)):
            slot = (1 << level) + mask
            place = self.came.at[slot - 1]
            remote(
                self.out.at[slot - 1],
                place,
                self.send.at[self.base + slot],
                self.recv.at[self.base + slot],
                self.lattice.peer(level),
            ).wait_recv()
            total = self.read(mask) + self.came[slot - 1].astype(F32)
            if mask and mask >= 1 << (level - 1):
                self.out[mask - 1] = total.astype(BF)
                self.push(mask)
            else:
                self.write(mask, total)

    def run(self):
        for level in reversed(range(len(self.lattice.steps))):
            self.level(level)

    def finish(self):
        for copy in self.sent:
            copy.wait_send()


def score_steps(all_t, all_d):
    if len(all_d) <= 2:
        rows_q = [("tensor", step) for step in all_t[:-2]] + [("dp", step) for step in all_d]
        rows_p = [("tensor", step) for step in all_t[-2:]]
    else:
        rows_q = [("tensor", step) for step in all_t[:-1]] + [("dp", step) for step in all_d[-1:]]
        rows_p = [("dp", step) for step in all_d[:-1]] + [("tensor", step) for step in all_t[-1:]]
    return rows_q, rows_p


def score_peers(all_t, rows_p):
    return [item for item in offsets([step for step in all_t if ("tensor", step) not in rows_p]) if item]


def greet(peers):
    barrier = pltpu.get_barrier_semaphore()
    for peer in peers:
        pl.semaphore_signal(barrier, inc=1, device_id=peer, device_id_type=MESH)
    pl.semaphore_wait(barrier, len(peers))


def forward_kernel(
    all_t, all_d, ship_bias,
    len_q, len_p, dense_cot, late_cot,
    x_q, x_p, w_qkv, qv_bias, w_out, up_piece, w_down, qkv_piece, bias_in, gain, shift, offset, w_colbert,
    o_q, o_k, o_v, o_lse, o_ctx, o_out, o_up, o_down, o_qkv, o_normed, o_slope, o_active,
    o_normal, o_unit, o_low, o_spread, o_grad,
    x, q, k, v, ctx, lse, ctx_rows, out_all, up, down, normed, slope, active, sums, s_out, s_in,
    first, normal, unit, vec, low, scales, wc, bias_all, bias_row, w_cols, w_turn,
    rows_q, rows_p, raised, pull, mass, mass_in, out_q, in_q, sum_p, out_p, in_p, grad,
    local, g_send, g_recv, a_send, a_recv, b_send, b_recv, n_send, n_recv, r_send, r_recv,
    gq_send, gq_recv, gp_send, gp_recv, m_send, m_recv, rq_send, rq_recv, rp_send, rp_recv,
):
    group, rank = lax.axis_index("dp"), lax.axis_index("tensor")
    ranks, groups = 1 << len(all_t), 1 << len(all_d)
    span, width = x_q.shape
    columns = w_qkv.shape[2]
    share = span // ranks
    units = up.shape[0]
    piece = units // ranks
    turn_up, turn_qkv = up_piece.shape[0] != piece, qkv_piece.shape[0] != 3 * columns // 2
    quarter = columns // 4
    rows = groups * share
    heads = columns // HEAD_DIM
    scale = HEAD_DIM**-0.5

    x_copies = [pltpu.make_async_copy(src, x.at[s], local.at[s]) for s, src in enumerate((x_q, x_p))]
    for copy in x_copies:
        copy.start()
    if turn_up:
        up_copy = pltpu.make_async_copy(
            up_piece.at[:, pl.ds(pl.multiple_of(group * piece, piece), piece)], w_cols, local.at[4]
        )
        up_copy.start()
    wc_copy = pltpu.make_async_copy(w_colbert, wc, local.at[2])
    wc_copy.start()
    greet([{"tensor": rank ^ item} for item in range(1, ranks)] + [{"dp": group ^ item} for item in all_d])

    tensor = Lattice([("tensor", step) for step in all_t])
    quad = Lattice([("tensor", step) for step in all_t] + [("dp", step) for step in all_d[-2:]])
    data = Lattice([("dp", step) for step in all_d])

    def quarters(ref, size):
        def view(mask):
            d, t = quad.shift(mask)
            return ref.at[rank ^ t, pl.ds(pl.multiple_of(((group ^ d) % 4) * size, size), size)]

        return view

    def unit_rows(ref):
        return lambda mask: ref.at[pl.ds(pl.multiple_of((rank ^ tensor.shift(mask)[1]) * piece, piece), piece)]

    wide, tall = quad.count, tensor.count
    far, near = list(range(len(all_t) - 1)), [len(all_t) - 1]
    at_quarter = pl.ds(pl.multiple_of((group % 4) * quarter, quarter), quarter)
    at_piece = pl.ds(pl.multiple_of(group * piece, piece), piece)
    take_out = Gather(quad, quarters(out_all, quarter), g_send, g_recv, 0, own=w_out.at[at_quarter])
    take_up = Gather(tensor, unit_rows(up), g_send, g_recv, wide, own=None if turn_up else up_piece)
    take_down = Gather(tensor, unit_rows(down), g_send, g_recv, wide + tall, own=w_down.at[at_piece])
    cores = Lattice([("tensor", step) for step in all_t] + [("dp", all_d[-1])])
    slab = 3 * columns // 2
    qkv_own = w_turn.at[pl.ds(pl.multiple_of((group % 2) * slab, slab), slab)] if turn_qkv else qkv_piece

    def slab_view(mask):
        d, t = cores.shift(mask)
        return o_qkv.at[rank ^ t, pl.ds(pl.multiple_of(((group ^ d) % 2) * slab, slab), slab)]

    take_qkv = Gather(cores, slab_view, g_send, g_recv, wide + 2 * tall, own=qkv_own)
    own_copies = [
        pltpu.make_async_copy(w_out.at[at_quarter], take_out.view(0), local.at[3]),
        pltpu.make_async_copy(w_down.at[at_piece], take_down.view(0), local.at[5]),
    ]
    if not turn_up:
        own_copies.append(pltpu.make_async_copy(up_piece, take_up.view(0), local.at[4]))
    early = [tall // 4] + list(range(1, tall // 4))
    late = list(range(tall // 4 + 1, tall // 2))
    take_out.start()
    if turn_up:
        up_copy.wait()
        take_up.view(0)[...] = w_cols[...].T
    take_up.start(near)
    for copy in own_copies:
        copy.start()
    pending = []
    bias_copies = []
    if ship_bias:
        bias_all[rank] = bias_in[...]
        for item in range(1, ranks):
            copy = remote(
                bias_in, bias_all.at[rank], b_send.at[item], b_recv.at[item], {"tensor": rank ^ item}
            )
            copy.start()
            bias_copies.append(copy)

    lengths = (len_q[group], len_p[group])
    def project(s):
        x_copies[s].wait()
        tokens = x[s]
        q[s] = (dot(tokens, w_qkv[0]) + qv_bias[0:1, :].astype(F32)).astype(BF)
        k[s] = dot(tokens, w_qkv[1]).astype(BF)
        v[s] = (dot(tokens, w_qkv[2]) + qv_bias[1:2, :].astype(F32)).astype(BF)

    block = min(BLOCK, span)

    def attention(s, begin, end):
        keep = lax.broadcasted_iota(jnp.int32, (1, span), 1) < lengths[s]

        @pl.loop(begin, end)
        def _(index):
            at = pl.ds(pl.multiple_of(index * block, block), block)
            query = q[s, at, :]
            total = jnp.zeros((block, columns), F32)
            for head in range(heads):
                mask = head_mask(columns, head)
                mine = jnp.where(mask, query, jnp.zeros_like(query)) * jnp.asarray(scale, BF)
                scores = jnp.where(keep, inner_rows(mine, k[s]), -1e30)
                top = jnp.max(scores, axis=-1, keepdims=True)
                weight = jnp.exp(scores - top)
                amount = jnp.sum(weight, axis=-1, keepdims=True)
                part = dot(weight.astype(BF), v[s]) / amount
                total = jnp.where(mask, part, total)
                column = jnp.broadcast_to(top + jnp.log(amount), (block, 128))
                lse[s, head : head + 1, at] = column.T[0:1, :]
            ctx[s, at, :] = total.astype(BF)

    sends = []

    def trade_context(s):
        at = pl.ds(s * share, share)
        for item in range(1, ranks):
            peer = rank ^ item
            copy = remote(
                ctx.at[s, pl.ds(pl.multiple_of(peer * share, share), share)],
                ctx_rows.at[rank, at],
                a_send.at[s * ranks + item],
                a_recv.at[s * ranks + item],
                {"tensor": peer},
            )
            copy.start()
            sends.append(copy)
        ctx_rows[rank, s * share : (s + 1) * share, :] = ctx[s, pl.ds(pl.multiple_of(rank * share, share), share), :]

    def context_here(s):
        at = pl.ds(s * share, share)
        for item in range(1, ranks):
            place = ctx_rows.at[rank ^ item, at]
            remote(
                place, place, a_send.at[s * ranks + item], a_recv.at[s * ranks + item], {"tensor": rank ^ item}
            ).wait_recv()

    def out_going(src, dst, index):
        copy = pltpu.make_async_copy(src, dst, local.at[index])
        copy.start()
        pending.append(copy)

    def arrive(taking, masks):
        for mask in masks:
            taking.arrive(mask)

    count = span // block
    take_down.start(near)
    project(0)
    arrive(take_out, early)
    take_up.start(far)
    arrive(take_out, late)
    attention(0, 0, count)
    trade_context(0)
    for copy in own_copies:
        copy.wait()
    project(1)
    arrive(take_up, early[:1])
    attention(1, 0, count // 2)
    arrive(take_up, early[1:])
    attention(1, count // 2, count)
    take_down.start(far)
    arrive(take_out, range(tall // 2, wide))
    if turn_qkv:
        for i in range(3):
            w_turn[i * columns : (i + 1) * columns, :] = w_qkv[i].T
    arrive(take_up, late)
    trade_context(1)
    out_going(q, o_q, 7)
    out_going(k, o_k, 8)
    out_going(v, o_v, 9)
    out_going(lse, o_lse, 10)

    def to_rows(s):
        at = slice(s * share, (s + 1) * share)
        context_here(s)
        if columns % 128 == 0:
            mix = jnp.concatenate([ctx_rows[r, at, :] for r in range(ranks)], axis=1)
            mixed = dot(mix, out_all[...].reshape(ranks * columns, width))
        else:
            mixed = dot(ctx_rows[0, at, :], out_all[0])
            for r in range(1, ranks):
                mixed = mixed + dot(ctx_rows[r, at, :], out_all[r])
        mine = x[s, pl.ds(pl.multiple_of(rank * share, share), share), :].astype(F32)
        value, plain, inverse = layer_norm(mine + mixed + offset[0:1, :], gain[0:1, :], shift[0:1, :])
        first[at, :] = value
        normal[0, at, :] = plain
        scales[0, at, :] = jnp.broadcast_to(inverse, (share, 128))
        normed[s, pl.ds(pl.multiple_of(group * share, share), share), :] = value.astype(BF)

        def view(mask):
            d, _ = data.shift(mask)
            return normed.at[s, pl.ds(pl.multiple_of((group ^ d) * share, share), share)]

        taking = Gather(data, view, n_send, n_recv, s * groups)
        taking.start()
        return taking

    normed_takes = [to_rows(0)]
    arrive(take_down, early)
    normed_takes.append(to_rows(1))
    arrive(take_up, range(tall // 2, tall))
    arrive(take_down, late)
    take_qkv.start()
    out_going(qkv_own, take_qkv.view(0), 6)
    if ship_bias:
        for item in range(1, ranks):
            place = bias_all.at[rank ^ item]
            remote(place, place, b_send.at[item], b_recv.at[item], {"tensor": rank ^ item}).wait_recv()
        for r in range(ranks):
            bias_row[0:1, r * piece : (r + 1) * piece] = bias_all[r, 0:1, :].astype(F32)
    else:
        bias_row[0:1, :] = bias_in[0:1, :]
    arrive(normed_takes[0], range(1, groups))

    def spot(mask):
        return pl.multiple_of((group ^ data.shift(mask)[0]) * share, share)

    gives = []
    for s in range(2):

        def read(mask, s=s):
            return sums[pl.ds(s * rows + spot(mask), share), :]

        def write(mask, value, s=s):
            sums[pl.ds(s * rows + spot(mask), share), :] = value

        gives.append(Scatter(data, read, write, s_out.at[s], s_in.at[s], r_send, r_recv, s * groups))

    tile = min(512, units)

    def expand(s):
        at_rows = slice(s * rows, (s + 1) * rows)

        @pl.loop(0, units // tile)
        def _(index):
            at = pl.ds(pl.multiple_of(index * tile, tile), tile)
            value = inner_rows(normed[s], up[at, :]) + bias_row[0:1, at]
            phi = 0.5 * (1.0 + lax.erf(value * 0.7071067811865476))
            active[at_rows, at] = (value * phi).astype(BF)
            slope[at_rows, at] = (phi + value * jnp.exp(-0.5 * value * value) * 0.3989422804014327).astype(BF)

    def reduce(s):
        at_rows = slice(s * rows, (s + 1) * rows)

        @pl.loop(0, width // 512)
        def _(index):
            at = pl.ds(pl.multiple_of(index * 512, 512), 512)
            sums[at_rows, at] = dot(active[at_rows, :], down[:, at])

        for mask in reversed(range(groups // 2, groups)):
            gives[s].put(mask)

    top = len(all_d) - 1
    expand(0)
    arrive(normed_takes[1], range(1, groups))
    expand(1)
    arrive(take_down, range(tall // 2, tall))
    reduce(0)
    arrive(take_qkv, early)
    reduce(1)
    gives[0].level(top)
    out_going(ctx_rows, o_ctx, 11)
    out_going(out_all, o_out, 12)
    out_going(up, o_up, 13)
    out_going(down, o_down, 14)
    out_going(normed, o_normed, 15)
    out_going(slope, o_slope, 16)
    out_going(active, o_active, 17)
    gives[1].level(top)
    wc_copy.wait()

    steps_q, steps_p = score_steps(all_t, all_d)
    lattice_q, lattice_p = Lattice(steps_q), Lattice(steps_p)
    levels_y = [level for level, (axis, _) in enumerate(steps_p) if axis == "dp"]
    count_y = 1 << len(levels_y)

    def spot_q(mask):
        return pl.multiple_of(lattice_q.index(mask) * share, share)

    def spot_p(mask):
        return pl.multiple_of(lattice_p.index(mask) * share, share)

    takes = (
        Gather(lattice_q, lambda m: rows_q.at[pl.ds(spot_q(m), share)], gq_send, gq_recv, own=vec.at[pl.ds(0, share)]),
        Gather(
            lattice_p, lambda m: rows_p.at[pl.ds(spot_p(m), share)], gp_send, gp_recv, own=vec.at[pl.ds(share, share)]
        ),
    )
    for s in range(2):
        at = slice(s * share, (s + 1) * share)
        for level in reversed(range(top)):
            gives[s].level(level)
        feed = gives[s].read(0)
        value, plain, inverse = layer_norm(first[at, :] + feed + offset[1:2, :], gain[1:2, :], shift[1:2, :])
        short = value.astype(BF)
        place = lax.broadcasted_iota(jnp.int32, (share, 1), 0) + rank * share
        chosen = jnp.where(place == 0, value, dot(short, wc[...]) + offset[2:3, :])
        norm = lax.rsqrt(jnp.sum(chosen * chosen, axis=-1, keepdims=True) + 1e-06)
        chosen = chosen * norm
        vec[at, :] = chosen.astype(BF)
        takes[s].start()
        unit[at, :] = chosen
        normal[1, at, :] = plain
        scales[1, at, :] = jnp.broadcast_to(inverse, (share, 128))
        scales[2, at, :] = jnp.broadcast_to(norm, (share, 128))
        low[at, :] = short
    rows_q[pl.ds(spot_q(0), share), :] = vec[0:share, :]
    rows_p[pl.ds(spot_p(0), share), :] = vec[share : 2 * share, :]
    take_q, take_p = takes
    many_q, many_p = lattice_q.count * share, lattice_p.count * share
    half_q, half_p = many_q // 2, many_p // 2
    arrive(take_q, range(1, lattice_q.count // 4))
    arrive(take_p, range(1, lattice_p.count // 2))
    arrive(take_q, [lattice_q.count // 4])
    arrive(take_q, range(lattice_q.count // 4 + 1, lattice_q.count // 2))
    out_going(normal, o_normal, 18)
    out_going(unit, o_unit, 19)
    out_going(low, o_low, 20)
    out_going(scales, o_spread, 21)

    lane = lax.broadcasted_iota(jnp.int32, (1, many_q), 1)
    block_q = lane // share
    group_q = lattice_q.member("dp", block_q)
    place_q = lattice_q.member("tensor", block_q) * share + lane % share
    temper = float(width) ** 0.5
    which_y = [sum(((y >> i) & 1) << level for i, level in enumerate(levels_y)) for y in range(count_y)]
    late_rows, dense_rows = [], []
    for y in range(count_y):
        which = lattice_p.member("dp", which_y[y])
        length, late_row, dense_row = 0, 0.0, 0.0
        for g in range(groups):
            length = jnp.where(group_q == g, len_q[g], length)
            late_row = jnp.where(group_q == g, temper * late_cot[g, which], late_row)
            dense_row = jnp.where(group_q == g, 50.0 * dense_cot[g, which], dense_row)
        late_rows.append(jnp.where((place_q >= 1) & (place_q < length), late_row, 0.0))
        dense_rows.append(jnp.where(place_q == 0, dense_row, 0.0))
    arrive(take_q, range(lattice_q.count // 2, lattice_q.count))
    arrive(take_p, range(lattice_p.count // 2, lattice_p.count))
    arrive(take_qkv, late)

    def place_p(block):
        first_place = lattice_p.member("tensor", block) * share
        return first_place + lax.broadcasted_iota(jnp.int32, (share, 1), 0)

    def part_of(block):
        return sum(((block >> level) & 1) << i for i, level in enumerate(levels_y))

    mass[...] = jnp.zeros_like(mass)
    for block in range(lattice_p.count):
        at = slice(block * share, (block + 1) * share)
        y = part_of(block)
        dots = inner_rows(rows_p[at, :], rows_q[...])
        place = place_p(block)
        counted = (place >= 1) & (place < len_p[lattice_p.member("dp", block)])
        value = jnp.where(counted, jnp.exp(dots * temper - temper), 0.0)
        raised[at, :] = value
        mass[y : y + 1, :] += jnp.sum(value, axis=0, keepdims=True)
    mass_copies = []
    for index, item in enumerate(score_peers(all_t, steps_p)):
        copy = remote(mass, mass_in.at[index], m_send.at[index], m_recv.at[index], {"tensor": rank ^ item})
        copy.start()
        mass_copies.append(copy)
    total = mass[...]
    for index, copy in enumerate(mass_copies):
        copy.wait_recv()
        total = total + mass_in[index]
    for block in range(lattice_p.count):
        at = slice(block * share, (block + 1) * share)
        y = part_of(block)
        value = raised[at, :] * (late_rows[y] / total[y : y + 1, :])
        pull[at, :] = (value + jnp.where(place_p(block) == 0, dense_rows[y], 0.0)).astype(BF)

    mine_q = (lax.axis_index(steps_q[-1][0]) // steps_q[-1][1]) % 2
    mine_p = (lax.axis_index(steps_p[-1][0]) // steps_p[-1][1]) % 2

    def fill_q(half):
        at = pl.ds(pl.multiple_of(half * half_q, half_q), half_q)
        sums[at, :] = outer_rows(pull[:, at], rows_p[...])

    def fill_p(half):
        at = pl.ds(pl.multiple_of(half * half_p, half_p), half_p)
        sum_p[at, :] = dot(pull[at, :], rows_q[...])

    def reader(ref, find):
        return lambda m: ref[pl.ds(find(m), share), :]

    def writer(ref, find):
        def write(m, value):
            ref[pl.ds(find(m), share), :] = value

        return write

    give_q = Scatter(lattice_q, reader(sums, spot_q), writer(sums, spot_q), out_q, in_q, rq_send, rq_recv)
    give_p = Scatter(lattice_p, reader(sum_p, spot_p), writer(sum_p, spot_p), out_p, in_p, rp_send, rp_recv)
    fill_q(1 - mine_q)
    for mask in reversed(range(lattice_q.count // 2, lattice_q.count)):
        give_q.put(mask)
    fill_p(1 - mine_p)
    for mask in reversed(range(lattice_p.count // 2, lattice_p.count)):
        give_p.put(mask)
    fill_q(mine_q)
    arrive(take_qkv, range(tall // 2, tall))
    give_q.level(len(steps_q) - 1)
    fill_p(mine_p)
    give_p.level(len(steps_p) - 1)
    for level in reversed(range(len(steps_q) - 1)):
        give_q.level(level)
    for level in reversed(range(len(steps_p) - 1)):
        give_p.level(level)
    grad[0:share, :] = sums[pl.ds(spot_q(0), share), :]
    grad[share : 2 * share, :] = sum_p[pl.ds(spot_p(0), share), :]
    out_going(grad, o_grad, 22)
    arrive(take_qkv, range(tall, 2 * tall))
    for move in [take_out, take_up, take_down, take_qkv, take_q, take_p, give_q, give_p] + normed_takes + gives:
        move.finish()
    for copy in sends + bias_copies + mass_copies:
        copy.wait_send()
    for copy in pending:
        copy.wait()


def forward(len_q, len_p, dense_cot, late_cot, queries, passages, w_qkv, qv_bias, w_out, up_piece, w_down, qkv_piece,
            bias_in, gain, shift, offset, w_colbert):
    groups, ranks = lax.axis_size("dp"), lax.axis_size("tensor")
    all_t, all_d = steps_of(ranks), steps_of(groups)
    span, width = queries.shape
    columns = w_qkv.shape[2]
    heads = columns // HEAD_DIM
    share = span // ranks
    piece = w_down.shape[0] // groups
    units = piece * ranks
    rows = groups * share
    ship_bias = bias_in.shape[0] == 16
    steps_q, steps_p = score_steps(all_t, all_d)
    blocks_q, blocks_p = 1 << len(steps_q), 1 << len(steps_p)
    many_q, many_p, peers = blocks_q * share, blocks_p * share, len(score_peers(all_t, steps_p))

    shapes = [
        ((2, span, columns), BF),
        ((2, span, columns), BF),
        ((2, span, columns), BF),
        ((2, heads, span), F32),
        ((ranks, 2 * share, columns), BF),
        ((ranks, columns, width), BF),
        ((units, width), BF),
        ((units, width), BF),
        ((ranks, 3 * columns, width), BF),
        ((2, rows, width), BF),
        ((2 * rows, units), BF),
        ((2 * rows, units), BF),
        ((2, 2 * share, width), F32),
        ((2 * share, width), F32),
        ((2 * share, width), BF),
        ((3, 2 * share, 128), F32),
        ((2 * share, width), F32),
    ]
    dma = pltpu.SemaphoreType.DMA
    vmem = pltpu.VMEM
    hold, leave = pl.BlockSpec(memory_space=pltpu.VMEM), pl.BlockSpec(memory_space=pl.ANY)
    flat = pl.BlockSpec(memory_space=pltpu.SMEM)

    def pair(count):
        return [dma((count,)), dma((count,))]

    return pl.pallas_call(
        functools.partial(forward_kernel, all_t, all_d, ship_bias),
        out_shape=[jax.ShapeDtypeStruct(*item) for item in shapes],
        in_specs=[flat] * 4
        + [leave, leave, hold, hold, leave, leave, leave, leave, hold, hold, hold, hold, leave],
        out_specs=[leave] * len(shapes),
        scratch_shapes=[
            vmem((2, span, width), BF),
            vmem((2, span, columns), BF),
            vmem((2, span, columns), BF),
            vmem((2, span, columns), BF),
            vmem((2, span, columns), BF),
            vmem((2, heads, span), F32),
            vmem((ranks, 2 * share, columns), BF),
            vmem((ranks, columns, width), BF),
            vmem((units, width), BF),
            vmem((units, width), BF),
            vmem((2, rows, width), BF),
            vmem((2 * rows, units), BF),
            vmem((2 * rows, units), BF),
            vmem((2 * rows, width), F32),
            vmem((2, groups - 1, share, width), BF),
            vmem((2, groups - 1, share, width), BF),
            vmem((2 * share, width), F32),
            vmem((2, 2 * share, width), F32),
            vmem((2 * share, width), F32),
            vmem((2 * share, width), BF),
            vmem((2 * share, width), BF),
            vmem((3, 2 * share, 128), F32),
            vmem((width, width), BF),
            vmem((ranks, 16, piece), BF),
            vmem((8, units), F32),
            vmem((width, piece), BF),
            vmem((3 * columns, width) if columns % 128 == 0 else (16, 128), BF),
            vmem((many_q, width), BF),
            vmem((many_p, width), BF),
            vmem((many_p, many_q), F32),
            vmem((many_p, many_q), BF),
            vmem((8, many_q), F32),
            vmem((peers, 8, many_q), F32),
            vmem((blocks_q - 1, share, width), BF),
            vmem((blocks_q - 1, share, width), BF),
            vmem((many_p, width), F32),
            vmem((blocks_p - 1, share, width), BF),
            vmem((blocks_p - 1, share, width), BF),
            vmem((2 * share, width), F32),
            dma((23,)),
        ]
        + pair(8 * ranks)
        + pair(2 * ranks)
        + pair(ranks)
        + pair(2 * groups)
        + pair(2 * groups)
        + pair(blocks_q)
        + pair(blocks_p)
        + pair(peers)
        + pair(blocks_q)
        + pair(blocks_p),
        compiler_params=pltpu.CompilerParams(
            collective_id=2, has_side_effects=True, vmem_limit_bytes=62 * 2**20
        ),
        cost_estimate=pl.CostEstimate(flops=10**11, bytes_accessed=40 * 2**20, transcendentals=2**23),
        name="forward",
    )(len_q, len_p, dense_cot, late_cot, queries, passages, w_qkv, qv_bias, w_out, up_piece, w_down, qkv_piece,
      bias_in, gain, shift, offset, w_colbert)


class Settle:
    def __init__(self, lattice, view, came, send, recv, base=0):
        self.lattice, self.view, self.came = lattice, view, came
        self.send, self.recv, self.base = send, recv, base
        self.sent = []

    def copy(self, mask):
        return remote(
            self.view(mask),
            self.came.at[mask - 1],
            self.send.at[self.base + mask],
            self.recv.at[self.base + mask],
            self.lattice.peer(mask.bit_length() - 1),
        )

    def push(self, mask):
        copy = self.copy(mask)
        copy.start()
        self.sent.append(copy)

    def start(self):
        for mask in reversed(range(self.lattice.count // 2, self.lattice.count)):
            self.push(mask)

    def level(self, level):
        for mask in reversed(range(1 << level)):
            slot = (1 << level) + mask
            self.copy(slot).wait_recv()
            place = self.view(mask)
            place[...] = (place[...].astype(F32) + self.came[slot - 1].astype(F32)).astype(BF)
            if mask and mask >= 1 << (level - 1):
                self.push(mask)

    def finish(self):
        for copy in self.sent:
            copy.wait_send()


def backward_kernel(
    all_t, all_d,
    len_q, len_p, grad_vec, h_unit, h_low, h_scales, h_normals, h_wc, h_down, h_up, h_slope, h_active, h_normed,
    h_out, h_ctx, h_q, h_k, h_v, h_lse, x_q, x_p, h_qkv, gain,
    o_tokens, o_down, o_up, o_out, o_wc, o_qkv, o_small,
    pool, slope, active, out_all, wc, ctx_rows, q, k, v, lse, g1, unit, low, proj, normals, scales, sums,
    s_out, s_in, turn, ctx_out, heads_grad, turned, turned_rows, dk_sum, dv_sum,
    g_down, g_down_in, g_up, g_up_in, g_out_in, g_wc_in, qkv_sum, qkv_low, qkv_in,
    small, small_in, stage, stage_in,
    local, n_send, n_recv, r_send, r_recv, d_send, d_recv, u_send, u_recv, w_send, w_recv, c_send, c_recv,
    a_send, a_recv, t_send, t_recv, f_send, f_recv, m_send, m_recv, y_send, y_recv, q_send, q_recv,
):
    group, rank = lax.axis_index("dp"), lax.axis_index("tensor")
    ranks, groups = 1 << len(all_t), 1 << len(all_d)
    far_d = all_d[:-1]
    span, width = x_q.shape
    columns = q.shape[2]
    share = span // ranks
    units = h_up.shape[0]
    piece = units // ranks
    quarter = columns // 4
    rows = groups * share
    heads = columns // HEAD_DIM
    scale = HEAD_DIM**-0.5
    flat = width // ranks // 4
    at_up, at_down = pl.ds(0, units), pl.ds(units, units)
    at_normed, at_feed = pl.ds(2 * units, 2 * rows), pl.ds(2 * units + 2 * rows, 2 * rows)
    feed_at = 2 * units + 2 * rows

    loads = []

    def load(src, dst):
        copy = pltpu.make_async_copy(src, dst, local.at[len(loads)])
        copy.start()
        loads.append(copy)
        return copy

    early = [load(grad_vec, g1), load(h_unit, unit), load(h_scales, scales), load(h_low, low), load(h_wc, wc)]
    early.append(load(h_normals, normals))
    ffn = [load(h_down, pool.at[at_down]), load(h_slope, slope), load(h_up, pool.at[at_up])]
    later = [load(h_active, active), load(h_normed, pool.at[at_normed])]
    last = [load(h_out, out_all), load(h_ctx, ctx_rows)]
    heads_in = [load(h_q, q), load(h_k, k), load(h_v, v), load(h_lse, lse)]
    greet([{"tensor": rank ^ item} for item in range(1, ranks)] + [{"dp": group ^ item} for item in all_d])

    tensor = Lattice([("tensor", step) for step in all_t])
    quad = Lattice([("tensor", step) for step in all_t] + [("dp", step) for step in all_d[-2:]])
    data = Lattice([("dp", step) for step in all_d])

    def quarters(ref, size, lattice=quad):
        def view(mask):
            d, t = lattice.shift(mask)
            return ref.at[pl.ds(pl.multiple_of(((rank ^ t) * 4 + (group ^ d) % 4) * size, size), size)]

        return view

    cross = Lattice(tensor.steps[:-2] + [tensor.steps[-1], tensor.steps[-2]])

    def pieces(ref, lattice):
        return lambda mask: ref.at[pl.ds(pl.multiple_of((rank ^ lattice.shift(mask)[1]) * piece, piece), piece)]

    def spot(mask):
        return pl.multiple_of((group ^ data.shift(mask)[0]) * share, share)

    flow = Lattice([("dp", all_d[-2])] + tensor.steps + [("dp", all_d[-1])])
    give_wc = Settle(flow, quarters(wc, flat, flow), g_wc_in, c_send, c_recv)
    give_out = Settle(quad, quarters(out_all, quarter), g_out_in, w_send, w_recv)
    give_down = Settle(tensor, pieces(g_down, tensor), g_down_in, d_send, d_recv)
    give_up = Settle(cross, pieces(g_up, cross), g_up_in, u_send, u_recv)

    small[...] = jnp.zeros_like(small)
    for copy in early[:4]:
        copy.wait()
    takes = []
    for s in range(2):
        at = slice(s * share, (s + 1) * share)
        grad, plain = g1[at, :], unit[at, :]
        chosen = scales[2, at, 0:1] * (grad - plain * jnp.sum(grad * plain, axis=-1, keepdims=True))
        leading = lax.broadcasted_iota(jnp.int32, (share, 1), 0) + rank * share == 0
        short = jnp.where(leading, 0.0, chosen).astype(BF)
        proj[at, :] = short
        if s == 0:
            early[4].wait()
        grad = jnp.where(leading, chosen, 0.0) + inner_rows(short, wc[...])
        if s == 0:
            early[5].wait()
        middle, gains, shifts = norm_back(grad, normals[1, at, :], scales[1, at, 0:1], gain[1:2, :])
        g1[at, :] = middle
        small[0, 1:2, :] += gains[None, :]
        small[0, 3:4, :] += shifts[None, :]
        small[0, 5:6, :] += jnp.sum(middle, axis=0, keepdims=True)
        small[0, 6:7, :] += jnp.sum(short.astype(F32), axis=0, keepdims=True)
        own = pl.multiple_of(feed_at + s * rows + group * share, share)
        pool[pl.ds(own, share), :] = middle.astype(BF)

        def view(mask, s=s):
            place = feed_at + s * rows + (group ^ data.shift(mask)[0]) * share
            return pool.at[pl.ds(pl.multiple_of(place, share), share)]

        taking = Gather(data, view, n_send, n_recv, s * groups)
        taking.start()
        takes.append(taking)

    @pl.loop(0, width // 512)
    def _(index):
        at = pl.ds(pl.multiple_of(index * 512, 512), 512)
        wc[at, :] = outer_rows(low[:, at], proj[...]).astype(BF)

    give_wc.start()

    gives = []
    for s in range(2):

        def read(mask, s=s):
            return sums[s, pl.ds(spot(mask), share), :]

        def write(mask, value, s=s):
            sums[s, pl.ds(spot(mask), share), :] = value

        gives.append(Scatter(data, read, write, s_out.at[s], s_in.at[s], r_send, r_recv, s * groups))
    for copy in ffn:
        copy.wait()
    tile = min(512, units)

    def shrink(s):
        at_rows = slice(s * rows, (s + 1) * rows)
        feed_rows = slice(feed_at + s * rows, feed_at + (s + 1) * rows)

        @pl.loop(0, units // tile)
        def _(index):
            at = pl.ds(pl.multiple_of(index * tile, tile), tile)
            down_at = pl.ds(pl.multiple_of(units + index * tile, tile), tile)
            value = inner_rows(pool[feed_rows, :], pool[down_at, :]) * slope[at_rows, at].astype(F32)
            value = value.astype(BF)
            slope[at_rows, at] = value
            small[0, 7:8, at] += jnp.sum(value.astype(F32), axis=0, keepdims=True)

        @pl.loop(0, width // 512)
        def _(index):
            at = pl.ds(pl.multiple_of(index * 512, 512), 512)
            sums[s, :, at] = dot(slope[at_rows, :], pool[at_up, at])

    def put(s):
        for mask in reversed(range(groups // 2, groups)):
            gives[s].put(mask)

    top = len(all_d) - 1
    last_t = len(all_t) - 1
    quad_top = len(all_t) + 1
    blocks = list(reversed(range(ranks // 2, ranks)))
    give_wc.level(quad_top)
    for mask in range(1, groups):
        takes[0].arrive(mask)
    shrink(0)
    put(0)
    for copy in later:
        copy.wait()
    for mask in range(1, groups):
        takes[1].arrive(mask)
    gives[0].level(top)

    @pl.loop(0, units // tile)
    def _(index):
        at = pl.ds(pl.multiple_of(index * tile, tile), tile)
        g_down[at, :] = outer_rows(active[:, at], pool[at_feed, :]).astype(BF)

    for mask in blocks[:2]:
        give_down.push(mask)
    give_wc.level(last_t + 1)
    shrink(1)
    put(1)

    @pl.loop(0, units // tile)
    def _(index):
        at = pl.ds(pl.multiple_of(index * tile, tile), tile)
        g_up[at, :] = outer_rows(slope[:, at], pool[at_normed, :]).astype(BF)

    gives[1].level(top)
    for mask in blocks[:1]:
        give_up.push(mask)

    for copy in last:
        copy.wait()
    def small_step(level):
        copy = remote(
            small.at[level], small_in.at[level], m_send.at[level], m_recv.at[level], {"tensor": rank ^ all_t[level]}
        )
        return copy

    small_copies = [small_step(level) for level in range(len(all_t))]

    def small_next(level):
        small_copies[level].wait_recv()
        small[level + 1] = small[level] + small_in[level]
        if level + 1 < len(all_t):
            small_copies[level + 1].start()

    sends = []
    for s in range(2):
        at = slice(s * share, (s + 1) * share)
        for level in reversed(range(top)):
            gives[s].level(level)
        grad = g1[at, :] + gives[s].read(0)
        hidden, gains, shifts = norm_back(grad, normals[0, at, :], scales[0, at, 0:1], gain[0:1, :])
        g1[at, :] = hidden
        small[0, 0:1, :] += gains[None, :]
        small[0, 2:3, :] += shifts[None, :]
        small[0, 4:5, :] += jnp.sum(hidden, axis=0, keepdims=True)
        short = hidden.astype(BF)
        turn[at, :] = short
        if columns % 128 == 0:
            value = inner_rows(short, out_all[...]).astype(BF)
            for r in range(ranks):
                ctx_out[r, at, :] = value[:, r * columns : (r + 1) * columns]
        else:
            for r in range(ranks):
                ctx_out[r, at, :] = inner_rows(short, out_all[r * columns : (r + 1) * columns, :]).astype(BF)
        mine = pl.ds(pl.multiple_of(rank * share, share), share)
        for item in range(1, ranks):
            copy = remote(
                ctx_out.at[rank ^ item, pl.ds(s * share, share)],
                heads_grad.at[s, mine],
                a_send.at[s * ranks + item],
                a_recv.at[s * ranks + item],
                {"tensor": rank ^ item},
            )
            copy.start()
            sends.append(copy)
        heads_grad[s, mine, :] = ctx_out[rank, at, :]
        if s == 1:
            for mask in blocks[1:2]:
                give_up.push(mask)
            small_copies[0].start()
    for taking in takes:
        taking.finish()
    tall = load(x_q, pool.at[pl.ds(0, span)]), load(x_p, pool.at[pl.ds(span, span)])
    at_qkv = 2 * span
    pairs = Lattice([("dp", step) for step in all_d[-2:]])
    back_in = load(h_qkv, pool.at[pl.ds(at_qkv, 3 * columns * ranks)])

    for r in range(ranks):
        out_all[r * columns : (r + 1) * columns, :] = outer_rows(ctx_rows[r], turn[...]).astype(BF)
    give_wc.level(last_t)
    give_out.start()

    block = min(BLOCK, span)

    lengths = (len_q[group], len_p[group])

    def attention(s, begin, end):
        keep = lax.broadcasted_iota(jnp.int32, (span, 1), 0) < lengths[s]

        @pl.loop(begin, end)
        def _(index):
            at = pl.ds(pl.multiple_of(index * block, block), block)
            query = q[s, at, :]
            grad = heads_grad[s, at, :]
            total = jnp.zeros((block, columns), F32)
            for head in range(heads):
                mask = head_mask(columns, head)
                mine = jnp.where(mask, query, jnp.zeros_like(query)) * jnp.asarray(scale, BF)
                back = jnp.where(mask, grad, jnp.zeros_like(grad))
                scores = jnp.where(keep, inner_rows(k[s], mine), -1e30)
                probs = jnp.exp(scores - lse[s, head : head + 1, at])
                slant = inner_rows(v[s], back)
                middle = jnp.sum(probs * slant, axis=0, keepdims=True)
                twist = (probs * (slant - middle)).astype(BF)
                dv_sum[...] += dot(probs.astype(BF), back)
                dk_sum[...] += dot(twist, mine)
                part = outer_rows(twist, k[s]) * scale
                total = jnp.where(mask, part, total)
            turned[s, at, 0:columns] = total.astype(BF)

    def attention_start(s):
        for item in range(1, ranks):
            place = heads_grad.at[s, pl.ds(pl.multiple_of((rank ^ item) * share, share), share)]
            remote(
                place, place, a_send.at[s * ranks + item], a_recv.at[s * ranks + item], {"tensor": rank ^ item}
            ).wait_recv()
        dk_sum[...] = jnp.zeros_like(dk_sum)
        dv_sum[...] = jnp.zeros_like(dv_sum)

    def attention_end(s):
        turned[s, :, columns : 2 * columns] = dk_sum[...].astype(BF)
        turned[s, :, 2 * columns : 3 * columns] = dv_sum[...].astype(BF)
        for item in range(1, ranks):
            copy = remote(
                turned.at[s, pl.ds(pl.multiple_of((rank ^ item) * share, share), share)],
                turned_rows.at[rank, pl.ds(s * share, share)],
                t_send.at[s * ranks + item],
                t_recv.at[s * ranks + item],
                {"tensor": rank ^ item},
            )
            copy.start()
            sends.append(copy)
        turned_rows[rank, s * share : (s + 1) * share, :] = turned[
            s, pl.ds(pl.multiple_of(rank * share, share), share), :
        ]

    many = qkv_sum.shape[1]

    def qkv_grad(s):
        tokens = pool[s * span : (s + 1) * span, :]
        for i in range(3):
            part = turned[s, :, i * columns : (i + 1) * columns]
            whole = outer_rows(tokens, part)
            line = jnp.broadcast_to(jnp.sum(part.astype(F32), axis=0, keepdims=True), (many - width, columns))
            if s == 0:
                qkv_sum[i, 0:width, :] = whole
                qkv_sum[i, width:many, :] = line
            else:
                qkv_sum[i, 0:width, :] += whole
                qkv_sum[i, width:many, :] += line

    for copy in heads_in:
        copy.wait()
    count = span // block
    attention_start(0)
    attention(0, 0, count // 2)
    for mask in blocks[2:]:
        give_down.push(mask)
    for level in reversed(range(1, last_t)):
        give_wc.level(level)
    small_next(0)
    give_wc.level(0)
    for mask in blocks[2:]:
        give_up.push(mask)
    attention(0, count // 2, count)
    attention_end(0)
    for copy in tall:
        copy.wait()
    qkv_grad(0)
    attention_start(1)
    for level in range(1, len(all_t)):
        small_next(level)
    attention(1, 0, count // 2)
    small_own = small.at[len(all_t)]
    small_take = Gather(data, lambda m: o_small.at[group ^ data.shift(m)[0]], f_send, f_recv, 0, own=small_own)
    small_take.start()
    small_copy = load(small_own, o_small.at[group])
    give_up.level(last_t)
    attention(1, count // 2, count)
    attention_end(1)
    give_out.level(quad_top)

    rest = all_d[:-2]

    def settle_stage(which, source, size):
        base = which * max(1, len(rest))
        copies = []
        for index, step in enumerate(rest):
            src = source if index == 0 else stage.at[base + index - 1, pl.ds(0, size)]
            dst = stage_in.at[base + index, pl.ds(0, size)]
            copies.append(remote(src, dst, y_send.at[base + index], y_recv.at[base + index], {"dp": group ^ step}))
        for index, copy in enumerate(copies):
            copy.start()
            copy.wait_recv()
            before = source[...] if index == 0 else stage[base + index - 1, 0:size, :]
            value = before.astype(F32) + stage_in[base + index, 0:size, :].astype(F32)
            stage[base + index, 0:size, :] = value.astype(BF)
        return (stage.at[base + len(rest) - 1, pl.ds(0, size)] if rest else source), copies

    def dp_view(ref):
        return lambda m: ref.at[pl.ds(pl.multiple_of((group ^ data.shift(m)[0]) * piece, piece), piece)]

    def out_view(mask):
        d, _ = pairs.shift(mask)
        return o_out.at[pl.ds(pl.multiple_of(((group ^ d) % 4) * quarter, quarter), quarter)]

    out_base = 2 * groups + quad.count

    def rows_end(s):
        at = slice(s * share, (s + 1) * share)
        for item in range(1, ranks):
            place = turned_rows.at[rank ^ item, pl.ds(s * share, share)]
            remote(
                place, place, t_send.at[s * ranks + item], t_recv.at[s * ranks + item], {"tensor": rank ^ item}
            ).wait_recv()
        total = g1[at, :]
        for r in range(ranks):
            begin = at_qkv + r * 3 * columns
            total = total + dot(turned_rows[r, at, :], pool[begin : begin + 3 * columns, :])
        unit[at, :] = total

    back_in.wait()
    rows_end(0)
    give_up.level(last_t - 1)
    give_down.level(last_t)
    qkv_grad(1)

    part = many // 2
    at_mine = pl.ds(pl.multiple_of((group % 2) * part, part), part)
    at_other = pl.ds(pl.multiple_of((1 - group % 2) * part, part), part)
    near = {"dp": group ^ all_d[-1]}
    qkv_low[0] = qkv_sum[:, at_other, :].astype(BF)
    qkv_copies = [remote(qkv_low.at[0], qkv_in.at[0], q_send.at[0], q_recv.at[0], near)]
    qkv_copies[0].start()
    for index, step in enumerate(far_d):
        slot = 1 + index
        qkv_copies.append(
            remote(qkv_low.at[slot], qkv_in.at[slot], q_send.at[slot], q_recv.at[slot], {"dp": group ^ step})
        )
    qkv_last = len(far_d) + 1
    qkv_own = qkv_low.at[qkv_last]
    qkv_copies.append(remote(qkv_own, o_qkv.at[:, at_mine], q_send.at[qkv_last], q_recv.at[qkv_last], near))

    wc_own, wc_copies = settle_stage(0, give_wc.view(0), flat)
    wc_take = Gather(quad, quarters(o_wc, flat), f_send, f_recv, groups, own=wc_own)
    wc_take.start()
    wc_copy = load(wc_own, wc_take.view(0))
    qkv_copies[0].wait_recv()
    sum_half = qkv_sum[:, at_mine, :].astype(BF).astype(F32) + qkv_in[0].astype(F32)
    qkv_low[1] = sum_half.astype(BF)
    qkv_copies[1].start()
    for level in reversed(range(last_t - 1)):
        give_up.level(level)
    up_own = give_up.view(0)
    up_take = Gather(data, dp_view(o_up), f_send, f_recv, out_base + 4, own=up_own)
    up_take.start()
    up_copy = load(up_own, up_take.view(0))
    give_out.level(quad_top - 1)
    for mask in range(1, ranks // 2):
        wc_take.arrive(mask)
    give_down.level(last_t - 1)
    give_out.level(last_t)
    for index in range(len(far_d)):
        qkv_copies[1 + index].wait_recv()
        qkv_low[2 + index] = (qkv_low[1 + index].astype(F32) + qkv_in[1 + index].astype(F32)).astype(BF)
        qkv_copies[index + 2].start()
    qkv_local = load(qkv_own, o_qkv.at[:, at_mine])
    for mask in range(ranks // 2, quad.count):
        wc_take.arrive(mask)
    for level in reversed(range(last_t - 1)):
        give_down.level(level)
    down_own = give_down.view(0)
    down_take = Gather(data, dp_view(o_down), f_send, f_recv, groups + quad.count, own=down_own)
    down_take.start()
    down_copy = load(down_own, down_take.view(0))
    give_out.level(last_t - 1)
    rows_end(1)
    tokens_copy = load(unit, o_tokens)
    for level in reversed(range(last_t - 1)):
        give_out.level(level)
    out_own, out_copies = settle_stage(1, give_out.view(0), quarter)
    out_take = Gather(pairs, out_view, f_send, f_recv, out_base, own=out_own)
    out_take.start()
    out_copy = load(out_own, out_view(0))
    for taking in (small_take, down_take, up_take):
        for mask in range(1, groups):
            taking.arrive(mask)
    for mask in range(1, 4):
        out_take.arrive(mask)
    at_theirs = o_qkv.at[:, at_other]
    remote(at_theirs, at_theirs, q_send.at[qkv_last], q_recv.at[qkv_last], near).wait_recv()
    for move in [give_wc, give_out, give_down, give_up, small_take, wc_take, down_take, up_take, out_take] + gives:
        move.finish()
    for copy in sends + small_copies + qkv_copies + wc_copies + out_copies:
        copy.wait_send()
    for copy in (tokens_copy, small_copy, wc_copy, down_copy, qkv_local, out_copy, up_copy):
        copy.wait()


def backward(len_q, len_p, grad_vec, unit, low, scales, normals, w_colbert, down, up, slope, active, normed, out_all,
             context_rows, query, key, value, lse, queries, passages, qkv_all, gain):
    groups, ranks = lax.axis_size("dp"), lax.axis_size("tensor")
    all_t, all_d = steps_of(ranks), steps_of(groups)
    span, width = queries.shape
    columns = query.shape[2]
    heads = columns // HEAD_DIM
    share = span // ranks
    units = up.shape[0]
    piece = units // ranks
    rows = groups * share
    quarter, flat = columns // 4, width // ranks // 4
    pool = max(2 * units + 4 * rows, 2 * span + 3 * columns * ranks)
    many = width + 32
    far = len(all_d) - 1
    dma = pltpu.SemaphoreType.DMA
    vmem = pltpu.VMEM
    hold, leave = pl.BlockSpec(memory_space=pltpu.VMEM), pl.BlockSpec(memory_space=pl.ANY)
    shapes = [
        ((2 * share, width), F32),
        ((units // ranks * groups, width), BF),
        ((units // ranks * groups, width), BF),
        ((columns, width), BF),
        ((width, width), BF),
        ((3, many, columns), BF),
        ((groups, 8, width), F32),
    ]
    smem = pl.BlockSpec(memory_space=pltpu.SMEM)
    rest = max(1, len(all_d) - 2)

    def pair(count):
        return [dma((count,)), dma((count,))]

    return pl.pallas_call(
        functools.partial(backward_kernel, all_t, all_d),
        out_shape=[jax.ShapeDtypeStruct(*item) for item in shapes],
        in_specs=[smem, smem] + [leave] * 20 + [hold],
        out_specs=[leave] * len(shapes),
        scratch_shapes=[
            vmem((pool, width), BF),
            vmem((2 * rows, units), BF),
            vmem((2 * rows, units), BF),
            vmem((ranks * columns, width), BF),
            vmem((width, width), BF),
            vmem((ranks, 2 * share, columns), BF),
            vmem((2, span, columns), BF),
            vmem((2, span, columns), BF),
            vmem((2, span, columns), BF),
            vmem((2, heads, span), F32),
            vmem((2 * share, width), F32),
            vmem((2 * share, width), F32),
            vmem((2 * share, width), BF),
            vmem((2 * share, width), BF),
            vmem((2, 2 * share, width), F32),
            vmem((3, 2 * share, 128), F32),
            vmem((2, rows, width), F32),
            vmem((2, groups - 1, share, width), BF),
            vmem((2, groups - 1, share, width), BF),
            vmem((2 * share, width), BF),
            vmem((ranks, 2 * share, columns), BF),
            vmem((2, span, columns), BF),
            vmem((2, span, 3 * columns), BF),
            vmem((ranks, 2 * share, 3 * columns), BF),
            vmem((span, columns), F32),
            vmem((span, columns), F32),
            vmem((units, width), BF),
            vmem((ranks - 1, piece, width), BF),
            vmem((units, width), BF),
            vmem((ranks - 1, piece, width), BF),
            vmem((4 * ranks - 1, quarter, width), BF),
            vmem((4 * ranks - 1, flat, width), BF),
            vmem((3, many, columns), F32),
            vmem((2 + far, 3, many // 2, columns), BF),
            vmem((1 + far, 3, many // 2, columns), BF),
            vmem((len(all_t) + 1, 8, width), F32),
            vmem((len(all_t), 8, width), F32),
            vmem((2 * rest, max(quarter, flat), width), BF),
            vmem((2 * rest, max(quarter, flat), width), BF),
            dma((32,)),
        ]
        + pair(2 * groups)
        + pair(2 * groups)
        + pair(ranks)
        + pair(ranks)
        + pair(4 * ranks)
        + pair(4 * ranks)
        + pair(2 * ranks)
        + pair(2 * ranks)
        + pair(3 * groups + 4 * ranks + 4)
        + pair(len(all_t))
        + pair(2 * rest)
        + pair(2 + far),
        compiler_params=pltpu.CompilerParams(
            collective_id=3, has_side_effects=True, vmem_limit_bytes=62 * 2**20
        ),
        cost_estimate=pl.CostEstimate(flops=10**11, bytes_accessed=40 * 2**20, transcendentals=2**22),
        name="backward",
    )(len_q, len_p, grad_vec, unit, low, scales, normals, w_colbert, down, up, slope, active, normed, out_all,
      context_rows, query, key, value, lse, queries, passages, qkv_all, gain)


def finish_kernel(
    rank_of, low, tokens, down, up, out, wc, qkv, small,
    out_q, out_p, tok_q, tok_p, g_qkv, g_bias, g_out, g_up, g_in, g_down, g_gain, g_shift, g_offset, g_wc,
    v_low, v_tokens, v_down, v_up, v_out, v_wc, v_qkv, f_down, f_up, f_out, f_wc, f_qkv, load, store,
):
    share, width = out_q.shape
    copies = []

    def begin(src, dst, sem):
        copy = pltpu.make_async_copy(src, dst, sem)
        copy.start()
        return copy

    loads = [
        begin(src, dst, load.at[index])
        for index, (src, dst) in enumerate(
            ((down, v_down), (up, v_up), (wc, v_wc), (qkv, v_qkv), (out, v_out), (low, v_low), (tokens, v_tokens))
        )
    ]
    loads[0].wait()
    f_down[...] = v_down[...].astype(F32)
    copies.append(begin(f_down, g_down, store.at[4]))
    loads[1].wait()
    f_up[...] = v_up[...].T.astype(F32)
    copies.append(begin(f_up, g_up, store.at[5]))
    loads[2].wait()
    f_wc[...] = v_wc[...].astype(F32)
    copies.append(begin(f_wc, g_wc, store.at[6]))
    loads[3].wait()
    f_qkv[...] = v_qkv[:, 0:width, :].astype(F32)
    copies.append(begin(f_qkv, g_qkv, store.at[7]))
    g_bias[0:1, :] = v_qkv[0, width : width + 16, :].astype(F32)[0:1, :]
    g_bias[1:2, :] = v_qkv[2, width : width + 16, :].astype(F32)[0:1, :]
    loads[4].wait()
    f_out[...] = v_out[...].astype(F32)
    copies.append(begin(f_out, g_out, store.at[8]))
    groups = small.shape[0]
    total = small[0]
    for index in range(1, groups):
        total = total + small[index]
    g_gain[...] = total[0:2]
    g_shift[...] = total[2:4]
    g_offset[...] = total[4:7]
    piece = g_in.shape[1]
    for index in range(groups):
        if piece % 128 == 0:
            at = pl.ds(pl.multiple_of(rank_of[0] * piece, piece), piece)
            g_in[index : index + 1, :] = small[index, 7:8, at]
    loads[5].wait()
    copies.append(begin(v_low.at[pl.ds(0, share)], out_q, store.at[0]))
    copies.append(begin(v_low.at[pl.ds(share, share)], out_p, store.at[1]))
    loads[6].wait()
    copies.append(begin(v_tokens.at[pl.ds(0, share)], tok_q, store.at[2]))
    copies.append(begin(v_tokens.at[pl.ds(share, share)], tok_p, store.at[3]))
    for copy in copies:
        copy.wait()


def finish(low, tokens, down, up, out, wc, qkv, small, piece):
    share, width = low.shape[0] // 2, low.shape[1]
    hidden, columns = down.shape[0], out.shape[0]
    groups = small.shape[0]
    hold, leave = pl.BlockSpec(memory_space=pltpu.VMEM), pl.BlockSpec(memory_space=pl.ANY)
    rank_of = lax.axis_index("tensor").reshape(1).astype(jnp.int32)
    shapes = [
        ((share, width), BF),
        ((share, width), BF),
        ((share, width), F32),
        ((share, width), F32),
        ((3, width, columns), F32),
        ((2, columns), F32),
        ((columns, width), F32),
        ((width, hidden), F32),
        ((groups, piece), F32),
        ((hidden, width), F32),
        ((2, width), F32),
        ((2, width), F32),
        ((3, width), F32),
        ((width, width), F32),
    ]
    vmem, dma = pltpu.VMEM, pltpu.SemaphoreType.DMA
    return pl.pallas_call(
        finish_kernel,
        out_shape=[jax.ShapeDtypeStruct(*item) for item in shapes],
        in_specs=[pl.BlockSpec(memory_space=pltpu.SMEM)] + [leave] * 7 + [hold],
        out_specs=[leave] * 5 + [hold, leave, leave, hold, leave, hold, hold, hold, leave],
        scratch_shapes=[
            vmem(low.shape, BF),
            vmem(tokens.shape, F32),
            vmem(down.shape, BF),
            vmem(up.shape, BF),
            vmem(out.shape, BF),
            vmem(wc.shape, BF),
            vmem(qkv.shape, BF),
            vmem(down.shape, F32),
            vmem((width, hidden), F32),
            vmem(out.shape, F32),
            vmem(wc.shape, F32),
            vmem((3, width, columns), F32),
            dma((7,)),
            dma((9,)),
        ],
        compiler_params=pltpu.CompilerParams(vmem_limit_bytes=62 * 2**20),
        name="finish",
    )(rank_of, low, tokens, down, up, out, wc, qkv, small)


def per_device(
    queries,
    passages,
    query_lengths,
    passage_lengths,
    w_qkv,
    qv_bias,
    w_out,
    w_in,
    in_bias,
    w_down,
    norm_gain,
    norm_shift,
    layer_bias,
    w_colbert,
    dense_cot,
    colbert_cot,
):
    groups, ranks = lax.axis_size("dp"), lax.axis_size("tensor")
    group, rank = lax.axis_index("dp"), lax.axis_index("tensor")
    width = queries.shape[1]
    columns = w_qkv.shape[2]
    piece = w_in.shape[1] // groups
    units = piece * ranks

    if piece % 128 == 0 and piece != w_in.shape[0]:
        up_piece = w_in
    else:
        up_piece = lax.dynamic_slice_in_dim(w_in, group * piece, piece, 1).T
    if columns % 128 == 0:
        qkv_piece = w_out
    else:
        slim = 3 * columns // 2
        turned = w_qkv.transpose(0, 2, 1).reshape(3 * columns, width)
        qkv_piece = lax.dynamic_slice_in_dim(turned, (group % 2) * slim, slim, 0)
    if piece % 128 == 0:
        bias_in = lax.dynamic_slice_in_dim(in_bias, group * piece, piece, 0)
        bias_in = jnp.broadcast_to(bias_in[None, :], (16, piece))
    else:
        bias_in = lax.all_gather(in_bias, "tensor").reshape(ranks, groups, piece)
        bias_in = lax.dynamic_index_in_dim(bias_in, group, 1, keepdims=False).reshape(1, -1).astype(F32)
    (
        query,
        key,
        value,
        lse,
        context_rows,
        out_all,
        up,
        down,
        qkv_all,
        normed,
        slope,
        active,
        normals,
        unit,
        low,
        scales,
        grad_vec,
    ) = forward(
        query_lengths, passage_lengths, dense_cot, colbert_cot, queries, passages, w_qkv, qv_bias, w_out, up_piece,
        w_down, qkv_piece, bias_in, norm_gain, norm_shift, layer_bias, w_colbert,
    )
    tokens, grad_down, grad_up, grad_out, colbert, grad_qkv, small = backward(
        query_lengths, passage_lengths, grad_vec, unit, low, scales, normals, w_colbert, down, up, slope, active,
        normed.reshape(-1, width), out_all.reshape(-1, width), context_rows, query, key, value, lse,
        queries, passages, qkv_all.reshape(-1, width), norm_gain,
    )
    results = list(finish(low, tokens, grad_down, grad_up, grad_out, colbert, grad_qkv, small, piece))
    if piece % 128:
        bias = small[:, 7, :units].reshape(groups, ranks, piece)
        results[8] = lax.dynamic_index_in_dim(bias, rank, 1, keepdims=False)
    results[8] = results[8].reshape(-1)
    return tuple(results)


def solution(mesh):
    both = P(("dp", "tensor"), None)
    return jax.shard_map(
        per_device,
        mesh=mesh,
        in_specs=(
            P("dp", None),
            P("dp", None),
            P(),
            P(),
            P(None, None, "tensor"),
            P(None, "tensor"),
            P("tensor", None),
            P(None, "tensor"),
            P("tensor"),
            P("tensor", None),
            P(),
            P(),
            P(),
            P(),
            P(),
            P(),
        ),
        out_specs=(
            both,
            both,
            both,
            both,
            P(None, None, "tensor"),
            P(None, "tensor"),
            P("tensor", None),
            P(None, "tensor"),
            P("tensor"),
            P("tensor", None),
            P(),
            P(),
            P(),
            P(),
        ),
        check_vma=False,
    )
```
